128 devices in a mesh: wide: 32 (over y, z, core), narrow: 4 (over x).
Axes of the slice: x: 4, y: 4, z: 4, core: 2. Of those that a mesh axis runs over, the one named last changes fastest.
Arguments:
- frames_lr: float32 [4, 256, 128, 128], P('narrow', 'wide'), may hold values from -24 to 24
- anchor_col: int32 [4, 256], P('narrow'), may hold values from 0 to 31, as said below
- shift_index: int32 [4, 256, 2], P('narrow'), may hold values from 0 to 15
- initial_guess: float32 [2048, 16384], P('narrow', 'wide'), may hold values from -6 to 6
Outputs:
- solution: float32 [2048, 16384], P('narrow', 'wide')
- residual: float32 [2048, 16384], P('narrow', 'wide')
The draws below stay inside these ranges and needn't reach their ends.
Inputs may be any that keep to these rules, and one draw needn't show every extreme that they name: `anchor_col`: frame f's anchor column differs from its owner column f // 8 by at most one.
All inputs are finite; a program needn't handle non-finite values.
Results may differ from the reference program's by a relative error of at most 0.0003.
Values sent between devices are 32-bit elements; how exact they have to be, the bound alone decides.
A program may use at most 64 MiB of HBM per device.

```python
import jax
import jax.numpy as jnp
from jax import lax

TS = 512
FS = 128
FR_DEV = 8
NSHIFT = 16
ITERS = 2
FRAMES_ROW = 256
NR = 2048
NC = 16384
N_WIDE = 32
N_NARROW = 4


def draw_anchor_col(key, part):
    key = jax.random.fold_in(key, 2)
    first, second, third = jax.random.split(key, 3)
    owner = jnp.arange(FRAMES_ROW, dtype=jnp.int32) // FR_DEV
    leaning = jax.random.randint(first, (N_NARROW, N_WIDE), -1, 2)
    picker = jax.random.randint(second, (N_NARROW, FRAMES_ROW), 0, 4)
    scatter = jax.random.randint(third, (N_NARROW, FRAMES_ROW), -1, 2)
    offset = jnp.where(picker < 3, leaning[:, owner], scatter)
    return jnp.clip(owner[None, :] + offset, 0, N_WIDE - 1).astype(jnp.int32)


def draw_frames_lr(key, part):
    key = jax.random.fold_in(key, 7)
    first = jax.random.fold_in(key, 0)
    owner = jnp.arange(FRAMES_ROW) // FR_DEV
    rising = 1.0 + 2.0 * owner.astype(jnp.float32) / max(N_WIDE - 1, 1)
    shape = (N_NARROW, FRAMES_ROW, FS, FS)
    values = jnp.clip(jax.random.normal(first, shape, jnp.float32), -8.0, 8.0)
    return values * rising[None, :, None, None]


def plant(result, stream_key, least, largest):
    spot = [jax.random.randint(jax.random.fold_in(stream_key, axis), (), 0, length) for axis, length in enumerate(result.shape)]
    widest = result.shape.index(max(result.shape))
    neighbour = spot[:widest] + [(spot[widest] + 1) % result.shape[widest]] + spot[widest + 1:]
    return result.at[tuple(spot)].set(least).at[tuple(neighbour)].set(largest)


def block_scale(rng, shape, cuts, least, high):
    loudness, own = 1.0, jax.random.fold_in(rng, 6)
    for position, blocks in cuts:
        draws = jnp.exp(jax.random.uniform(jax.random.fold_in(own, position), (blocks,), jnp.float32, least / len(cuts), high / len(cuts)))
        loudness = loudness * jnp.repeat(draws, shape[position] // blocks).reshape([-1 if axis == position else 1 for axis in range(len(shape))])
    return loudness


def gaussian(key, shape, scale, reach, pieces=(), kind=jnp.bfloat16):
    drawn = scale * jax.random.normal(key, shape, jnp.float32)
    if pieces:
        drawn = drawn * block_scale(key, shape, pieces, -0.22, 0.18)
    return jnp.clip(drawn, -reach, reach).astype(kind)


def setup_inputs(seed: int = 0) -> dict:
    streams_of = jax.random.split(jax.random.key(seed), 5)
    return {
        "frames_lr": draw_frames_lr(jax.random.fold_in(streams_of[4], 71), 0),
        "anchor_col": draw_anchor_col(jax.random.fold_in(streams_of[4], 71), 0),
        "shift_index": plant(jax.random.randint(streams_of[2], (N_NARROW, FRAMES_ROW, 2), 0, NSHIFT), jax.random.fold_in(streams_of[2], 1), 0, NSHIFT - 1).astype(jnp.int32),
        "initial_guess": gaussian(streams_of[3], (NR, NC), 1.0, 6.0, ((0, 4), (1, 32)), jnp.float32),
    }


highest = lax.Precision.HIGHEST
damping = 0.05


def tap_table():
    fraction = jnp.arange(NSHIFT, dtype=jnp.float32) / NSHIFT
    offsets = jnp.arange(8, dtype=jnp.float32)[None, :] - 3.0 - fraction[:, None]
    lanczos = jnp.sinc(offsets) * jnp.sinc(offsets / 4.0)
    lanczos = lanczos / jnp.sum(lanczos, axis=1, keepdims=True)
    spread = jnp.arange(11)[None, :] - jnp.arange(8)[:, None]
    blur = jnp.where((spread >= 0) & (spread < 4), 0.25, 0.0).astype(jnp.float32)
    return jnp.dot(lanczos, blur, precision=highest, preferred_element_type=jnp.float32)


def operator_matrix(tap_rows, index, low_size, high_size):
    weights = tap_rows[index]
    offsets = jnp.arange(high_size)[None, :] - 4 * jnp.arange(low_size)[:, None]
    matrix = jnp.zeros((low_size, high_size), jnp.float32)
    for place in range(11):
        matrix = matrix + jnp.where(offsets == place, weights[place], 0.0).astype(jnp.float32)
    return matrix


def frame_pass(window, observed, tap_rows, kernels):
    low_size = observed.shape[0]
    high_size = window.shape[0]
    row_map = operator_matrix(tap_rows, kernels[0], low_size, high_size)
    col_map = operator_matrix(tap_rows, kernels[1], low_size, high_size)
    model = jnp.dot(jnp.dot(row_map, window, precision=highest, preferred_element_type=jnp.float32), col_map.T, precision=highest, preferred_element_type=jnp.float32)
    mismatch = model - observed
    right = jnp.dot(mismatch, col_map, precision=highest, preferred_element_type=jnp.float32)
    return jnp.dot(row_map.T, right, precision=highest, preferred_element_type=jnp.float32)


def reference(frames_lr, anchor_col, shift_index, initial_guess):
    tap_rows = tap_table()
    extent = TS + 8
    tile_rows = jnp.repeat(jnp.arange(N_NARROW, dtype=jnp.int32), FRAMES_ROW)
    anchors = anchor_col.reshape(-1).astype(jnp.int32)
    kernels_all = shift_index.reshape(-1, 2)
    observed_all = frames_lr.reshape(-1, FS, FS)

    def normal_pass(vector, scale_data):
        padded = jnp.pad(vector, 4)

        def accumulate(total, record):
            tile_row, anchor, kernels, observed = record
            first = (tile_row * TS).astype(jnp.int32)
            second = (anchor * TS).astype(jnp.int32)
            window = lax.dynamic_slice(padded, (first, second), (extent, extent))
            contrib = frame_pass(window, scale_data * observed, tap_rows, kernels)
            current = lax.dynamic_slice(total, (first, second), (extent, extent))
            return lax.dynamic_update_slice(total, current + contrib, (first, second)), None

        total, _ = lax.scan(accumulate, jnp.zeros_like(padded), (tile_rows, anchors, kernels_all, observed_all))
        return total[4:-4, 4:-4]

    solution = initial_guess
    residual = -(normal_pass(initial_guess, 1.0) + damping * initial_guess)
    direction = residual
    norm_now = jnp.sum(residual * residual)
    for step in range(ITERS):
        image = normal_pass(direction, 0.0) + damping * direction
        alpha = norm_now / jnp.sum(direction * image)
        solution = solution + alpha * direction
        residual = residual - alpha * image
        norm_next = jnp.sum(residual * residual)
        direction = residual + (norm_next / norm_now) * direction
        norm_now = norm_next
    return solution, residual
```

```python
import functools

import jax
import jax.numpy as jnp
import numpy as np
from jax import lax
from jax.experimental import pallas as pl
from jax.experimental.pallas import tpu as pltpu
from jax.sharding import PartitionSpec as P

NSHIFT = 16
DAMP = 0.05
TS = 512
FS = 128
ROWS = TS + 16
TILES = ROWS // 8
GROUP = 11
PACK = GROUP * 8
F32 = jnp.float32
BF16 = jnp.bfloat16
HIGHEST = lax.Precision.HIGHEST


def tables():
    fraction = np.arange(NSHIFT, dtype=np.float64) / NSHIFT
    offsets = np.arange(8, dtype=np.float64)[None, :] - 3.0 - fraction[:, None]
    lanczos = np.sinc(offsets) * np.sinc(offsets / 4.0)
    lanczos = lanczos / lanczos.sum(axis=1, keepdims=True)
    spread = np.arange(11)[None, :] - np.arange(8)[:, None]
    taps = lanczos @ np.where((spread >= 0) & (spread < 4), 0.25, 0.0)
    out = np.zeros((3, 128, 128), np.float64)
    for feature in range(8):
        weight = feature + 4 if feature < 4 else feature - 4
        for r in range(16):
            for second in range(2):
                if 0 <= r - 4 * second <= 10:
                    out[second, feature * 16 + r, :NSHIFT] = taps[:, r - 4 * second]
            out[2, feature * 16 + r, :NSHIFT] = lanczos[:, weight] * 0.25
    return out.astype(np.float32)


def halves(x):
    high = x.astype(BF16)
    return high, (x - high.astype(F32)).astype(BF16)


def dot(a, b):
    return jnp.dot(a, b, preferred_element_type=F32)


def dot_nt(a, b, precision=None):
    return lax.dot_general(a, b, (((1,), (1,)), ((), ())), precision=precision, preferred_element_type=F32)


def total_of(x):
    return jnp.broadcast_to(jnp.sum(x, axis=(0, 1), keepdims=True), (8, 128))


def kernel(
    n_wide, n_narrow,
    frames, anchor, shift, guess, table,
    r_out, w_out, z_out, coef,
    vec, feat, acc, frb, perm, lhs, lhsb,
    from_side, from_row, from_corner, sums_a, sums_b,
    send, recv, fsend, frecv, floc, asend, arecv, bsend, brecv,
):
    column = lax.axis_index("wide")
    row = lax.axis_index("narrow")
    left, right = lax.rem(column + n_wide - 1, n_wide), lax.rem(column + 1, n_wide)
    up, down = lax.rem(row + n_narrow - 1, n_narrow), lax.rem(row + 1, n_narrow)
    core, chip = lax.rem(column, 2), column // 2
    n_chip = n_wide // 2

    def at(w, n):
        return {"wide": w, "narrow": n}

    near = [at(right, row), at(left, row), at(column, down), at(column, up),
            at(right, down), at(left, down), at(right, up), at(left, up)]
    mates_a = [(row + (k // 2), core + (k % 2)) for k in range(1, 2 * n_narrow)]
    mates_a = [at(chip * 2 + lax.rem(c, 2), lax.rem(r, n_narrow)) for r, c in mates_a]
    mates_b = [at(lax.rem(chip + k, n_chip) * 2 + core, row) for k in range(1, n_chip)]

    barrier = pltpu.get_barrier_semaphore()
    everyone = near + mates_a + mates_b
    for device in everyone:
        pl.semaphore_signal(barrier, inc=1, device_id=device, device_id_type=pl.DeviceIdType.MESH)

    own = pltpu.make_async_copy(frames, frb.at[8 * FS : 16 * FS], floc)
    own.start()

    lane = lax.broadcasted_iota(jnp.int32, (8, 128), 1)
    first, last = lane == 0, lane == 127
    edge = first | last

    k_id = lax.broadcasted_iota(jnp.int32, (512, 512), 0)
    n_id = lax.broadcasted_iota(jnp.int32, (512, 512), 1)
    perm[0] = jnp.where(n_id == 128 * lax.rem(k_id, 4) + k_id // 4, 1.0, 0.0).astype(BF16)
    perm[1] = jnp.where(n_id == 4 * lax.rem(k_id, 128) + k_id // 128, 1.0, 0.0).astype(BF16)

    def pack_tile(v, tile, group, inner, sides):
        packed = None
        for q in range(4):
            for part, offset in sides(q):
                term = pltpu.roll(jnp.where(edge, part, 0.0), 4 * q + offset, axis=1)
                packed = term if packed is None else packed + term
        packed = pltpu.roll(packed, 16 * group, axis=1)
        spot = pl.ds(pl.multiple_of(inner * 8, 8), 8)
        vec[v, 4, spot, :] = vec[v, 4, spot, :] + packed

    def place(tile):
        group = tile // GROUP
        return group, tile - group * GROUP

    zero8 = jnp.zeros((8, 128), F32)

    for q in range(4):
        vec[0, q, 0:8, :] = zero8
        vec[0, q, ROWS - 8 : ROWS, :] = zero8
    for v in range(4):
        vec[v, 4] = jnp.zeros((ROWS, 128), F32)

    def spread_guess(b, carry):
        rows = pl.ds(pl.multiple_of(b * 128, 128), 128)
        high, low = halves(guess[rows, :])
        x = dot(high, perm[0]) + dot(low, perm[0])
        for q in range(4):
            vec[0, q, pl.ds(pl.multiple_of(b * 128 + 8, 8), 128), :] = x[:, q * 128 : q * 128 + 128]
        return carry

    lax.fori_loop(0, 4, spread_guess, 0)

    def pack_guess(i, carry):
        for u in range(4):
            tile = 1 + i * 4 + u
            group, inner = place(tile)
            rows = pl.ds(pl.multiple_of(tile * 8, 8), 8)
            pack_tile(0, tile, group, inner, lambda q: ((vec[0, q, rows, :], 1),))
        return carry

    lax.fori_loop(0, 16, pack_guess, 0)
    vec[0, 4, 512:528, :] = vec[0, 4, 72:88, :]

    pl.semaphore_wait(barrier, len(everyone))

    def exchange(v):
        edges = vec.at[v, 4]
        parts = [
            (edges.at[0:PACK], from_side.at[v, 0]),
            (edges.at[0:PACK], from_side.at[v, 1]),
            (vec.at[v, :, 512:528], from_row.at[v, 0]),
            (vec.at[v, :, 0:16], from_row.at[v, 1]),
            (edges.at[72:88], from_corner.at[v, 0]),
            (edges.at[72:88], from_corner.at[v, 1]),
            (edges.at[0:16], from_corner.at[v, 2]),
            (edges.at[0:16], from_corner.at[v, 3]),
        ]
        copies = []
        for k, (source, target) in enumerate(parts):
            copy = pltpu.make_async_remote_copy(
                src_ref=source, dst_ref=target, send_sem=send.at[v, k], recv_sem=recv.at[v, k],
                device_id=near[k], device_id_type=pl.DeviceIdType.MESH)
            copy.start()
            copies.append(copy)
        return copies

    def settle(v, copies):
        for copy in copies:
            copy.wait()
        has_left, has_right = column > 0, column < n_wide - 1
        has_up, has_down = row > 0, row < n_narrow - 1
        lane16 = lax.broadcasted_iota(jnp.int32, (16, 128), 1)
        sub16 = lax.broadcasted_iota(jnp.int32, (16, 128), 0)
        in_top, in_low = lane16 < 16, (lane16 >= 80) & (lane16 < 96)

        def with_rows(middle, above, below):
            above = jnp.where(in_top & has_up, pltpu.roll(above, 48, axis=1), 0.0)
            below = jnp.where(in_low & has_down, pltpu.roll(below, 80, axis=1), 0.0)
            return jnp.concatenate([middle[0:16] + above, middle[16:72], middle[72:88] + below], axis=0)

        mine = with_rows(vec[v, 4, 0:PACK, :], from_row[v, 0, 4], from_row[v, 1, 4])
        lefts = with_rows(from_side[v, 0], from_corner[v, 0], from_corner[v, 2])
        rights = with_rows(from_side[v, 1], from_corner[v, 1], from_corner[v, 3])
        kind = lax.rem(lax.broadcasted_iota(jnp.int32, (PACK, 128), 1), 4)
        other = jnp.where(kind == 1, pltpu.roll(lefts, 127, axis=1), 0.0)
        other = jnp.where(kind == 3, pltpu.roll(lefts, 3, axis=1), other)
        other = jnp.where(((kind == 1) | (kind == 3)) & has_left, other, 0.0)
        facing = jnp.where(kind == 0, pltpu.roll(rights, 125, axis=1), 0.0)
        facing = jnp.where(kind == 2, pltpu.roll(rights, 1, axis=1), facing)
        facing = jnp.where(((kind == 0) | (kind == 2)) & has_right, facing, 0.0)
        both = mine + other + facing
        both = jnp.where((kind == 3) & (column == 0), 0.0, both)
        both = jnp.where((kind == 2) & (column == n_wide - 1), 0.0, both)
        top = jnp.where(in_top & (sub16 < 8) & (row == 0), 0.0, both[0:16])
        low = jnp.where(in_low & (sub16 >= 8) & (row == n_narrow - 1), 0.0, both[72:88])
        vec[v, 4, 0:PACK, :] = jnp.concatenate([top, both[16:72], low], axis=0)
        for q in range(4):
            x = vec[v, q, 0:16, :] + jnp.where(has_up, from_row[v, 0, q], 0.0)
            vec[v, q, 0:16, :] = jnp.where((sub16 < 8) & (row == 0), 0.0, x)
            x = vec[v, q, 512:528, :] + jnp.where(has_down, from_row[v, 1, q], 0.0)
            vec[v, q, 512:528, :] = jnp.where((sub16 >= 8) & (row == n_narrow - 1), 0.0, x)

    moves = exchange(0)
    frame_moves = []
    for k, device in enumerate((at(right, row), at(left, row))):
        copy = pltpu.make_async_remote_copy(
            src_ref=frames, dst_ref=frb.at[16 * FS * k : 16 * FS * k + 8 * FS], send_sem=fsend.at[k],
            recv_sem=frecv.at[k], device_id=device, device_id_type=pl.DeviceIdType.MESH)
        copy.start()
        frame_moves.append(copy)

    n_frames = 8 * n_wide
    f_id = lax.broadcasted_iota(jnp.int32, (n_frames, 128), 0)
    slot = lax.broadcasted_iota(jnp.int32, (n_frames, 128), 1)
    slot = slot - (slot // 32) * 32
    wanted = lax.rem(slot + 8 * left, n_frames)
    pick = jnp.where((f_id == wanted) & (slot < 24), 1.0, 0.0).astype(BF16)
    looks = jnp.where(jnp.broadcast_to(anchor[...], (16, n_frames)) == column, 1.0, 0.0).astype(BF16)
    used = dot(looks, pick)[0:1]
    codes = [shift[0, pl.ds(pl.multiple_of(8 * o, 8), 8), :] for o in (left, column, right)]
    codes = jnp.concatenate((codes + [jnp.zeros((8, 2), jnp.int32)]) * 4, axis=0)
    lane128 = lax.broadcasted_iota(jnp.int32, (128, 128), 1)
    one_a = jnp.where(codes[:, 0:1] == lane128, 1.0, 0.0)
    one_b = jnp.where(codes[:, 1:2] == lane128, 1.0, 0.0)
    second = lax.rem(lane128 // 32, 2) == 1
    tall = dot_nt(table[2], one_b, HIGHEST) * jnp.where(
        second, dot_nt(table[1], one_a, HIGHEST), dot_nt(table[0], one_a, HIGHEST)) * used
    for which, keep in enumerate((second, lane128 >= 0, jnp.logical_not(second))):
        kept = jnp.where(keep, tall, 0.0)
        high, low = halves(kept)
        lhsb[which, :, 0:128] = high
        lhsb[which, :, 128:256] = jnp.where(lane128 < 64, low.astype(F32), 0.0).astype(BF16)
        half = jnp.where(lane128 < 64, kept, 0.0)
        high, low = halves(dot_nt(half, half, HIGHEST))
        lhs[which, :, 0:128] = high
        lhs[which, :, 128:256] = high
        lhs[which, :, 256:384] = low

    settle(0, moves)

    def unfold(v):
        def tile_step(tile):
            group, inner = place(tile)
            rows = pl.ds(pl.multiple_of(tile * 8, 8), 8)
            packed = vec[v, 4, pl.ds(pl.multiple_of(inner * 8, 8), 8), :]
            packed = pltpu.roll(packed, 127 - 16 * group, axis=1)
            mid, nxt, prv = [], [], []
            for q in range(4):
                spun = packed if q == 0 else pltpu.roll(packed, 128 - 4 * q, axis=1)
                x = jnp.where(edge, spun, vec[v, q, rows, :])
                vec[v, q, rows, :] = x
                side = pltpu.roll(packed, 126 - 4 * q, axis=1)
                mid.append(x)
                prv.append(jnp.where(first, side, pltpu.roll(x, 1, axis=1)))
                if q < 3:
                    nxt.append(jnp.where(last, side, pltpu.roll(x, 127, axis=1)))
            m23, p23 = mid[2] + mid[3], prv[2] + prv[3]
            m123, p123 = mid[1] + m23, prv[1] + p23
            m01, n01 = mid[0] + mid[1], nxt[0] + nxt[1]
            out = [mid[0] + m123, m123 + nxt[0], m23 + n01, mid[3] + (n01 + nxt[2]),
                   prv[0] + p123, p123 + mid[0], p23 + m01, prv[3] + (m01 + mid[2])]
            for f in range(8):
                feat[f, rows, :] = out[f]

        def step(i, carry):
            for u in range(3):
                tile_step(i * 3 + u)
            return carry

        lax.fori_loop(0, TILES // 3, step, 0)

    def blocks(starts):
        highs, lows = [], []
        for start in starts:
            pairs = [halves(feat[f, pl.ds(start, 16), :]) for f in range(8)]
            highs.append(jnp.concatenate([p[0] for p in pairs], axis=0))
            lows.append(jnp.concatenate([p[1] for p in pairs], axis=0))
        high = highs[0] if len(starts) == 1 else jnp.concatenate(highs, axis=1)
        low = lows[0] if len(starts) == 1 else jnp.concatenate(lows, axis=1)
        return jnp.concatenate([high, low, high], axis=0)

    def mix():
        out = dot(lhs[0], blocks([0]))
        for f in range(8):
            acc[f, 0:8, :] = out[16 * f : 16 * f + 8]
        carry = tuple(out[16 * f + 8 : 16 * f + 16] for f in range(8))

        def pair(i, carry):
            start = pl.multiple_of(8 + i * 16, 8)
            out = dot(lhs[1], blocks([start, start + 8]))
            later = []
            for f in range(8):
                acc[f, pl.ds(start, 8), :] = carry[f] + out[16 * f : 16 * f + 8, 0:128]
                acc[f, pl.ds(start + 8, 8), :] = (
                    out[16 * f + 8 : 16 * f + 16, 0:128] + out[16 * f : 16 * f + 8, 128:256])
                later.append(out[16 * f + 8 : 16 * f + 16, 128:256])
            return tuple(later)

        carry = lax.fori_loop(0, 31, pair, carry)
        for start, which in ((504, 1), (512, 2)):
            out = dot(lhs[which], blocks([start]))
            for f in range(8):
                acc[f, start : start + 8, :] = carry[f] + out[16 * f : 16 * f + 8]
            carry = tuple(out[16 * f + 8 : 16 * f + 16] for f in range(8))
        for f in range(8):
            acc[f, 520:528, :] = carry[f]

    def take_frames():
        def block(start, before, after, which):
            parts = []
            for i in (before, after):
                parts.append(frb[pl.ds(i, 24, stride=FS), :])
                parts.append(zero8)
            high, low = halves(jnp.concatenate(parts, axis=0))
            both = jnp.concatenate([high, low], axis=0)
            out = dot(lhsb[which, :, 0:128], both) + dot(lhsb[which, :, 128:256], both)
            for f in range(8):
                acc[f, pl.ds(start, 16), :] = acc[f, pl.ds(start, 16), :] - out[16 * f : 16 * f + 16]

        block(0, 0, 0, 0)

        def step(i, carry):
            for u in range(3):
                a = 1 + i * 3 + u
                block(pl.multiple_of(8 * a, 8), 2 * a - 1, 2 * a, 1)
            return carry

        lax.fori_loop(0, 21, step, 0)
        block(512, 127, 127, 2)

    def fold(v, sign, measure):
        def tile_step(tile, inside, sums):
            group, inner = place(tile)
            rows = pl.ds(pl.multiple_of(tile * 8, 8), 8)
            cur = [acc[q, rows, :] for q in range(4)]
            pre = [acc[4 + q, rows, :] for q in range(4)]
            rolled = [pltpu.roll(x, 127, axis=1) for x in pre]
            here = [c + jnp.where(last, 0.0, p) for c, p in zip(cur, rolled)]
            back = [p + jnp.where(last, 0.0, c) for c, p in zip(cur, rolled)]
            h01 = here[0] + here[1]
            h012 = h01 + here[2]
            k23 = back[2] + back[3]
            out = [here[0] + pltpu.roll(back[1] + k23, 1, axis=1), h01 + pltpu.roll(k23, 1, axis=1),
                   h012 + pltpu.roll(back[3], 1, axis=1), h012 + here[3]]
            h23 = here[2] + here[3]
            r01 = pre[0] + pre[1]
            r012 = r01 + pre[2]
            over = [jnp.where(first, pre[0], here[1] + h23), jnp.where(first, r01, h23),
                    jnp.where(first, r012, here[3]), jnp.where(first, r012 + pre[3], 0.0)]
            old = [vec[v, q, rows, :] for q in range(4)]
            if inside:
                out = [o + DAMP * x for o, x in zip(out, old)]
            if sign < 0:
                out, over = [-o for o in out], [-o for o in over]
            for q in range(4):
                vec[v + 1, q, rows, :] = out[q]
            pack_tile(v + 1, tile, group, inner, lambda q: ((out[q], 1), (over[q], 3)))
            return measure(rows, inside, old, out, sums)

        def step(i, sums):
            for u in range(4):
                sums = tile_step(1 + i * 4 + u, True, sums)
            return sums

        sums = tile_step(0, False, (zero8, zero8, zero8))
        sums = lax.fori_loop(0, 16, step, sums)
        sums = tile_step(TILES - 1, False, sums)
        vec[v + 1, 4, 512:528, :] = vec[v + 1, 4, 72:88, :]
        return sums

    def outer_columns(product):
        kind = lax.rem(lax.broadcasted_iota(jnp.int32, (PACK, 128), 1), 4)
        product = jnp.where(kind >= 2, product, 0.0)
        while product.shape[0] > 8:
            product = product[0:8] + product[8:] if product.shape[0] == 16 else jnp.concatenate(
                [product[0:8] + product[8:16], product[16:]], axis=0)
        return product

    def gather_a(call, values):
        for i, value in enumerate(values):
            sums_a[call, 0, i] = value
        copies = []
        for k, device in enumerate(mates_a):
            copy = pltpu.make_async_remote_copy(
                src_ref=sums_a.at[call, 0], dst_ref=sums_a.at[call, k + 1], send_sem=asend.at[call, k],
                recv_sem=arecv.at[call, k], device_id=device, device_id_type=pl.DeviceIdType.MESH)
            copy.start()
            copies.append(copy)
        return copies

    def gather_b(call, copies):
        for copy in copies:
            copy.wait()
        for i in range(3):
            value = sums_a[call, 0, i]
            for k in range(len(mates_a)):
                value = value + sums_a[call, k + 1, i]
            sums_b[call, 0, i] = value
        copies = []
        for k, device in enumerate(mates_b):
            copy = pltpu.make_async_remote_copy(
                src_ref=sums_b.at[call, 0], dst_ref=sums_b.at[call, k + 1], send_sem=bsend.at[call, k],
                recv_sem=brecv.at[call, k], device_id=device, device_id_type=pl.DeviceIdType.MESH)
            copy.start()
            copies.append(copy)
        return copies

    def finish_sums(call, copies):
        for copy in copies:
            copy.wait()
        values = []
        for i in range(3):
            value = sums_b[call, 0, i]
            for k in range(len(mates_b)):
                value = value + sums_b[call, k + 1, i]
            values.append(total_of(value))
        return values

    def write_pixels(v, out):
        def step(b, carry):
            rows = pl.ds(pl.multiple_of(b * 128 + 8, 8), 128)
            x = jnp.concatenate([vec[v, q, rows, :] for q in range(4)], axis=1)
            high, low = halves(x)
            out[pl.ds(pl.multiple_of(b * 128, 128), 128), :] = dot(high, perm[1]) + dot(low, perm[1])
            return carry

        lax.fori_loop(0, 4, step, 0)

    def patch_edges(v):
        def step(i, carry):
            for u in range(4):
                tile = 1 + i * 4 + u
                group, inner = place(tile)
                rows = pl.ds(pl.multiple_of(tile * 8, 8), 8)
                packed = vec[v, 4, pl.ds(pl.multiple_of(inner * 8, 8), 8), :]
                packed = pltpu.roll(packed, 127 - 16 * group, axis=1)
                for q in range(4):
                    spun = packed if q == 0 else pltpu.roll(packed, 128 - 4 * q, axis=1)
                    vec[v, q, rows, :] = jnp.where(edge, spun, vec[v, q, rows, :])
            return carry

        lax.fori_loop(0, 16, step, 0)

    unfold(0)
    mix()
    own.wait()
    for copy in frame_moves:
        copy.wait()
    take_frames()
    fold(0, -1.0, lambda rows, inside, old, out, sums: sums)
    settle(1, exchange(1))

    unfold(1)
    mix()

    def measure_w(rows, inside, old, out, sums):
        rr, rw, _ = sums
        for q in range(4):
            rw = rw + old[q] * out[q]
            if inside:
                rr = rr + old[q] * old[q]
        return rr, rw, zero8

    rr, rw, _ = fold(1, 1.0, measure_w)
    rw = rw + outer_columns(vec[1, 4, 0:PACK, :] * vec[2, 4, 0:PACK, :])
    moves = exchange(2)
    first_sums = gather_a(0, (rr, rw, zero8))
    write_pixels(1, r_out)
    settle(2, moves)
    first_sums = gather_b(0, first_sums)

    unfold(2)
    mix()
    rr, rw, _ = finish_sums(0, first_sums)
    alpha = rr / rw

    def measure_z(rows, inside, old, out, sums):
        ss, sw, sz = sums
        for q in range(4):
            s = vec[1, q, rows, :] - alpha * old[q]
            sz = sz + s * out[q]
            if inside:
                ss = ss + s * s
                sw = sw + s * old[q]
        return ss, sw, sz

    ss, sw, sz = fold(2, 1.0, measure_z)
    s_edge = vec[1, 4, 0:PACK, :] - alpha[0:1, :] * vec[2, 4, 0:PACK, :]
    sz = sz + outer_columns(s_edge * vec[3, 4, 0:PACK, :])
    last_sums = gather_a(1, (ss, sw, sz))
    moves = exchange(3)
    write_pixels(2, w_out)
    last_sums = gather_b(1, last_sums)
    settle(3, moves)
    patch_edges(3)
    write_pixels(3, z_out)
    ss, sw, sz = finish_sums(1, last_sums)
    beta = ss / rr
    curve = (sw - alpha * sz) + 2.0 * beta * sw + beta * beta * rw
    step = ss / curve
    coef[0] = alpha + step * (1.0 + beta)
    coef[1] = step * alpha


def on_device(n_wide, n_narrow, frames, anchor, shift, guess):
    vmem = pl.BlockSpec(memory_space=pltpu.VMEM)
    image = jax.ShapeDtypeStruct((TS, TS), F32)
    dma = pltpu.SemaphoreType.DMA
    n_a, n_b = 2 * n_narrow, n_wide // 2
    r, w, z, coef = pl.pallas_call(
        functools.partial(kernel, n_wide, n_narrow),
        out_shape=(image, image, image, jax.ShapeDtypeStruct((2, 8, 128), F32)),
        in_specs=[pl.BlockSpec(memory_space=pl.ANY), vmem, vmem, vmem, vmem],
        out_specs=(vmem, vmem, vmem, vmem),
        scratch_shapes=[
            pltpu.VMEM((4, 5, ROWS, 128), F32),
            pltpu.VMEM((8, ROWS, 128), F32),
            pltpu.VMEM((8, ROWS, 128), F32),
            pltpu.VMEM((24 * FS, 128), F32),
            pltpu.VMEM((2, 512, 512), BF16),
            pltpu.VMEM((3, 128, 384), BF16),
            pltpu.VMEM((3, 128, 256), BF16),
            pltpu.VMEM((4, 2, PACK, 128), F32),
            pltpu.VMEM((4, 2, 5, 16, 128), F32),
            pltpu.VMEM((4, 4, 16, 128), F32),
            pltpu.VMEM((2, n_a, 3, 8, 128), F32),
            pltpu.VMEM((2, n_b, 3, 8, 128), F32),
            dma((4, 8)), dma((4, 8)), dma((2,)), dma((2,)), dma,
            dma((2, n_a)), dma((2, n_a)), dma((2, n_b)), dma((2, n_b)),
        ],
        compiler_params=pltpu.CompilerParams(
            collective_id=0, has_side_effects=True, vmem_limit_bytes=48 * 2**20),
    )(frames.reshape(8 * FS, FS), anchor, shift, guess, jnp.asarray(tables()))
    c1, c2 = coef[0, 0, 0], coef[1, 0, 0]
    return guess + c1 * r - c2 * w, r - c1 * w + c2 * z


def solution(mesh):
    placed = (P("narrow", "wide", None, None), P("narrow", None), P("narrow", None, None), P("narrow", "wide"))
    return jax.shard_map(
        functools.partial(on_device, mesh.shape["wide"], mesh.shape["narrow"]),
        mesh=mesh,
        in_specs=placed,
        out_specs=(P("narrow", "wide"), P("narrow", "wide")),
        check_vma=False,
    )
```

```python
import functools

import jax
import jax.numpy as jnp
import numpy as np
from jax import lax
from jax.experimental import pallas as pl
from jax.experimental.pallas import tpu as pltpu
from jax.sharding import PartitionSpec as P

NSHIFT = 16
DAMP = 0.05
TS = 512
FS = 128
ROWS = TS + 16
TILES = ROWS // 8
GROUP = 11
PACK = GROUP * 8
F32 = jnp.float32
BF16 = jnp.bfloat16
UNFOLD = 264
FOLD = 264
MIX = 32
HIGHEST = lax.Precision.HIGHEST


def tables():
    fraction = np.arange(NSHIFT, dtype=np.float64) / NSHIFT
    offsets = np.arange(8, dtype=np.float64)[None, :] - 3.0 - fraction[:, None]
    lanczos = np.sinc(offsets) * np.sinc(offsets / 4.0)
    lanczos = lanczos / lanczos.sum(axis=1, keepdims=True)
    spread = np.arange(11)[None, :] - np.arange(8)[:, None]
    taps = lanczos @ np.where((spread >= 0) & (spread < 4), 0.25, 0.0)
    out = np.zeros((3, 128, 128), np.float64)
    for feature in range(8):
        weight = feature + 4 if feature < 4 else feature - 4
        for r in range(16):
            for second in range(2):
                if 0 <= r - 4 * second <= 10:
                    out[second, feature * 16 + r, :NSHIFT] = taps[:, r - 4 * second]
            out[2, feature * 16 + r, :NSHIFT] = lanczos[:, weight] * 0.25
    return out.astype(np.float32)


def halves(x):
    high = x.astype(BF16)
    return high, (x - high.astype(F32)).astype(BF16)


def dot(a, b):
    return jnp.dot(a, b, preferred_element_type=F32)


def dot_nt(a, b, precision=None):
    return lax.dot_general(a, b, (((1,), (1,)), ((), ())), precision=precision, preferred_element_type=F32)


def total_of(x):
    return jnp.broadcast_to(jnp.sum(x, axis=(0, 1), keepdims=True), (8, 128))


def kernel(
    n_wide, n_narrow,
    frames, anchor, shift, guess, table,
    r_out, w_out, z_out, coef,
    vec, whole, wide_edges, feat, acc, more, frb, perm, lhs, lhsb,
    from_side, from_row, from_corner, sums_a, sums_b,
    send, recv, fsend, frecv, floc, asend, arecv, bsend, brecv,
):
    column = lax.axis_index("wide")
    row = lax.axis_index("narrow")
    left, right = lax.rem(column + n_wide - 1, n_wide), lax.rem(column + 1, n_wide)
    up, down = lax.rem(row + n_narrow - 1, n_narrow), lax.rem(row + 1, n_narrow)
    core, chip = lax.rem(column, 2), column // 2
    n_chip = n_wide // 2

    def at(w, n):
        return {"wide": w, "narrow": n}

    near = [at(right, row), at(left, row), at(column, down), at(column, up),
            at(right, down), at(left, down), at(right, up), at(left, up)]
    mates_a = [(row + (k // 2), core + (k % 2)) for k in range(1, 2 * n_narrow)]
    mates_a = [at(chip * 2 + lax.rem(c, 2), lax.rem(r, n_narrow)) for r, c in mates_a]
    mates_b = [at(lax.rem(chip + k, n_chip) * 2 + core, row) for k in range(1, n_chip)]

    barrier = pltpu.get_barrier_semaphore()
    everyone = near + mates_a + mates_b
    for device in everyone:
        pl.semaphore_signal(barrier, inc=1, device_id=device, device_id_type=pl.DeviceIdType.MESH)

    own = pltpu.make_async_copy(frames, frb.at[8 * FS : 16 * FS], floc)
    own.start()

    k_id = lax.broadcasted_iota(jnp.int32, (512, 128), 0)
    n_id = lax.broadcasted_iota(jnp.int32, (512, 128), 1)
    for which, target in enumerate((128 * (k_id & 3) + (k_id >> 2), 4 * (k_id & 127) + (k_id >> 7))):
        for c in range(4):
            perm[which, :, c * 128 : c * 128 + 128] = jnp.where(n_id + 128 * c == target, 1.0, 0.0).astype(BF16)

    zero8 = jnp.zeros((8, 128), F32)

    def edge_masks(size):
        lane = lax.broadcasted_iota(jnp.int32, (size, 128), 1)
        return lane == 0, lane == 127

    def gather_edges(sides):
        packed = None
        for shift_by, part in sides:
            first, last = edge_masks(part.shape[0])
            term = pltpu.roll(jnp.where(first | last, part, 0.0), shift_by, axis=1)
            packed = term if packed is None else packed + term
        return packed

    def pack(v):
        packed = wide_edges[0:PACK, :]
        for g in range(1, 6):
            packed = packed + pltpu.roll(wide_edges[g * PACK : g * PACK + PACK, :], 16 * g, axis=1)
        vec[v, 4, 0:PACK, :] = packed
        vec[v, 4, 512:528, :] = packed[72:88]

    def unpack(v):
        for g in range(6):
            wide_edges[g * PACK : g * PACK + PACK, :] = pltpu.roll(vec[v, 4, 0:PACK, :], 127 - 16 * g, axis=1)

    for q in range(4):
        vec[0, q, 0:8, :] = zero8
        vec[0, q, ROWS - 8 : ROWS, :] = zero8
    wide_edges[0:8, :] = zero8
    wide_edges[ROWS - 8 : ROWS, :] = zero8

    def spread_guess(b, carry):
        rows = pl.ds(pl.multiple_of(b * 128, 128), 128)
        into = pl.ds(pl.multiple_of(b * 128 + 8, 8), 128)
        high, low = halves(guess[rows, :])
        x = dot(high, perm[0]) + dot(low, perm[0])
        x = [x[:, q * 128 : q * 128 + 128] for q in range(4)]
        for q in range(4):
            vec[0, q, into, :] = x[q]
        wide_edges[into, :] = gather_edges([(4 * q + 1, x[q]) for q in range(4)])
        return carry

    lax.fori_loop(0, 4, spread_guess, 0)
    pack(0)

    pl.semaphore_wait(barrier, len(everyone))

    def exchange(v):
        edges = vec.at[v, 4]
        parts = [
            (edges.at[0:PACK], from_side.at[v, 0]),
            (edges.at[0:PACK], from_side.at[v, 1]),
            (vec.at[v, :, 512:528], from_row.at[v, 0]),
            (vec.at[v, :, 0:16], from_row.at[v, 1]),
            (edges.at[72:88], from_corner.at[v, 0]),
            (edges.at[72:88], from_corner.at[v, 1]),
            (edges.at[0:16], from_corner.at[v, 2]),
            (edges.at[0:16], from_corner.at[v, 3]),
        ]
        copies = []
        for k, (source, target) in enumerate(parts):
            copy = pltpu.make_async_remote_copy(
                src_ref=source, dst_ref=target, send_sem=send.at[v, k], recv_sem=recv.at[v, k],
                device_id=near[k], device_id_type=pl.DeviceIdType.MESH)
            copy.start()
            copies.append(copy)
        return copies

    def settle(v, copies):
        for copy in copies:
            copy.wait()
        has_left, has_right = column > 0, column < n_wide - 1
        has_up, has_down = row > 0, row < n_narrow - 1
        lane16 = lax.broadcasted_iota(jnp.int32, (16, 128), 1)
        sub16 = lax.broadcasted_iota(jnp.int32, (16, 128), 0)
        in_top, in_low = lane16 < 16, (lane16 >= 80) & (lane16 < 96)

        def with_rows(middle, above, below):
            above = jnp.where(in_top & has_up, pltpu.roll(above, 48, axis=1), 0.0)
            below = jnp.where(in_low & has_down, pltpu.roll(below, 80, axis=1), 0.0)
            return jnp.concatenate([middle[0:16] + above, middle[16:72], middle[72:88] + below], axis=0)

        mine = with_rows(vec[v, 4, 0:PACK, :], from_row[v, 0, 4], from_row[v, 1, 4])
        lefts = with_rows(from_side[v, 0], from_corner[v, 0], from_corner[v, 2])
        rights = with_rows(from_side[v, 1], from_corner[v, 1], from_corner[v, 3])
        kind = lax.rem(lax.broadcasted_iota(jnp.int32, (PACK, 128), 1), 4)
        other = jnp.where(kind == 1, pltpu.roll(lefts, 127, axis=1), 0.0)
        other = jnp.where(kind == 3, pltpu.roll(lefts, 3, axis=1), other)
        other = jnp.where(((kind == 1) | (kind == 3)) & has_left, other, 0.0)
        facing = jnp.where(kind == 0, pltpu.roll(rights, 125, axis=1), 0.0)
        facing = jnp.where(kind == 2, pltpu.roll(rights, 1, axis=1), facing)
        facing = jnp.where(((kind == 0) | (kind == 2)) & has_right, facing, 0.0)
        both = mine + other + facing
        both = jnp.where((kind == 3) & (column == 0), 0.0, both)
        both = jnp.where((kind == 2) & (column == n_wide - 1), 0.0, both)
        top = jnp.where(in_top & (sub16 < 8) & (row == 0), 0.0, both[0:16])
        low = jnp.where(in_low & (sub16 >= 8) & (row == n_narrow - 1), 0.0, both[72:88])
        vec[v, 4, 0:PACK, :] = jnp.concatenate([top, both[16:72], low], axis=0)
        for q in range(4):
            x = vec[v, q, 0:16, :] + jnp.where(has_up, from_row[v, 0, q], 0.0)
            vec[v, q, 0:16, :] = jnp.where((sub16 < 8) & (row == 0), 0.0, x)
            x = vec[v, q, 512:528, :] + jnp.where(has_down, from_row[v, 1, q], 0.0)
            vec[v, q, 512:528, :] = jnp.where((sub16 >= 8) & (row == n_narrow - 1), 0.0, x)

    moves = exchange(0)
    frame_moves = []
    for k, device in enumerate((at(right, row), at(left, row))):
        copy = pltpu.make_async_remote_copy(
            src_ref=frames, dst_ref=frb.at[16 * FS * k : 16 * FS * k + 8 * FS], send_sem=fsend.at[k],
            recv_sem=frecv.at[k], device_id=device, device_id_type=pl.DeviceIdType.MESH)
        copy.start()
        frame_moves.append(copy)

    n_frames = 8 * n_wide
    f_id = lax.broadcasted_iota(jnp.int32, (n_frames, 128), 0)
    slot = lax.broadcasted_iota(jnp.int32, (n_frames, 128), 1)
    slot = slot - (slot // 32) * 32
    wanted = lax.rem(slot + 8 * left, n_frames)
    pick = jnp.where((f_id == wanted) & (slot < 24), 1.0, 0.0).astype(BF16)
    looks = jnp.where(jnp.broadcast_to(anchor[...], (16, n_frames)) == column, 1.0, 0.0).astype(BF16)
    used = dot(looks, pick)[0:1]
    codes = [shift[0, pl.ds(pl.multiple_of(8 * o, 8), 8), :] for o in (left, column, right)]
    codes = jnp.concatenate((codes + [jnp.zeros((8, 2), jnp.int32)]) * 4, axis=0)
    lane128 = lax.broadcasted_iota(jnp.int32, (128, 128), 1)
    one_a = jnp.where(codes[:, 0:1] == lane128, 1.0, 0.0)
    one_b = jnp.where(codes[:, 1:2] == lane128, 1.0, 0.0)
    second = lax.rem(lane128 // 32, 2) == 1
    tall = dot_nt(table[2], one_b, HIGHEST) * jnp.where(
        second, dot_nt(table[1], one_a, HIGHEST), dot_nt(table[0], one_a, HIGHEST)) * used
    for which, keep in enumerate((second, lane128 >= 0, jnp.logical_not(second))):
        kept = jnp.where(keep, tall, 0.0)
        high, low = halves(kept)
        lhsb[which, :, 0:128] = high
        lhsb[which, :, 128:256] = jnp.where(lane128 < 64, low.astype(F32), 0.0).astype(BF16)
        half = jnp.where(lane128 < 64, kept, 0.0)
        high, low = halves(dot_nt(half, half, HIGHEST))
        lhs[which, :, 0:128] = high
        lhs[which, :, 128:256] = high
        lhs[which, :, 256:384] = low

    settle(0, moves)

    def unfold(v, features=True):
        unpack(v)

        def step(i, carry):
            rows = pl.ds(pl.multiple_of(i * UNFOLD, 8), UNFOLD)
            first, last = edge_masks(UNFOLD)
            packed = wide_edges[rows, :]
            raw = [vec[v, q, rows, :] for q in range(4)]
            mid, nxt, prv = [], [], []
            for q in range(4):
                spun = packed if q == 0 else pltpu.roll(packed, 128 - 4 * q, axis=1)
                x = jnp.where(first | last, spun, raw[q])
                mid.append(x)
                if features:
                    side = pltpu.roll(packed, 126 - 4 * q, axis=1)
                    prv.append(jnp.where(first, side, pltpu.roll(x, 1, axis=1)))
                    if q < 3:
                        nxt.append(jnp.where(last, side, pltpu.roll(x, 127, axis=1)))
            for q in range(4):
                whole[v, q, rows, :] = mid[q]
            if not features:
                return carry
            m23, p23 = mid[2] + mid[3], prv[2] + prv[3]
            m123, p123 = mid[1] + m23, prv[1] + p23
            m01, n01 = mid[0] + mid[1], nxt[0] + nxt[1]
            out = [mid[0] + m123, m123 + nxt[0], m23 + n01, mid[3] + (n01 + nxt[2]),
                   prv[0] + p123, p123 + mid[0], p23 + m01, prv[3] + (m01 + mid[2])]
            for f in range(8):
                feat[f, rows, :] = out[f]
            return carry

        lax.fori_loop(0, ROWS // UNFOLD, step, 0)

    def join(parts):
        return parts[0] if len(parts) == 1 else jnp.concatenate(parts, axis=1)

    def blocks(starts):
        highs, lows = [], []
        for start in starts:
            pairs = [halves(feat[f, pl.ds(start, 16), :]) for f in range(8)]
            highs.append(jnp.concatenate([p[0] for p in pairs], axis=0))
            lows.append(jnp.concatenate([p[1] for p in pairs], axis=0))
        high, low = join(highs), join(lows)
        return jnp.concatenate([high, low, high], axis=0)

    def stack(outs, carry):
        done = []
        for out in outs:
            done.append([out[16 * f : 16 * f + 8] if carry is None else carry[f] + out[16 * f : 16 * f + 8]
                         for f in range(8)])
            carry = [out[16 * f + 8 : 16 * f + 16] for f in range(8)]
        return done, carry

    def sweep(results, save):
        def some(starts, kinds, carry):
            outs = []
            for k in range(0, len(starts), 2):
                outs.extend(results(starts[k : k + 2], kinds[k : k + 2]))
            done, carry = stack(outs, carry)
            for start, tiles in zip(starts, done):
                save(start, tiles)
            return tuple(carry)

        carry = some([8 * k for k in range(MIX)], [0] + [1] * (MIX - 1), None)

        def step(i, carry):
            start = pl.multiple_of(i * (8 * MIX), 8)
            return some([start + 8 * k for k in range(MIX)], [1] * MIX, carry)

        carry = lax.fori_loop(1, 64 // MIX, step, carry)
        carry = some([512], [2], carry)
        save(520, carry)

    def cut(out):
        return [out[:, 128 * k : 128 * k + 128] for k in range(out.shape[1] // 128)]

    def mix():
        def results(starts, kinds):
            if len(set(kinds)) > 1:
                return [dot(lhs[w], blocks([s])) for s, w in zip(starts, kinds)]
            return cut(dot(lhs[kinds[0]], blocks(starts)))

        def save(start, tiles):
            for f in range(8):
                acc[f, pl.ds(start, 8), :] = tiles[f]

        sweep(results, save)

    def take_frames():
        def pixels(start, kind):
            sample = start // 4
            rows = [0 if kind == 0 else sample - 1, FS - 1 if kind == 2 else sample]
            parts = []
            for i in rows:
                parts += [frb[pl.ds(i, 24, stride=FS), :], zero8]
            high, low = halves(jnp.concatenate(parts, axis=0))
            return jnp.concatenate([high, low], axis=0)

        def results(starts, kinds):
            if len(set(kinds)) > 1:
                return [results([s], [w])[0] for s, w in zip(starts, kinds)]
            both = join([pixels(s, w) for s, w in zip(starts, kinds)])
            return cut(dot(lhsb[kinds[0]], jnp.concatenate([both, both], axis=0)))

        def save(start, tiles):
            for f in range(8):
                more[f, pl.ds(start, 8), :] = tiles[f]

        sweep(results, save)

    def fold(v, sign, measure, counts):
        def step(i, sums):
            rows = pl.ds(pl.multiple_of(i * FOLD, 8), FOLD)
            first, last = edge_masks(FOLD)
            row_id = i * FOLD + lax.broadcasted_iota(jnp.int32, (FOLD, 128), 0)
            inside = (row_id >= 8) & (row_id < ROWS - 8)
            damp = jnp.where(inside, DAMP, 0.0)
            cur = [acc[q, rows, :] for q in range(4)]
            pre = [acc[4 + q, rows, :] for q in range(4)]
            if v == 0:
                cur = [c - more[q, rows, :] for q, c in enumerate(cur)]
                pre = [p - more[4 + q, rows, :] for q, p in enumerate(pre)]
            old = [whole[v, q, rows, :] for q in range(4)]
            rolled = [pltpu.roll(x, 127, axis=1) for x in pre]
            here = [c + jnp.where(last, 0.0, p) for c, p in zip(cur, rolled)]
            back = [p + jnp.where(last, 0.0, c) for c, p in zip(cur, rolled)]
            h01 = here[0] + here[1]
            h012 = h01 + here[2]
            k23 = back[2] + back[3]
            out = [here[0] + pltpu.roll(back[1] + k23, 1, axis=1), h01 + pltpu.roll(k23, 1, axis=1),
                   h012 + pltpu.roll(back[3], 1, axis=1), h012 + here[3]]
            h23 = here[2] + here[3]
            r01 = pre[0] + pre[1]
            r012 = r01 + pre[2]
            over = [jnp.where(first, pre[0], here[1] + h23), jnp.where(first, r01, h23),
                    jnp.where(first, r012, here[3]), jnp.where(first, r012 + pre[3], 0.0)]
            out = [o + damp * x for o, x in zip(out, old)]
            if sign < 0:
                out, over = [-o for o in out], [-o for o in over]
            packed = gather_edges([(4 * q + 1, out[q]) for q in range(4)] + [(4 * q + 3, over[q]) for q in range(4)])
            more_sums = measure(rows, inside, old, out)
            for q in range(4):
                vec[v + 1, q, rows, :] = out[q]
            wide_edges[rows, :] = packed
            return tuple(s + m for s, m in zip(sums, more_sums))

        sums = lax.fori_loop(0, ROWS // FOLD, step, (jnp.zeros((FOLD, 128), F32),) * counts)
        pack(v + 1)
        return [fewer_rows(s) for s in sums]

    def fewer_rows(x):
        total = x[0:8]
        for k in range(8, x.shape[0], 8):
            total = total + x[k : k + 8]
        return total

    def outer_columns(product):
        kind = lax.broadcasted_iota(jnp.int32, (PACK, 128), 1) & 3
        return fewer_rows(jnp.where(kind >= 2, product, 0.0))

    def gather_a(call, values):
        for i, value in enumerate(values):
            sums_a[call, 0, i] = value
        copies = []
        for k, device in enumerate(mates_a):
            copy = pltpu.make_async_remote_copy(
                src_ref=sums_a.at[call, 0], dst_ref=sums_a.at[call, k + 1], send_sem=asend.at[call, k],
                recv_sem=arecv.at[call, k], device_id=device, device_id_type=pl.DeviceIdType.MESH)
            copy.start()
            copies.append(copy)
        return copies

    def gather_b(call, copies):
        for copy in copies:
            copy.wait()
        for i in range(3):
            value = sums_a[call, 0, i]
            for k in range(len(mates_a)):
                value = value + sums_a[call, k + 1, i]
            sums_b[call, 0, i] = value
        copies = []
        for k, device in enumerate(mates_b):
            copy = pltpu.make_async_remote_copy(
                src_ref=sums_b.at[call, 0], dst_ref=sums_b.at[call, k + 1], send_sem=bsend.at[call, k],
                recv_sem=brecv.at[call, k], device_id=device, device_id_type=pl.DeviceIdType.MESH)
            copy.start()
            copies.append(copy)
        return copies

    def finish_sums(call, copies):
        for copy in copies:
            copy.wait()
        values = []
        for i in range(3):
            value = sums_b[call, 0, i]
            for k in range(len(mates_b)):
                value = value + sums_b[call, k + 1, i]
            values.append(total_of(value))
        return values

    def write_pixels(v, out):
        def step(b, carry):
            rows = pl.ds(pl.multiple_of(b * 128 + 8, 8), 128)
            x = jnp.concatenate([whole[v, q, rows, :] for q in range(4)], axis=1)
            high, low = halves(x)
            out[pl.ds(pl.multiple_of(b * 128, 128), 128), :] = dot(high, perm[1]) + dot(low, perm[1])
            return carry

        lax.fori_loop(0, 4, step, 0)

    unfold(0)
    mix()
    own.wait()
    for copy in frame_moves:
        copy.wait()
    take_frames()
    fold(0, -1.0, lambda rows, inside, old, out: (), 0)
    settle(1, exchange(1))

    unfold(1)
    mix()

    def measure_w(rows, inside, old, out):
        rr = old[0] * old[0] + old[1] * old[1] + (old[2] * old[2] + old[3] * old[3])
        rw = old[0] * out[0] + old[1] * out[1] + (old[2] * out[2] + old[3] * out[3])
        return jnp.where(inside, rr, 0.0), rw

    rr, rw = fold(1, 1.0, measure_w, 2)
    rw = rw + outer_columns(vec[1, 4, 0:PACK, :] * vec[2, 4, 0:PACK, :])
    moves = exchange(2)
    first_sums = gather_a(0, (rr, rw, zero8))
    write_pixels(1, r_out)
    settle(2, moves)
    first_sums = gather_b(0, first_sums)

    unfold(2)
    mix()
    rr, rw, _ = finish_sums(0, first_sums)
    alpha = rr / rw

    def measure_z(rows, inside, old, out):
        rate = jnp.broadcast_to(alpha[0:1], old[0].shape)
        ss, sw, sz = 0.0, 0.0, 0.0
        for q in range(4):
            s = whole[1, q, rows, :] - rate * old[q]
            ss, sw, sz = ss + s * s, sw + s * old[q], sz + s * out[q]
        return jnp.where(inside, ss, 0.0), jnp.where(inside, sw, 0.0), sz

    ss, sw, sz = fold(2, 1.0, measure_z, 3)
    s_edge = vec[1, 4, 0:PACK, :] - alpha[0:1, :] * vec[2, 4, 0:PACK, :]
    sz = sz + outer_columns(s_edge * vec[3, 4, 0:PACK, :])
    last_sums = gather_a(1, (ss, sw, sz))
    moves = exchange(3)
    write_pixels(2, w_out)
    last_sums = gather_b(1, last_sums)
    settle(3, moves)
    unfold(3, features=False)
    write_pixels(3, z_out)
    ss, sw, sz = finish_sums(1, last_sums)
    beta = ss / rr
    curve = (sw - alpha * sz) + 2.0 * beta * sw + beta * beta * rw
    step = ss / curve
    coef[0] = alpha + step * (1.0 + beta)
    coef[1] = step * alpha


def on_device(n_wide, n_narrow, frames, anchor, shift, guess):
    vmem = pl.BlockSpec(memory_space=pltpu.VMEM)
    image = jax.ShapeDtypeStruct((TS, TS), F32)
    dma = pltpu.SemaphoreType.DMA
    n_a, n_b = 2 * n_narrow, n_wide // 2
    r, w, z, coef = pl.pallas_call(
        functools.partial(kernel, n_wide, n_narrow),
        out_shape=(image, image, image, jax.ShapeDtypeStruct((2, 8, 128), F32)),
        in_specs=[pl.BlockSpec(memory_space=pl.ANY), vmem, vmem, vmem, vmem],
        out_specs=(vmem, vmem, vmem, vmem),
        scratch_shapes=[
            pltpu.VMEM((4, 5, ROWS, 128), F32),
            pltpu.VMEM((4, 4, ROWS, 128), F32),
            pltpu.VMEM((ROWS, 128), F32),
            pltpu.VMEM((8, ROWS, 128), F32),
            pltpu.VMEM((8, ROWS, 128), F32),
            pltpu.VMEM((8, ROWS, 128), F32),
            pltpu.VMEM((24 * FS, 128), F32),
            pltpu.VMEM((2, 512, 512), BF16),
            pltpu.VMEM((3, 128, 384), BF16),
            pltpu.VMEM((3, 128, 256), BF16),
            pltpu.VMEM((4, 2, PACK, 128), F32),
            pltpu.VMEM((4, 2, 5, 16, 128), F32),
            pltpu.VMEM((4, 4, 16, 128), F32),
            pltpu.VMEM((2, n_a, 3, 8, 128), F32),
            pltpu.VMEM((2, n_b, 3, 8, 128), F32),
            dma((4, 8)), dma((4, 8)), dma((2,)), dma((2,)), dma,
            dma((2, n_a)), dma((2, n_a)), dma((2, n_b)), dma((2, n_b)),
        ],
        compiler_params=pltpu.CompilerParams(
            collective_id=0, has_side_effects=True, vmem_limit_bytes=48 * 2**20),
    )(frames.reshape(8 * FS, FS), anchor, shift, guess, jnp.asarray(tables()))
    c1, c2 = coef[0, 0, 0], coef[1, 0, 0]
    return guess + c1 * r - c2 * w, r - c1 * w + c2 * z


def solution(mesh):
    placed = (P("narrow", "wide", None, None), P("narrow", None), P("narrow", None, None), P("narrow", "wide"))
    return jax.shard_map(
        functools.partial(on_device, mesh.shape["wide"], mesh.shape["narrow"]),
        mesh=mesh,
        in_specs=placed,
        out_specs=(P("narrow", "wide"), P("narrow", "wide")),
        check_vma=False,
    )
```

```python
import functools

import jax
import jax.numpy as jnp
import numpy as np
from jax import lax
from jax.experimental import pallas as pl
from jax.experimental.pallas import tpu as pltpu
from jax.sharding import PartitionSpec as P

NSHIFT = 16
DAMP = 0.05
TS = 512
FS = 128
ROWS = TS + 16
TILES = ROWS // 8
GROUP = 11
PACK = GROUP * 8
F32 = jnp.float32
BF16 = jnp.bfloat16
UNFOLD = 264
FOLD = 264
MIX = 32
HIGHEST = lax.Precision.HIGHEST


def tables():
    fraction = np.arange(NSHIFT, dtype=np.float64) / NSHIFT
    offsets = np.arange(8, dtype=np.float64)[None, :] - 3.0 - fraction[:, None]
    lanczos = np.sinc(offsets) * np.sinc(offsets / 4.0)
    lanczos = lanczos / lanczos.sum(axis=1, keepdims=True)
    spread = np.arange(11)[None, :] - np.arange(8)[:, None]
    taps = lanczos @ np.where((spread >= 0) & (spread < 4), 0.25, 0.0)
    out = np.zeros((3, 128, 128), np.float64)
    for feature in range(8):
        weight = feature + 4 if feature < 4 else feature - 4
        for r in range(16):
            for second in range(2):
                if 0 <= r - 4 * second <= 10:
                    out[second, feature * 16 + r, :NSHIFT] = taps[:, r - 4 * second]
            out[2, feature * 16 + r, :NSHIFT] = lanczos[:, weight] * 0.25
    return out.astype(np.float32)


def halves(x):
    high = x.astype(BF16)
    return high, (x - high.astype(F32)).astype(BF16)


def dot(a, b):
    return jnp.dot(a, b, preferred_element_type=F32)


def exact_dot(a, b):
    return jnp.dot(a, b, precision=HIGHEST, preferred_element_type=F32)


def exact_dot_nt(a, b):
    return lax.dot_general(a, b, (((1,), (1,)), ((), ())), precision=HIGHEST, preferred_element_type=F32)


def total_of(x):
    return jnp.broadcast_to(jnp.sum(x, axis=(0, 1), keepdims=True), (8, 128))


def kernel(
    n_wide, n_narrow,
    frames, anchor, shift, guess_hbm, table_hbm,
    r_out, w_out, z_out, coef,
    guess, table, vec, whole, wide_edges, feat, acc, more, frb, perm, lhs, lhsb,
    from_side, from_row, from_corner, sums_a, sums_b,
    send, recv, fsend, frecv, loc, asend, arecv, bsend, brecv,
):
    column = lax.axis_index("wide")
    row = lax.axis_index("narrow")
    left, right = lax.rem(column + n_wide - 1, n_wide), lax.rem(column + 1, n_wide)
    up, down = lax.rem(row + n_narrow - 1, n_narrow), lax.rem(row + 1, n_narrow)
    core, chip = lax.rem(column, 2), column // 2
    n_chip = n_wide // 2

    def at(w, n):
        return {"wide": w, "narrow": n}

    near = [at(right, row), at(left, row), at(column, down), at(column, up),
            at(right, down), at(left, down), at(right, up), at(left, up)]
    mates_a = [(row + (k // 2), core + (k % 2)) for k in range(1, 2 * n_narrow)]
    mates_a = [at(chip * 2 + lax.rem(c, 2), lax.rem(r, n_narrow)) for r, c in mates_a]
    mates_b = [at(lax.rem(chip + k, n_chip) * 2 + core, row) for k in range(1, n_chip)]

    barrier = pltpu.get_barrier_semaphore()
    everyone = near + mates_a + mates_b
    for device in everyone:
        pl.semaphore_signal(barrier, inc=1, device_id=device, device_id_type=pl.DeviceIdType.MESH)

    load_guess = pltpu.make_async_copy(guess_hbm, guess, loc.at[0])
    load_table = pltpu.make_async_copy(table_hbm, table, loc.at[1])
    own = pltpu.make_async_copy(frames, frb.at[8 * FS : 16 * FS], loc.at[2])
    load_guess.start()
    load_table.start()

    k_id = lax.broadcasted_iota(jnp.int32, (512, 128), 0)
    n_id = lax.broadcasted_iota(jnp.int32, (512, 128), 1)

    def permutation(which, target):
        for c in range(4):
            perm[which, :, c * 128 : c * 128 + 128] = jnp.where(n_id + 128 * c == target, 1.0, 0.0).astype(BF16)

    permutation(0, 128 * (k_id & 3) + (k_id >> 2))

    zero8 = jnp.zeros((8, 128), F32)

    def edge_masks(size):
        lane = lax.broadcasted_iota(jnp.int32, (size, 128), 1)
        return lane == 0, lane == 127

    def gather_edges(sides):
        packed = None
        for shift_by, part in sides:
            first, last = edge_masks(part.shape[0])
            term = pltpu.roll(jnp.where(first | last, part, 0.0), shift_by, axis=1)
            packed = term if packed is None else packed + term
        return packed

    def pack(v):
        packed = wide_edges[0:PACK, :]
        for g in range(1, 6):
            packed = packed + pltpu.roll(wide_edges[g * PACK : g * PACK + PACK, :], 16 * g, axis=1)
        vec[v, 4, 0:PACK, :] = packed
        vec[v, 4, 512:528, :] = packed[72:88]

    def unpack(v):
        for g in range(6):
            wide_edges[g * PACK : g * PACK + PACK, :] = pltpu.roll(vec[v, 4, 0:PACK, :], 127 - 16 * g, axis=1)

    for q in range(4):
        vec[0, q, 0:8, :] = zero8
        vec[0, q, ROWS - 8 : ROWS, :] = zero8
    wide_edges[0:8, :] = zero8
    wide_edges[ROWS - 8 : ROWS, :] = zero8

    def spread_guess(b):
        into = slice(b * 128 + 8, b * 128 + 136)
        high, low = halves(guess[b * 128 : b * 128 + 128, :])
        x = dot(high, perm[0]) + dot(low, perm[0])
        x = [x[:, q * 128 : q * 128 + 128] for q in range(4)]
        for q in range(4):
            vec[0, q, into, :] = x[q]
        wide_edges[into, :] = gather_edges([(4 * q + 1, x[q]) for q in range(4)])

    load_guess.wait()
    for b in range(4):
        spread_guess(b)
    pack(0)

    pl.semaphore_wait(barrier, len(everyone))

    def exchange(v):
        edges = vec.at[v, 4]
        parts = [
            (edges.at[0:PACK], from_side.at[v, 0]),
            (edges.at[0:PACK], from_side.at[v, 1]),
            (vec.at[v, :, 512:528], from_row.at[v, 0]),
            (vec.at[v, :, 0:16], from_row.at[v, 1]),
            (edges.at[72:88], from_corner.at[v, 0]),
            (edges.at[72:88], from_corner.at[v, 1]),
            (edges.at[0:16], from_corner.at[v, 2]),
            (edges.at[0:16], from_corner.at[v, 3]),
        ]
        copies = []
        for k, (source, target) in enumerate(parts):
            copy = pltpu.make_async_remote_copy(
                src_ref=source, dst_ref=target, send_sem=send.at[v, k], recv_sem=recv.at[v, k],
                device_id=near[k], device_id_type=pl.DeviceIdType.MESH)
            copy.start()
            copies.append(copy)
        return copies

    def settle(v, copies):
        for copy in copies:
            copy.wait()
        has_left, has_right = column > 0, column < n_wide - 1
        has_up, has_down = row > 0, row < n_narrow - 1
        lane16 = lax.broadcasted_iota(jnp.int32, (16, 128), 1)
        sub16 = lax.broadcasted_iota(jnp.int32, (16, 128), 0)
        in_top, in_low = lane16 < 16, (lane16 >= 80) & (lane16 < 96)

        def with_rows(middle, above, below):
            above = jnp.where(in_top & has_up, pltpu.roll(above, 48, axis=1), 0.0)
            below = jnp.where(in_low & has_down, pltpu.roll(below, 80, axis=1), 0.0)
            return jnp.concatenate([middle[0:16] + above, middle[16:72], middle[72:88] + below], axis=0)

        mine = with_rows(vec[v, 4, 0:PACK, :], from_row[v, 0, 4], from_row[v, 1, 4])
        lefts = with_rows(from_side[v, 0], from_corner[v, 0], from_corner[v, 2])
        rights = with_rows(from_side[v, 1], from_corner[v, 1], from_corner[v, 3])
        kind = lax.rem(lax.broadcasted_iota(jnp.int32, (PACK, 128), 1), 4)
        other = jnp.where(kind == 1, pltpu.roll(lefts, 127, axis=1), 0.0)
        other = jnp.where(kind == 3, pltpu.roll(lefts, 3, axis=1), other)
        other = jnp.where(((kind == 1) | (kind == 3)) & has_left, other, 0.0)
        facing = jnp.where(kind == 0, pltpu.roll(rights, 125, axis=1), 0.0)
        facing = jnp.where(kind == 2, pltpu.roll(rights, 1, axis=1), facing)
        facing = jnp.where(((kind == 0) | (kind == 2)) & has_right, facing, 0.0)
        both = mine + other + facing
        both = jnp.where((kind == 3) & (column == 0), 0.0, both)
        both = jnp.where((kind == 2) & (column == n_wide - 1), 0.0, both)
        top = jnp.where(in_top & (sub16 < 8) & (row == 0), 0.0, both[0:16])
        low = jnp.where(in_low & (sub16 >= 8) & (row == n_narrow - 1), 0.0, both[72:88])
        vec[v, 4, 0:PACK, :] = jnp.concatenate([top, both[16:72], low], axis=0)
        for q in range(4):
            x = vec[v, q, 0:16, :] + jnp.where(has_up, from_row[v, 0, q], 0.0)
            vec[v, q, 0:16, :] = jnp.where((sub16 < 8) & (row == 0), 0.0, x)
            x = vec[v, q, 512:528, :] + jnp.where(has_down, from_row[v, 1, q], 0.0)
            vec[v, q, 512:528, :] = jnp.where((sub16 >= 8) & (row == n_narrow - 1), 0.0, x)

    moves = exchange(0)
    frame_moves = []
    for k, device in enumerate((at(right, row), at(left, row))):
        copy = pltpu.make_async_remote_copy(
            src_ref=frames, dst_ref=frb.at[16 * FS * k : 16 * FS * k + 8 * FS], send_sem=fsend.at[k],
            recv_sem=frecv.at[k], device_id=device, device_id_type=pl.DeviceIdType.MESH)
        copy.start()
        frame_moves.append(copy)
    own.start()
    permutation(1, 4 * (k_id & 127) + (k_id >> 7))

    n_frames = 8 * n_wide
    f_id = lax.broadcasted_iota(jnp.int32, (n_frames, 128), 0)
    slot = lax.broadcasted_iota(jnp.int32, (n_frames, 128), 1)
    slot = slot - (slot // 32) * 32
    wanted = lax.rem(slot + 8 * left, n_frames)
    pick = jnp.where((f_id == wanted) & (slot < 24), 1.0, 0.0).astype(BF16)
    looks = jnp.where(jnp.broadcast_to(anchor[...], (16, n_frames)) == column, 1.0, 0.0)
    code_row = lax.broadcasted_iota(jnp.int32, (16, n_frames), 0)
    codes = jnp.where(code_row == 0, looks, jnp.where(
        code_row == 1, jnp.broadcast_to(shift[0, 0:1, :], (16, n_frames)).astype(F32),
        jnp.broadcast_to(shift[0, 1:2, :], (16, n_frames)).astype(F32)))
    codes = dot(codes.astype(BF16), pick)
    used = codes[0:1]
    load_table.wait()
    lane128 = lax.broadcasted_iota(jnp.int32, (128, 128), 1)
    sub128 = lax.broadcasted_iota(jnp.int32, (128, 128), 0)
    one_a = jnp.where(jnp.broadcast_to(codes[1:2], (128, 128)).astype(jnp.int32) == sub128, 1.0, 0.0)
    one_b = jnp.where(jnp.broadcast_to(codes[2:3], (128, 128)).astype(jnp.int32) == sub128, 1.0, 0.0)
    second = lax.rem(lane128 // 32, 2) == 1
    tall = exact_dot(table[2], one_b) * jnp.where(
        second, exact_dot(table[1], one_a), exact_dot(table[0], one_a)) * used
    for which, keep in enumerate((second, lane128 >= 0, jnp.logical_not(second))):
        kept = jnp.where(keep, tall, 0.0)
        high, low = halves(kept)
        lhsb[which, :, 0:128] = high
        lhsb[which, :, 128:256] = jnp.where(lane128 < 64, low.astype(F32), 0.0).astype(BF16)
        half = jnp.where(lane128 < 64, kept, 0.0)
        high, low = halves(exact_dot_nt(half, half))
        lhs[which, :, 0:128] = high
        lhs[which, :, 128:256] = high
        lhs[which, :, 256:384] = low

    settle(0, moves)

    def unfold(v, features=True):
        unpack(v)

        def step(i, carry):
            rows = pl.ds(pl.multiple_of(i * UNFOLD, 8), UNFOLD)
            first, last = edge_masks(UNFOLD)
            packed = wide_edges[rows, :]
            raw = [vec[v, q, rows, :] for q in range(4)]
            mid, nxt, prv = [], [], []
            for q in range(4):
                spun = packed if q == 0 else pltpu.roll(packed, 128 - 4 * q, axis=1)
                x = jnp.where(first | last, spun, raw[q])
                mid.append(x)
                if features:
                    side = pltpu.roll(packed, 126 - 4 * q, axis=1)
                    prv.append(jnp.where(first, side, pltpu.roll(x, 1, axis=1)))
                    if q < 3:
                        nxt.append(jnp.where(last, side, pltpu.roll(x, 127, axis=1)))
            for q in range(4):
                whole[v, q, rows, :] = mid[q]
            if not features:
                return carry
            m23, p23 = mid[2] + mid[3], prv[2] + prv[3]
            m123, p123 = mid[1] + m23, prv[1] + p23
            m01, n01 = mid[0] + mid[1], nxt[0] + nxt[1]
            out = [mid[0] + m123, m123 + nxt[0], m23 + n01, mid[3] + (n01 + nxt[2]),
                   prv[0] + p123, p123 + mid[0], p23 + m01, prv[3] + (m01 + mid[2])]
            for f in range(8):
                feat[f, rows, :] = out[f]
            return carry

        lax.fori_loop(0, ROWS // UNFOLD, step, 0)

    def join(parts):
        return parts[0] if len(parts) == 1 else jnp.concatenate(parts, axis=1)

    def blocks(starts):
        highs, lows = [], []
        for start in starts:
            pairs = [halves(feat[f, pl.ds(start, 16), :]) for f in range(8)]
            highs.append(jnp.concatenate([p[0] for p in pairs], axis=0))
            lows.append(jnp.concatenate([p[1] for p in pairs], axis=0))
        high, low = join(highs), join(lows)
        return jnp.concatenate([high, low, high], axis=0)

    def stack(outs, carry):
        done = []
        for out in outs:
            done.append([out[16 * f : 16 * f + 8] if carry is None else carry[f] + out[16 * f : 16 * f + 8]
                         for f in range(8)])
            carry = [out[16 * f + 8 : 16 * f + 16] for f in range(8)]
        return done, carry

    def sweep(results, save):
        def some(starts, kinds, carry):
            outs = []
            for k in range(0, len(starts), 2):
                outs.extend(results(starts[k : k + 2], kinds[k : k + 2]))
            done, carry = stack(outs, carry)
            for start, tiles in zip(starts, done):
                save(start, tiles)
            return tuple(carry)

        carry = some([8 * k for k in range(MIX)], [0] + [1] * (MIX - 1), None)

        def step(i, carry):
            start = pl.multiple_of(i * (8 * MIX), 8)
            return some([start + 8 * k for k in range(MIX)], [1] * MIX, carry)

        carry = lax.fori_loop(1, 64 // MIX, step, carry)
        carry = some([512], [2], carry)
        save(520, carry)

    def cut(out):
        return [out[:, 128 * k : 128 * k + 128] for k in range(out.shape[1] // 128)]

    def mix():
        def results(starts, kinds):
            if len(set(kinds)) > 1:
                return [dot(lhs[w], blocks([s])) for s, w in zip(starts, kinds)]
            return cut(dot(lhs[kinds[0]], blocks(starts)))

        def save(start, tiles):
            for f in range(8):
                acc[f, pl.ds(start, 8), :] = tiles[f]

        sweep(results, save)

    def take_frames():
        def pixels(start, kind):
            sample = start // 4
            rows = [0 if kind == 0 else sample - 1, FS - 1 if kind == 2 else sample]
            parts = []
            for i in rows:
                parts += [frb[pl.ds(i, 24, stride=FS), :], zero8]
            high, low = halves(jnp.concatenate(parts, axis=0))
            return jnp.concatenate([high, low], axis=0)

        def results(starts, kinds):
            if len(set(kinds)) > 1:
                return [results([s], [w])[0] for s, w in zip(starts, kinds)]
            both = join([pixels(s, w) for s, w in zip(starts, kinds)])
            return cut(dot(lhsb[kinds[0]], jnp.concatenate([both, both], axis=0)))

        def save(start, tiles):
            for f in range(8):
                more[f, pl.ds(start, 8), :] = tiles[f]

        sweep(results, save)

    def fold(v, sign, measure, counts):
        def step(i, sums):
            rows = pl.ds(pl.multiple_of(i * FOLD, 8), FOLD)
            first, last = edge_masks(FOLD)
            row_id = i * FOLD + lax.broadcasted_iota(jnp.int32, (FOLD, 128), 0)
            inside = (row_id >= 8) & (row_id < ROWS - 8)
            damp = jnp.where(inside, DAMP, 0.0)
            cur = [acc[q, rows, :] for q in range(4)]
            pre = [acc[4 + q, rows, :] for q in range(4)]
            if v == 0:
                cur = [c - more[q, rows, :] for q, c in enumerate(cur)]
                pre = [p - more[4 + q, rows, :] for q, p in enumerate(pre)]
            old = [whole[v, q, rows, :] for q in range(4)]
            rolled = [pltpu.roll(x, 127, axis=1) for x in pre]
            here = [c + jnp.where(last, 0.0, p) for c, p in zip(cur, rolled)]
            back = [p + jnp.where(last, 0.0, c) for c, p in zip(cur, rolled)]
            h01 = here[0] + here[1]
            h012 = h01 + here[2]
            k23 = back[2] + back[3]
            out = [here[0] + pltpu.roll(back[1] + k23, 1, axis=1), h01 + pltpu.roll(k23, 1, axis=1),
                   h012 + pltpu.roll(back[3], 1, axis=1), h012 + here[3]]
            h23 = here[2] + here[3]
            r01 = pre[0] + pre[1]
            r012 = r01 + pre[2]
            over = [jnp.where(first, pre[0], here[1] + h23), jnp.where(first, r01, h23),
                    jnp.where(first, r012, here[3]), jnp.where(first, r012 + pre[3], 0.0)]
            out = [o + damp * x for o, x in zip(out, old)]
            if sign < 0:
                out, over = [-o for o in out], [-o for o in over]
            packed = gather_edges([(4 * q + 1, out[q]) for q in range(4)] + [(4 * q + 3, over[q]) for q in range(4)])
            more_sums = measure(rows, inside, old, out)
            for q in range(4):
                vec[v + 1, q, rows, :] = out[q]
            wide_edges[rows, :] = packed
            return tuple(s + m for s, m in zip(sums, more_sums))

        sums = lax.fori_loop(0, ROWS // FOLD, step, (jnp.zeros((FOLD, 128), F32),) * counts)
        pack(v + 1)
        return [fewer_rows(s) for s in sums]

    def fewer_rows(x):
        total = x[0:8]
        for k in range(8, x.shape[0], 8):
            total = total + x[k : k + 8]
        return total

    def no_sums(rows, inside, old, out):
        return ()

    def outer_columns(product):
        kind = lax.broadcasted_iota(jnp.int32, (PACK, 128), 1) & 3
        return fewer_rows(jnp.where(kind >= 2, product, 0.0))

    def gather(values, slots, mates, sent, landed):
        for i, value in enumerate(values):
            slots[0, i] = value
        copies = []
        for k, device in enumerate(mates):
            copy = pltpu.make_async_remote_copy(
                src_ref=slots.at[0], dst_ref=slots.at[k + 1], send_sem=sent.at[k],
                recv_sem=landed.at[k], device_id=device, device_id_type=pl.DeviceIdType.MESH)
            copy.start()
            copies.append(copy)
        return copies

    def collect(copies, slots):
        for copy in copies:
            copy.wait()
        values = []
        for i in range(4):
            value = slots[0, i]
            for k in range(len(copies)):
                value = value + slots[k + 1, i]
            values.append(value)
        return values

    def gather_a(values):
        return gather(values, sums_a, mates_a, asend, arecv)

    def gather_b(copies):
        return gather(collect(copies, sums_a), sums_b, mates_b, bsend, brecv)

    def finish_sums(copies):
        return [total_of(value) for value in collect(copies, sums_b)]

    def write_pixels(v, out):
        for b in range(4):
            x = jnp.concatenate([whole[v, q, b * 128 + 8 : b * 128 + 136, :] for q in range(4)], axis=1)
            high, low = halves(x)
            out[b * 128 : b * 128 + 128, :] = dot(high, perm[1]) + dot(low, perm[1])

    unfold(0)
    mix()
    own.wait()
    for copy in frame_moves:
        copy.wait()
    take_frames()
    fold(0, -1.0, no_sums, 0)
    settle(1, exchange(1))

    unfold(1)
    mix()

    def measure_w(rows, inside, old, out):
        rr = old[0] * old[0] + old[1] * old[1] + (old[2] * old[2] + old[3] * old[3])
        rw = old[0] * out[0] + old[1] * out[1] + (old[2] * out[2] + old[3] * out[3])
        return jnp.where(inside, rr, 0.0), rw

    rr, rw = fold(1, 1.0, measure_w, 2)
    rw = rw + outer_columns(vec[1, 4, 0:PACK, :] * vec[2, 4, 0:PACK, :])
    moves = exchange(2)
    write_pixels(1, r_out)
    settle(2, moves)

    unfold(2)
    mix()
    ww = jnp.zeros((8, 128), F32)
    for q in range(4):
        own_rows = whole[2, q, 8 : ROWS - 8, :]
        ww = ww + fewer_rows(own_rows * own_rows)
    wz = DAMP * ww
    for f in range(8):
        wz = wz + fewer_rows(feat[f] * acc[f])
    sums = gather_a((rr, rw, ww, wz))
    fold(2, 1.0, no_sums, 0)
    moves = exchange(3)
    sums = gather_b(sums)
    write_pixels(2, w_out)
    settle(3, moves)
    unfold(3, features=False)
    write_pixels(3, z_out)
    rr, rw, ww, wz = finish_sums(sums)
    alpha = rr / rw
    ss = alpha * alpha * ww - rr
    sw = rw - alpha * ww
    beta = ss / rr
    curve = (sw - alpha * (ww - alpha * wz)) + 2.0 * beta * sw + beta * beta * rw
    step = ss / curve
    coef[0] = alpha + step * (1.0 + beta)
    coef[1] = step * alpha


def closing(guess_hbm, r, w, z, coef, solution_hbm, residual_hbm, guess, first, second, sems):
    load = pltpu.make_async_copy(guess_hbm, guess, sems.at[0])
    load.start()
    c1, c2 = coef[0, 0:1, 0:1], coef[1, 0:1, 0:1]
    stores = []
    for b in range(4):
        rows = slice(b * 128, b * 128 + 128)
        second[rows, :] = r[rows, :] - c1 * w[rows, :] + c2 * z[rows, :]
        stores.append(pltpu.make_async_copy(second.at[rows], residual_hbm.at[rows], sems.at[1 + b]))
        stores[-1].start()
    load.wait()
    for b in range(4):
        rows = slice(b * 128, b * 128 + 128)
        first[rows, :] = guess[rows, :] + c1 * r[rows, :] - c2 * w[rows, :]
        stores.append(pltpu.make_async_copy(first.at[rows], solution_hbm.at[rows], sems.at[5 + b]))
        stores[-1].start()
    for store in stores:
        store.wait()


def on_device(n_wide, n_narrow, frames, anchor, shift, guess):
    vmem, hbm = pl.BlockSpec(memory_space=pltpu.VMEM), pl.BlockSpec(memory_space=pltpu.HBM)
    image = jax.ShapeDtypeStruct((TS, TS), F32)
    dma = pltpu.SemaphoreType.DMA
    n_a, n_b = 2 * n_narrow, n_wide // 2
    r, w, z, coef = pl.pallas_call(
        functools.partial(kernel, n_wide, n_narrow),
        out_shape=(image, image, image, jax.ShapeDtypeStruct((2, 8, 128), F32)),
        in_specs=[hbm, vmem, vmem, hbm, hbm],
        out_specs=(vmem, vmem, vmem, vmem),
        scratch_shapes=[
            pltpu.VMEM((TS, TS), F32),
            pltpu.VMEM((3, 128, 128), F32),
            pltpu.VMEM((4, 5, ROWS, 128), F32),
            pltpu.VMEM((4, 4, ROWS, 128), F32),
            pltpu.VMEM((ROWS, 128), F32),
            pltpu.VMEM((8, ROWS, 128), F32),
            pltpu.VMEM((8, ROWS, 128), F32),
            pltpu.VMEM((8, ROWS, 128), F32),
            pltpu.VMEM((24 * FS, 128), F32),
            pltpu.VMEM((2, 512, 512), BF16),
            pltpu.VMEM((3, 128, 384), BF16),
            pltpu.VMEM((3, 128, 256), BF16),
            pltpu.VMEM((4, 2, PACK, 128), F32),
            pltpu.VMEM((4, 2, 5, 16, 128), F32),
            pltpu.VMEM((4, 4, 16, 128), F32),
            pltpu.VMEM((n_a, 4, 8, 128), F32),
            pltpu.VMEM((n_b, 4, 8, 128), F32),
            dma((4, 8)), dma((4, 8)), dma((2,)), dma((2,)), dma((3,)),
            dma((n_a,)), dma((n_a,)), dma((n_b,)), dma((n_b,)),
        ],
        compiler_params=pltpu.CompilerParams(
            collective_id=0, has_side_effects=True, vmem_limit_bytes=48 * 2**20),
    )(frames.reshape(8 * FS, FS), anchor, shift.transpose(0, 2, 1), guess, jnp.asarray(tables()))
    return pl.pallas_call(
        closing,
        out_shape=(image, image),
        in_specs=[hbm, vmem, vmem, vmem, vmem],
        out_specs=(hbm, hbm),
        scratch_shapes=[pltpu.VMEM((TS, TS), F32)] * 3 + [dma((9,))],
    )(guess, r, w, z, coef)


def solution(mesh):
    placed = (P("narrow", "wide", None, None), P("narrow", None), P("narrow", None, None), P("narrow", "wide"))
    return jax.shard_map(
        functools.partial(on_device, mesh.shape["wide"], mesh.shape["narrow"]),
        mesh=mesh,
        in_specs=placed,
        out_specs=(P("narrow", "wide"), P("narrow", "wide")),
        check_vma=False,
    )
```

```python
import functools

import jax
import jax.numpy as jnp
import numpy as np
from jax import lax
from jax.experimental import pallas as pl
from jax.experimental.pallas import tpu as pltpu
from jax.sharding import PartitionSpec as P

NSHIFT = 16
DAMP = 0.05
TS = 512
FS = 128
ROWS = TS + 16
TILES = ROWS // 8
GROUP = 11
PACK = GROUP * 8
F32 = jnp.float32
BF16 = jnp.bfloat16
UNFOLD = 264
FOLD = 264
MIX = 32
CLOSE = 4
VMEM_BYTES = 62 * 2**20
HIGHEST = lax.Precision.HIGHEST


def tables():
    fraction = np.arange(NSHIFT, dtype=np.float64) / NSHIFT
    offsets = np.arange(8, dtype=np.float64)[None, :] - 3.0 - fraction[:, None]
    lanczos = np.sinc(offsets) * np.sinc(offsets / 4.0)
    lanczos = lanczos / lanczos.sum(axis=1, keepdims=True)
    spread = np.arange(11)[None, :] - np.arange(8)[:, None]
    taps = lanczos @ np.where((spread >= 0) & (spread < 4), 0.25, 0.0)
    out = np.zeros((3, 128, 128), np.float64)
    for feature in range(8):
        weight = feature + 4 if feature < 4 else feature - 4
        for r in range(16):
            for second in range(2):
                if 0 <= r - 4 * second <= 10:
                    out[second, feature * 16 + r, :NSHIFT] = taps[:, r - 4 * second]
            out[2, feature * 16 + r, :NSHIFT] = lanczos[:, weight] * 0.25
    return out.astype(np.float32)


def halves(x):
    high = x.astype(BF16)
    return high, (x - high.astype(F32)).astype(BF16)


def dot(a, b):
    return jnp.dot(a, b, preferred_element_type=F32)


def exact_dot(a, b):
    return jnp.dot(a, b, precision=HIGHEST, preferred_element_type=F32)


def exact_dot_nt(a, b):
    return lax.dot_general(a, b, (((1,), (1,)), ((), ())), precision=HIGHEST, preferred_element_type=F32)


def total_of(x):
    return jnp.broadcast_to(jnp.sum(x, axis=(0, 1), keepdims=True), (8, 128))


def kernel(
    n_wide, n_narrow,
    frames, anchor, shift, guess_hbm, table_hbm,
    r_hbm, w_hbm, z_hbm, coef,
    guess, pixels, table, vec, whole, wide_edges, feat, acc, more, frb, perm, lhs, lhsb,
    from_side, from_row, from_corner, sums_a, sums_b,
    send, recv, fsend, frecv, loc, stores, asend, arecv, bsend, brecv,
):
    column = lax.axis_index("wide")
    row = lax.axis_index("narrow")
    left, right = lax.rem(column + n_wide - 1, n_wide), lax.rem(column + 1, n_wide)
    up, down = lax.rem(row + n_narrow - 1, n_narrow), lax.rem(row + 1, n_narrow)
    core, chip = lax.rem(column, 2), column // 2
    n_chip = n_wide // 2

    def at(w, n):
        return {"wide": w, "narrow": n}

    near = [at(right, row), at(left, row), at(column, down), at(column, up),
            at(right, down), at(left, down), at(right, up), at(left, up)]
    mates_a = [(row + (k // 2), core + (k % 2)) for k in range(1, 2 * n_narrow)]
    mates_a = [at(chip * 2 + lax.rem(c, 2), lax.rem(r, n_narrow)) for r, c in mates_a]
    mates_b = [at(lax.rem(chip + k, n_chip) * 2 + core, row) for k in range(1, n_chip)]

    barrier = pltpu.get_barrier_semaphore()
    everyone = near + mates_a + mates_b
    for device in everyone:
        pl.semaphore_signal(barrier, inc=1, device_id=device, device_id_type=pl.DeviceIdType.MESH)

    load_guess = pltpu.make_async_copy(guess_hbm, guess, loc.at[0])
    load_table = pltpu.make_async_copy(table_hbm, table, loc.at[1])
    own = pltpu.make_async_copy(frames, frb.at[8 * FS : 16 * FS], loc.at[2])
    load_guess.start()
    load_table.start()

    k_id = lax.broadcasted_iota(jnp.int32, (512, 128), 0)
    n_id = lax.broadcasted_iota(jnp.int32, (512, 128), 1)

    def permutation(which, target):
        for c in range(4):
            perm[which, :, c * 128 : c * 128 + 128] = jnp.where(n_id + 128 * c == target, 1.0, 0.0).astype(BF16)

    permutation(0, 128 * (k_id & 3) + (k_id >> 2))

    zero8 = jnp.zeros((8, 128), F32)

    def edge_masks(size):
        lane = lax.broadcasted_iota(jnp.int32, (size, 128), 1)
        return lane == 0, lane == 127

    def gather_edges(sides):
        packed = None
        for shift_by, part in sides:
            first, last = edge_masks(part.shape[0])
            term = pltpu.roll(jnp.where(first | last, part, 0.0), shift_by, axis=1)
            packed = term if packed is None else packed + term
        return packed

    def pack(v):
        packed = wide_edges[0:PACK, :]
        for g in range(1, 6):
            packed = packed + pltpu.roll(wide_edges[g * PACK : g * PACK + PACK, :], 16 * g, axis=1)
        vec[v, 4, 0:PACK, :] = packed
        vec[v, 4, 512:528, :] = packed[72:88]

    def unpack(v):
        for g in range(6):
            wide_edges[g * PACK : g * PACK + PACK, :] = pltpu.roll(vec[v, 4, 0:PACK, :], 127 - 16 * g, axis=1)

    for q in range(4):
        vec[0, q, 0:8, :] = zero8
        vec[0, q, ROWS - 8 : ROWS, :] = zero8
    wide_edges[0:8, :] = zero8
    wide_edges[ROWS - 8 : ROWS, :] = zero8

    def spread_guess(b):
        into = slice(b * 128 + 8, b * 128 + 136)
        high, low = halves(guess[b * 128 : b * 128 + 128, :])
        x = dot(high, perm[0]) + dot(low, perm[0])
        x = [x[:, q * 128 : q * 128 + 128] for q in range(4)]
        for q in range(4):
            vec[0, q, into, :] = x[q]
        wide_edges[into, :] = gather_edges([(4 * q + 1, x[q]) for q in range(4)])

    load_guess.wait()
    for b in range(4):
        spread_guess(b)
    pack(0)

    pl.semaphore_wait(barrier, len(everyone))

    def exchange(v):
        edges = vec.at[v, 4]
        parts = [
            (edges.at[0:PACK], from_side.at[v, 0]),
            (edges.at[0:PACK], from_side.at[v, 1]),
            (vec.at[v, :, 512:528], from_row.at[v, 0]),
            (vec.at[v, :, 0:16], from_row.at[v, 1]),
            (edges.at[72:88], from_corner.at[v, 0]),
            (edges.at[72:88], from_corner.at[v, 1]),
            (edges.at[0:16], from_corner.at[v, 2]),
            (edges.at[0:16], from_corner.at[v, 3]),
        ]
        copies = []
        for k, (source, target) in enumerate(parts):
            copy = pltpu.make_async_remote_copy(
                src_ref=source, dst_ref=target, send_sem=send.at[v, k], recv_sem=recv.at[v, k],
                device_id=near[k], device_id_type=pl.DeviceIdType.MESH)
            copy.start()
            copies.append(copy)
        return copies

    def settle(v, copies):
        for copy in copies:
            copy.wait()
        has_left, has_right = column > 0, column < n_wide - 1
        has_up, has_down = row > 0, row < n_narrow - 1
        lane16 = lax.broadcasted_iota(jnp.int32, (16, 128), 1)
        sub16 = lax.broadcasted_iota(jnp.int32, (16, 128), 0)
        in_top, in_low = lane16 < 16, (lane16 >= 80) & (lane16 < 96)

        def with_rows(middle, above, below):
            above = jnp.where(in_top & has_up, pltpu.roll(above, 48, axis=1), 0.0)
            below = jnp.where(in_low & has_down, pltpu.roll(below, 80, axis=1), 0.0)
            return jnp.concatenate([middle[0:16] + above, middle[16:72], middle[72:88] + below], axis=0)

        mine = with_rows(vec[v, 4, 0:PACK, :], from_row[v, 0, 4], from_row[v, 1, 4])
        lefts = with_rows(from_side[v, 0], from_corner[v, 0], from_corner[v, 2])
        rights = with_rows(from_side[v, 1], from_corner[v, 1], from_corner[v, 3])
        kind = lax.rem(lax.broadcasted_iota(jnp.int32, (PACK, 128), 1), 4)
        other = jnp.where(kind == 1, pltpu.roll(lefts, 127, axis=1), 0.0)
        other = jnp.where(kind == 3, pltpu.roll(lefts, 3, axis=1), other)
        other = jnp.where(((kind == 1) | (kind == 3)) & has_left, other, 0.0)
        facing = jnp.where(kind == 0, pltpu.roll(rights, 125, axis=1), 0.0)
        facing = jnp.where(kind == 2, pltpu.roll(rights, 1, axis=1), facing)
        facing = jnp.where(((kind == 0) | (kind == 2)) & has_right, facing, 0.0)
        both = mine + other + facing
        both = jnp.where((kind == 3) & (column == 0), 0.0, both)
        both = jnp.where((kind == 2) & (column == n_wide - 1), 0.0, both)
        top = jnp.where(in_top & (sub16 < 8) & (row == 0), 0.0, both[0:16])
        low = jnp.where(in_low & (sub16 >= 8) & (row == n_narrow - 1), 0.0, both[72:88])
        vec[v, 4, 0:PACK, :] = jnp.concatenate([top, both[16:72], low], axis=0)
        for q in range(4):
            x = vec[v, q, 0:16, :] + jnp.where(has_up, from_row[v, 0, q], 0.0)
            vec[v, q, 0:16, :] = jnp.where((sub16 < 8) & (row == 0), 0.0, x)
            x = vec[v, q, 512:528, :] + jnp.where(has_down, from_row[v, 1, q], 0.0)
            vec[v, q, 512:528, :] = jnp.where((sub16 >= 8) & (row == n_narrow - 1), 0.0, x)

    moves = exchange(0)
    frame_moves = []
    for k, device in enumerate((at(right, row), at(left, row))):
        copy = pltpu.make_async_remote_copy(
            src_ref=frames, dst_ref=frb.at[16 * FS * k : 16 * FS * k + 8 * FS], send_sem=fsend.at[k],
            recv_sem=frecv.at[k], device_id=device, device_id_type=pl.DeviceIdType.MESH)
        copy.start()
        frame_moves.append(copy)
    own.start()
    permutation(1, 4 * (k_id & 127) + (k_id >> 7))

    n_frames = 8 * n_wide
    f_id = lax.broadcasted_iota(jnp.int32, (n_frames, 128), 0)
    slot = lax.broadcasted_iota(jnp.int32, (n_frames, 128), 1)
    slot = slot - (slot // 32) * 32
    wanted = lax.rem(slot + 8 * left, n_frames)
    pick = jnp.where((f_id == wanted) & (slot < 24), 1.0, 0.0).astype(BF16)
    looks = jnp.where(jnp.broadcast_to(anchor[...], (16, n_frames)) == column, 1.0, 0.0)
    code_row = lax.broadcasted_iota(jnp.int32, (16, n_frames), 0)
    codes = jnp.where(code_row == 0, looks, jnp.where(
        code_row == 1, jnp.broadcast_to(shift[0, 0:1, :], (16, n_frames)).astype(F32),
        jnp.broadcast_to(shift[0, 1:2, :], (16, n_frames)).astype(F32)))
    codes = dot(codes.astype(BF16), pick)
    used = codes[0:1]
    load_table.wait()
    lane128 = lax.broadcasted_iota(jnp.int32, (128, 128), 1)
    sub128 = lax.broadcasted_iota(jnp.int32, (128, 128), 0)
    one_a = jnp.where(jnp.broadcast_to(codes[1:2], (128, 128)).astype(jnp.int32) == sub128, 1.0, 0.0)
    one_b = jnp.where(jnp.broadcast_to(codes[2:3], (128, 128)).astype(jnp.int32) == sub128, 1.0, 0.0)
    second = lax.rem(lane128 // 32, 2) == 1
    tall = exact_dot(table[2], one_b) * jnp.where(
        second, exact_dot(table[1], one_a), exact_dot(table[0], one_a)) * used
    for which, keep in enumerate((second, lane128 >= 0, jnp.logical_not(second))):
        kept = jnp.where(keep, tall, 0.0)
        high, low = halves(kept)
        lhsb[which, :, 0:128] = high
        lhsb[which, :, 128:256] = jnp.where(lane128 < 64, low.astype(F32), 0.0).astype(BF16)
        half = jnp.where(lane128 < 64, kept, 0.0)
        high, low = halves(exact_dot_nt(half, half))
        lhs[which, :, 0:128] = high
        lhs[which, :, 128:256] = high
        lhs[which, :, 256:384] = low

    settle(0, moves)

    def unfold(v, features=True):
        unpack(v)

        def step(i, carry):
            rows = pl.ds(pl.multiple_of(i * UNFOLD, 8), UNFOLD)
            first, last = edge_masks(UNFOLD)
            packed = wide_edges[rows, :]
            raw = [vec[v, q, rows, :] for q in range(4)]
            mid, nxt, prv = [], [], []
            for q in range(4):
                spun = packed if q == 0 else pltpu.roll(packed, 128 - 4 * q, axis=1)
                x = jnp.where(first | last, spun, raw[q])
                mid.append(x)
                if features:
                    side = pltpu.roll(packed, 126 - 4 * q, axis=1)
                    prv.append(jnp.where(first, side, pltpu.roll(x, 1, axis=1)))
                    if q < 3:
                        nxt.append(jnp.where(last, side, pltpu.roll(x, 127, axis=1)))
            for q in range(4):
                whole[v, q, rows, :] = mid[q]
            if not features:
                return carry
            m23, p23 = mid[2] + mid[3], prv[2] + prv[3]
            m123, p123 = mid[1] + m23, prv[1] + p23
            m01, n01 = mid[0] + mid[1], nxt[0] + nxt[1]
            out = [mid[0] + m123, m123 + nxt[0], m23 + n01, mid[3] + (n01 + nxt[2]),
                   prv[0] + p123, p123 + mid[0], p23 + m01, prv[3] + (m01 + mid[2])]
            for f in range(8):
                feat[f, rows, :] = out[f]
            return carry

        lax.fori_loop(0, ROWS // UNFOLD, step, 0)

    def join(parts):
        return parts[0] if len(parts) == 1 else jnp.concatenate(parts, axis=1)

    def blocks(starts):
        highs, lows = [], []
        for start in starts:
            pairs = [halves(feat[f, pl.ds(start, 16), :]) for f in range(8)]
            highs.append(jnp.concatenate([p[0] for p in pairs], axis=0))
            lows.append(jnp.concatenate([p[1] for p in pairs], axis=0))
        high, low = join(highs), join(lows)
        return jnp.concatenate([high, low, high], axis=0)

    def stack(outs, carry):
        done = []
        for out in outs:
            done.append([out[16 * f : 16 * f + 8] if carry is None else carry[f] + out[16 * f : 16 * f + 8]
                         for f in range(8)])
            carry = [out[16 * f + 8 : 16 * f + 16] for f in range(8)]
        return done, carry

    def sweep(results, save):
        def some(starts, kinds, carry):
            outs = []
            for k in range(0, len(starts), 2):
                outs.extend(results(starts[k : k + 2], kinds[k : k + 2]))
            done, carry = stack(outs, carry)
            for start, tiles in zip(starts, done):
                save(start, tiles)
            return tuple(carry)

        carry = some([8 * k for k in range(MIX)], [0] + [1] * (MIX - 1), None)

        def step(i, carry):
            start = pl.multiple_of(i * (8 * MIX), 8)
            return some([start + 8 * k for k in range(MIX)], [1] * MIX, carry)

        carry = lax.fori_loop(1, 64 // MIX, step, carry)
        carry = some([512], [2], carry)
        save(520, carry)

    def cut(out):
        return [out[:, 128 * k : 128 * k + 128] for k in range(out.shape[1] // 128)]

    def mix():
        def results(starts, kinds):
            if len(set(kinds)) > 1:
                return [dot(lhs[w], blocks([s])) for s, w in zip(starts, kinds)]
            return cut(dot(lhs[kinds[0]], blocks(starts)))

        def save(start, tiles):
            for f in range(8):
                acc[f, pl.ds(start, 8), :] = tiles[f]

        sweep(results, save)

    def take_frames():
        def pixels(start, kind):
            sample = start // 4
            rows = [0 if kind == 0 else sample - 1, FS - 1 if kind == 2 else sample]
            parts = []
            for i in rows:
                parts += [frb[pl.ds(i, 24, stride=FS), :], zero8]
            high, low = halves(jnp.concatenate(parts, axis=0))
            return jnp.concatenate([high, low], axis=0)

        def results(starts, kinds):
            if len(set(kinds)) > 1:
                return [results([s], [w])[0] for s, w in zip(starts, kinds)]
            both = join([pixels(s, w) for s, w in zip(starts, kinds)])
            return cut(dot(lhsb[kinds[0]], jnp.concatenate([both, both], axis=0)))

        def save(start, tiles):
            for f in range(8):
                more[f, pl.ds(start, 8), :] = tiles[f]

        sweep(results, save)

    def fold(v, sign, measure, counts):
        def step(i, sums):
            rows = pl.ds(pl.multiple_of(i * FOLD, 8), FOLD)
            first, last = edge_masks(FOLD)
            row_id = i * FOLD + lax.broadcasted_iota(jnp.int32, (FOLD, 128), 0)
            inside = (row_id >= 8) & (row_id < ROWS - 8)
            damp = jnp.where(inside, DAMP, 0.0)
            cur = [acc[q, rows, :] for q in range(4)]
            pre = [acc[4 + q, rows, :] for q in range(4)]
            if v == 0:
                cur = [c - more[q, rows, :] for q, c in enumerate(cur)]
                pre = [p - more[4 + q, rows, :] for q, p in enumerate(pre)]
            old = [whole[v, q, rows, :] for q in range(4)]
            rolled = [pltpu.roll(x, 127, axis=1) for x in pre]
            here = [c + jnp.where(last, 0.0, p) for c, p in zip(cur, rolled)]
            back = [p + jnp.where(last, 0.0, c) for c, p in zip(cur, rolled)]
            h01 = here[0] + here[1]
            h012 = h01 + here[2]
            k23 = back[2] + back[3]
            out = [here[0] + pltpu.roll(back[1] + k23, 1, axis=1), h01 + pltpu.roll(k23, 1, axis=1),
                   h012 + pltpu.roll(back[3], 1, axis=1), h012 + here[3]]
            h23 = here[2] + here[3]
            r01 = pre[0] + pre[1]
            r012 = r01 + pre[2]
            over = [jnp.where(first, pre[0], here[1] + h23), jnp.where(first, r01, h23),
                    jnp.where(first, r012, here[3]), jnp.where(first, r012 + pre[3], 0.0)]
            out = [o + damp * x for o, x in zip(out, old)]
            if sign < 0:
                out, over = [-o for o in out], [-o for o in over]
            packed = gather_edges([(4 * q + 1, out[q]) for q in range(4)] + [(4 * q + 3, over[q]) for q in range(4)])
            more_sums = measure(rows, inside, old, out)
            for q in range(4):
                vec[v + 1, q, rows, :] = out[q]
            wide_edges[rows, :] = packed
            return tuple(s + m for s, m in zip(sums, more_sums))

        sums = lax.fori_loop(0, ROWS // FOLD, step, (jnp.zeros((FOLD, 128), F32),) * counts)
        pack(v + 1)
        return [fewer_rows(s) for s in sums]

    def fewer_rows(x):
        total = x[0:8]
        for k in range(8, x.shape[0], 8):
            total = total + x[k : k + 8]
        return total

    def no_sums(rows, inside, old, out):
        return ()

    def outer_columns(product):
        kind = lax.broadcasted_iota(jnp.int32, (PACK, 128), 1) & 3
        return fewer_rows(jnp.where(kind >= 2, product, 0.0))

    def gather(values, slots, mates, sent, landed):
        for i, value in enumerate(values):
            slots[0, i] = value
        copies = []
        for k, device in enumerate(mates):
            copy = pltpu.make_async_remote_copy(
                src_ref=slots.at[0], dst_ref=slots.at[k + 1], send_sem=sent.at[k],
                recv_sem=landed.at[k], device_id=device, device_id_type=pl.DeviceIdType.MESH)
            copy.start()
            copies.append(copy)
        return copies

    def collect(copies, slots):
        for copy in copies:
            copy.wait()
        values = []
        for i in range(4):
            value = slots[0, i]
            for k in range(len(copies)):
                value = value + slots[k + 1, i]
            values.append(value)
        return values

    def gather_a(values):
        return gather(values, sums_a, mates_a, asend, arecv)

    def gather_b(copies):
        return gather(collect(copies, sums_a), sums_b, mates_b, bsend, brecv)

    def finish_sums(copies):
        return [total_of(value) for value in collect(copies, sums_b)]

    def write_pixels(v, out):
        for b in range(4):
            rows = slice(b * 128, b * 128 + 128)
            x = jnp.concatenate([whole[v, q, b * 128 + 8 : b * 128 + 136, :] for q in range(4)], axis=1)
            high, low = halves(x)
            pixels[v - 1, rows, :] = dot(high, perm[1]) + dot(low, perm[1])
        store = pltpu.make_async_copy(pixels.at[v - 1], out, stores.at[v - 1])
        store.start()
        return store

    unfold(0)
    mix()
    own.wait()
    for copy in frame_moves:
        copy.wait()
    take_frames()
    fold(0, -1.0, no_sums, 0)
    settle(1, exchange(1))

    unfold(1)
    mix()

    def measure_w(rows, inside, old, out):
        rr = old[0] * old[0] + old[1] * old[1] + (old[2] * old[2] + old[3] * old[3])
        rw = old[0] * out[0] + old[1] * out[1] + (old[2] * out[2] + old[3] * out[3])
        return jnp.where(inside, rr, 0.0), rw

    rr, rw = fold(1, 1.0, measure_w, 2)
    rw = rw + outer_columns(vec[1, 4, 0:PACK, :] * vec[2, 4, 0:PACK, :])
    moves = exchange(2)
    written = [write_pixels(1, r_hbm)]
    settle(2, moves)

    unfold(2)
    mix()
    ww = jnp.zeros((8, 128), F32)
    for q in range(4):
        own_rows = whole[2, q, 8 : ROWS - 8, :]
        ww = ww + fewer_rows(own_rows * own_rows)
    wz = DAMP * ww
    for f in range(8):
        wz = wz + fewer_rows(feat[f] * acc[f])
    sums = gather_a((rr, rw, ww, wz))
    fold(2, 1.0, no_sums, 0)
    moves = exchange(3)
    sums = gather_b(sums)
    written.append(write_pixels(2, w_hbm))
    settle(3, moves)
    unfold(3, features=False)
    written.append(write_pixels(3, z_hbm))
    rr, rw, ww, wz = finish_sums(sums)
    alpha = rr / rw
    ss = alpha * alpha * ww - rr
    sw = rw - alpha * ww
    beta = ss / rr
    curve = (sw - alpha * (ww - alpha * wz)) + 2.0 * beta * sw + beta * beta * rw
    step = ss / curve
    coef[0] = alpha + step * (1.0 + beta)
    coef[1] = step * alpha
    for store in written:
        store.wait()


def closing(guess_hbm, r_hbm, w_hbm, z_hbm, coef, solution_hbm, residual_hbm, held, made, loads, stores):
    sources = (r_hbm, w_hbm, z_hbm, guess_hbm)
    copies = {}
    for b in range(CLOSE):
        rows = slice(b * (TS // CLOSE), (b + 1) * (TS // CLOSE))
        for k, source in enumerate(sources):
            copies[b, k] = pltpu.make_async_copy(source.at[rows], held.at[k, rows], loads.at[b, k])
            copies[b, k].start()
    c1, c2 = coef[0, 0:1, 0:1], coef[1, 0:1, 0:1]
    writes = []
    for b in range(CLOSE):
        rows = slice(b * (TS // CLOSE), (b + 1) * (TS // CLOSE))
        for k in range(4):
            copies[b, k].wait()
        r, w = held[0, rows, :], held[1, rows, :]
        made[1, rows, :] = r - c1 * w + c2 * held[2, rows, :]
        made[0, rows, :] = held[3, rows, :] + c1 * r - c2 * w
        for k, target in enumerate((solution_hbm, residual_hbm)):
            writes.append(pltpu.make_async_copy(made.at[k, rows], target.at[rows], stores.at[b, k]))
            writes[-1].start()
    for write in writes:
        write.wait()


def on_device(n_wide, n_narrow, frames, anchor, shift, guess):
    vmem, hbm = pl.BlockSpec(memory_space=pltpu.VMEM), pl.BlockSpec(memory_space=pltpu.HBM)
    image = jax.ShapeDtypeStruct((TS, TS), F32)
    dma = pltpu.SemaphoreType.DMA
    n_a, n_b = 2 * n_narrow, n_wide // 2
    r, w, z, coef = pl.pallas_call(
        functools.partial(kernel, n_wide, n_narrow),
        out_shape=(image, image, image, jax.ShapeDtypeStruct((2, 8, 128), F32)),
        in_specs=[hbm, vmem, vmem, hbm, hbm],
        out_specs=(hbm, hbm, hbm, vmem),
        scratch_shapes=[
            pltpu.VMEM((TS, TS), F32),
            pltpu.VMEM((3, TS, TS), F32),
            pltpu.VMEM((3, 128, 128), F32),
            pltpu.VMEM((4, 5, ROWS, 128), F32),
            pltpu.VMEM((4, 4, ROWS, 128), F32),
            pltpu.VMEM((ROWS, 128), F32),
            pltpu.VMEM((8, ROWS, 128), F32),
            pltpu.VMEM((8, ROWS, 128), F32),
            pltpu.VMEM((8, ROWS, 128), F32),
            pltpu.VMEM((24 * FS, 128), F32),
            pltpu.VMEM((2, 512, 512), BF16),
            pltpu.VMEM((3, 128, 384), BF16),
            pltpu.VMEM((3, 128, 256), BF16),
            pltpu.VMEM((4, 2, PACK, 128), F32),
            pltpu.VMEM((4, 2, 5, 16, 128), F32),
            pltpu.VMEM((4, 4, 16, 128), F32),
            pltpu.VMEM((n_a, 4, 8, 128), F32),
            pltpu.VMEM((n_b, 4, 8, 128), F32),
            dma((4, 8)), dma((4, 8)), dma((2,)), dma((2,)), dma((3,)), dma((3,)),
            dma((n_a,)), dma((n_a,)), dma((n_b,)), dma((n_b,)),
        ],
        compiler_params=pltpu.CompilerParams(
            collective_id=0, has_side_effects=True, vmem_limit_bytes=VMEM_BYTES),
    )(frames.reshape(8 * FS, FS), anchor, shift.transpose(0, 2, 1), guess, jnp.asarray(tables()))
    return pl.pallas_call(
        closing,
        out_shape=(image, image),
        in_specs=[hbm, hbm, hbm, hbm, vmem],
        out_specs=(hbm, hbm),
        scratch_shapes=[pltpu.VMEM((4, TS, TS), F32), pltpu.VMEM((2, TS, TS), F32), dma((CLOSE, 4)), dma((CLOSE, 2))],
        compiler_params=pltpu.CompilerParams(vmem_limit_bytes=VMEM_BYTES),
    )(guess, r, w, z, coef)


def solution(mesh):
    placed = (P("narrow", "wide", None, None), P("narrow", None), P("narrow", None, None), P("narrow", "wide"))
    return jax.shard_map(
        functools.partial(on_device, mesh.shape["wide"], mesh.shape["narrow"]),
        mesh=mesh,
        in_specs=placed,
        out_specs=(P("narrow", "wide"), P("narrow", "wide")),
        check_vma=False,
    )
```

```python
import functools

import jax
import jax.numpy as jnp
import numpy as np
from jax import lax
from jax.experimental import pallas as pl
from jax.experimental.pallas import tpu as pltpu
from jax.sharding import PartitionSpec as P

NSHIFT = 16
DAMP = 0.05
TS = 512
FS = 128
ROWS = TS + 16
TILES = ROWS // 8
GROUP = 11
PACK = GROUP * 8
F32 = jnp.float32
BF16 = jnp.bfloat16
UNFOLD = 528
FOLD = 528
MIX = 64
CLOSE = 4
VMEM_BYTES = 62 * 2**20
HIGHEST = lax.Precision.HIGHEST


def tables():
    fraction = np.arange(NSHIFT, dtype=np.float64) / NSHIFT
    offsets = np.arange(8, dtype=np.float64)[None, :] - 3.0 - fraction[:, None]
    lanczos = np.sinc(offsets) * np.sinc(offsets / 4.0)
    lanczos = lanczos / lanczos.sum(axis=1, keepdims=True)
    spread = np.arange(11)[None, :] - np.arange(8)[:, None]
    taps = lanczos @ np.where((spread >= 0) & (spread < 4), 0.25, 0.0)
    out = np.zeros((3, 128, 128), np.float64)
    for feature in range(8):
        weight = feature + 4 if feature < 4 else feature - 4
        for r in range(16):
            for second in range(2):
                if 0 <= r - 4 * second <= 10:
                    out[second, feature * 16 + r, :NSHIFT] = taps[:, r - 4 * second]
            out[2, feature * 16 + r, :NSHIFT] = lanczos[:, weight] * 0.25
    return out.astype(np.float32)


def halves(x):
    high = x.astype(BF16)
    return high, (x - high.astype(F32)).astype(BF16)


def dot(a, b):
    return jnp.dot(a, b, preferred_element_type=F32)


def exact_dot(a, b):
    return jnp.dot(a, b, precision=HIGHEST, preferred_element_type=F32)


def exact_dot_nt(a, b):
    return lax.dot_general(a, b, (((1,), (1,)), ((), ())), precision=HIGHEST, preferred_element_type=F32)


def kernel(
    n_wide, n_narrow,
    frames, anchor, shift, guess_hbm, table_hbm,
    r_hbm, w_hbm, z_hbm, coef,
    guess, pixels, table, vec, whole, wide_edges, feat, acc, more, frb, perm, lhs, lhsb,
    from_side, from_row, from_corner, sums_a, sums_b,
    send, recv, fsend, frecv, loc, stores, asend, arecv, bsend, brecv,
):
    column = lax.axis_index("wide")
    row = lax.axis_index("narrow")
    left, right = lax.rem(column + n_wide - 1, n_wide), lax.rem(column + 1, n_wide)
    up, down = lax.rem(row + n_narrow - 1, n_narrow), lax.rem(row + 1, n_narrow)
    core, chip = lax.rem(column, 2), column // 2
    n_chip = n_wide // 2

    def at(w, n):
        return {"wide": w, "narrow": n}

    near = [at(right, row), at(left, row), at(column, down), at(column, up),
            at(right, down), at(left, down), at(right, up), at(left, up)]
    mates_a = [(row + (k // 2), core + (k % 2)) for k in range(1, 2 * n_narrow)]
    mates_a = [at(chip * 2 + lax.rem(c, 2), lax.rem(r, n_narrow)) for r, c in mates_a]
    mates_b = [at(lax.rem(chip + k, n_chip) * 2 + core, row) for k in range(1, n_chip)]

    barrier = pltpu.get_barrier_semaphore()
    everyone = near + mates_a + mates_b
    for device in everyone:
        pl.semaphore_signal(barrier, inc=1, device_id=device, device_id_type=pl.DeviceIdType.MESH)

    load_guess = pltpu.make_async_copy(guess_hbm, guess, loc.at[0])
    load_table = pltpu.make_async_copy(table_hbm, table, loc.at[1])
    own = pltpu.make_async_copy(frames, frb.at[8 * FS : 16 * FS], loc.at[2])
    load_guess.start()
    load_table.start()

    k_id = lax.broadcasted_iota(jnp.int32, (512, 128), 0)
    n_id = lax.broadcasted_iota(jnp.int32, (512, 128), 1)

    def permutation(which, target):
        for c in range(4):
            perm[which, :, c * 128 : c * 128 + 128] = jnp.where(n_id + 128 * c == target, 1.0, 0.0).astype(BF16)

    permutation(0, 128 * (k_id & 3) + (k_id >> 2))

    zero8 = jnp.zeros((8, 128), F32)

    def edge_masks(size):
        lane = lax.broadcasted_iota(jnp.int32, (size, 128), 1)
        return lane == 0, lane == 127

    def gather_edges(sides):
        packed = None
        for shift_by, part in sides:
            first, last = edge_masks(part.shape[0])
            term = pltpu.roll(jnp.where(first | last, part, 0.0), shift_by, axis=1)
            packed = term if packed is None else packed + term
        return packed

    def pack(v):
        packed = wide_edges[0:PACK, :]
        for g in range(1, 6):
            packed = packed + pltpu.roll(wide_edges[g * PACK : g * PACK + PACK, :], 16 * g, axis=1)
        vec[v, 4, 0:PACK, :] = packed
        vec[v, 4, 512:528, :] = packed[72:88]

    def unpack(v):
        for g in range(6):
            wide_edges[g * PACK : g * PACK + PACK, :] = pltpu.roll(vec[v, 4, 0:PACK, :], 127 - 16 * g, axis=1)

    for q in range(4):
        vec[0, q, 0:8, :] = zero8
        vec[0, q, ROWS - 8 : ROWS, :] = zero8
    wide_edges[0:8, :] = zero8
    wide_edges[ROWS - 8 : ROWS, :] = zero8

    def spread_guess(b):
        into = slice(b * 128 + 8, b * 128 + 136)
        high, low = halves(guess[b * 128 : b * 128 + 128, :])
        x = dot(high, perm[0]) + dot(low, perm[0])
        x = [x[:, q * 128 : q * 128 + 128] for q in range(4)]
        for q in range(4):
            vec[0, q, into, :] = x[q]
        wide_edges[into, :] = gather_edges([(4 * q + 1, x[q]) for q in range(4)])

    load_guess.wait()
    for b in range(4):
        spread_guess(b)
    pack(0)

    pl.semaphore_wait(barrier, len(everyone))

    def exchange(v):
        edges = vec.at[v, 4]
        parts = [
            (edges.at[0:PACK], from_side.at[v, 0]),
            (edges.at[0:PACK], from_side.at[v, 1]),
            (vec.at[v, :, 512:528], from_row.at[v, 0]),
            (vec.at[v, :, 0:16], from_row.at[v, 1]),
            (edges.at[72:88], from_corner.at[v, 0]),
            (edges.at[72:88], from_corner.at[v, 1]),
            (edges.at[0:16], from_corner.at[v, 2]),
            (edges.at[0:16], from_corner.at[v, 3]),
        ]
        copies = []
        for k, (source, target) in enumerate(parts):
            copy = pltpu.make_async_remote_copy(
                src_ref=source, dst_ref=target, send_sem=send.at[v, k], recv_sem=recv.at[v, k],
                device_id=near[k], device_id_type=pl.DeviceIdType.MESH)
            copy.start()
            copies.append(copy)
        return copies

    def settle(v, copies):
        for copy in copies:
            copy.wait()
        has_left, has_right = column > 0, column < n_wide - 1
        has_up, has_down = row > 0, row < n_narrow - 1
        lane16 = lax.broadcasted_iota(jnp.int32, (16, 128), 1)
        sub16 = lax.broadcasted_iota(jnp.int32, (16, 128), 0)
        in_top, in_low = lane16 < 16, (lane16 >= 80) & (lane16 < 96)

        def with_rows(middle, above, below):
            above = jnp.where(in_top & has_up, pltpu.roll(above, 48, axis=1), 0.0)
            below = jnp.where(in_low & has_down, pltpu.roll(below, 80, axis=1), 0.0)
            return jnp.concatenate([middle[0:16] + above, middle[16:72], middle[72:88] + below], axis=0)

        mine = with_rows(vec[v, 4, 0:PACK, :], from_row[v, 0, 4], from_row[v, 1, 4])
        lefts = with_rows(from_side[v, 0], from_corner[v, 0], from_corner[v, 2])
        rights = with_rows(from_side[v, 1], from_corner[v, 1], from_corner[v, 3])
        kind = lax.rem(lax.broadcasted_iota(jnp.int32, (PACK, 128), 1), 4)
        other = jnp.where(kind == 1, pltpu.roll(lefts, 127, axis=1), 0.0)
        other = jnp.where(kind == 3, pltpu.roll(lefts, 3, axis=1), other)
        other = jnp.where(((kind == 1) | (kind == 3)) & has_left, other, 0.0)
        facing = jnp.where(kind == 0, pltpu.roll(rights, 125, axis=1), 0.0)
        facing = jnp.where(kind == 2, pltpu.roll(rights, 1, axis=1), facing)
        facing = jnp.where(((kind == 0) | (kind == 2)) & has_right, facing, 0.0)
        both = mine + other + facing
        both = jnp.where((kind == 3) & (column == 0), 0.0, both)
        both = jnp.where((kind == 2) & (column == n_wide - 1), 0.0, both)
        top = jnp.where(in_top & (sub16 < 8) & (row == 0), 0.0, both[0:16])
        low = jnp.where(in_low & (sub16 >= 8) & (row == n_narrow - 1), 0.0, both[72:88])
        vec[v, 4, 0:PACK, :] = jnp.concatenate([top, both[16:72], low], axis=0)
        for q in range(4):
            x = vec[v, q, 0:16, :] + jnp.where(has_up, from_row[v, 0, q], 0.0)
            vec[v, q, 0:16, :] = jnp.where((sub16 < 8) & (row == 0), 0.0, x)
            x = vec[v, q, 512:528, :] + jnp.where(has_down, from_row[v, 1, q], 0.0)
            vec[v, q, 512:528, :] = jnp.where((sub16 >= 8) & (row == n_narrow - 1), 0.0, x)

    moves = exchange(0)
    frame_moves = []
    for k, device in enumerate((at(right, row), at(left, row))):
        copy = pltpu.make_async_remote_copy(
            src_ref=frames, dst_ref=frb.at[16 * FS * k : 16 * FS * k + 8 * FS], send_sem=fsend.at[k],
            recv_sem=frecv.at[k], device_id=device, device_id_type=pl.DeviceIdType.MESH)
        copy.start()
        frame_moves.append(copy)
    own.start()
    permutation(1, 4 * (k_id & 127) + (k_id >> 7))

    n_frames = 8 * n_wide
    f_id = lax.broadcasted_iota(jnp.int32, (n_frames, 128), 0)
    slot = lax.broadcasted_iota(jnp.int32, (n_frames, 128), 1)
    slot = slot - (slot // 32) * 32
    wanted = lax.rem(slot + 8 * left, n_frames)
    pick = jnp.where((f_id == wanted) & (slot < 24), 1.0, 0.0).astype(BF16)
    looks = jnp.where(jnp.broadcast_to(anchor[...], (16, n_frames)) == column, 1.0, 0.0)
    code_row = lax.broadcasted_iota(jnp.int32, (16, n_frames), 0)
    codes = jnp.where(code_row == 0, looks, jnp.where(
        code_row == 1, jnp.broadcast_to(shift[0, 0:1, :], (16, n_frames)).astype(F32),
        jnp.broadcast_to(shift[0, 1:2, :], (16, n_frames)).astype(F32)))
    codes = dot(codes.astype(BF16), pick)
    used = codes[0:1]
    load_table.wait()
    lane128 = lax.broadcasted_iota(jnp.int32, (128, 128), 1)
    sub128 = lax.broadcasted_iota(jnp.int32, (128, 128), 0)
    one_a = jnp.where(jnp.broadcast_to(codes[1:2], (128, 128)).astype(jnp.int32) == sub128, 1.0, 0.0)
    one_b = jnp.where(jnp.broadcast_to(codes[2:3], (128, 128)).astype(jnp.int32) == sub128, 1.0, 0.0)
    second = lax.rem(lane128 // 32, 2) == 1
    tall = exact_dot(table[2], one_b) * jnp.where(
        second, exact_dot(table[1], one_a), exact_dot(table[0], one_a)) * used
    for which, keep in enumerate((second, lane128 >= 0, jnp.logical_not(second))):
        kept = jnp.where(keep, tall, 0.0)
        high, low = halves(kept)
        lhsb[which, :, 0:128] = high
        lhsb[which, :, 128:256] = jnp.where(lane128 < 64, low.astype(F32), 0.0).astype(BF16)
        half = jnp.where(lane128 < 64, kept, 0.0)
        high, low = halves(exact_dot_nt(half, half))
        lhs[which, :, 0:128] = high
        lhs[which, :, 128:256] = high
        lhs[which, :, 256:384] = low

    settle(0, moves)

    def unfold(v, features=True):
        unpack(v)

        def step(i, carry):
            rows = pl.ds(pl.multiple_of(i * UNFOLD, 8), UNFOLD)
            first, last = edge_masks(UNFOLD)
            packed = wide_edges[rows, :]
            raw = [vec[v, q, rows, :] for q in range(4)]
            mid, nxt, prv = [], [], []
            for q in range(4):
                spun = packed if q == 0 else pltpu.roll(packed, 128 - 4 * q, axis=1)
                x = jnp.where(first | last, spun, raw[q])
                mid.append(x)
                if features:
                    side = pltpu.roll(packed, 126 - 4 * q, axis=1)
                    prv.append(jnp.where(first, side, pltpu.roll(x, 1, axis=1)))
                    if q < 3:
                        nxt.append(jnp.where(last, side, pltpu.roll(x, 127, axis=1)))
            for q in range(4):
                whole[v, q, rows, :] = mid[q]
            if not features:
                return carry
            m23, p23 = mid[2] + mid[3], prv[2] + prv[3]
            m123, p123 = mid[1] + m23, prv[1] + p23
            m01, n01 = mid[0] + mid[1], nxt[0] + nxt[1]
            out = [mid[0] + m123, m123 + nxt[0], m23 + n01, mid[3] + (n01 + nxt[2]),
                   prv[0] + p123, p123 + mid[0], p23 + m01, prv[3] + (m01 + mid[2])]
            for f in range(8):
                feat[f, rows, :] = out[f]
            return carry

        lax.fori_loop(0, ROWS // UNFOLD, step, 0)

    def join(parts):
        return parts[0] if len(parts) == 1 else jnp.concatenate(parts, axis=1)

    def blocks(starts):
        highs, lows = [], []
        for start in starts:
            pairs = [halves(feat[f, pl.ds(start, 16), :]) for f in range(8)]
            highs.append(jnp.concatenate([p[0] for p in pairs], axis=0))
            lows.append(jnp.concatenate([p[1] for p in pairs], axis=0))
        high, low = join(highs), join(lows)
        return jnp.concatenate([high, low, high], axis=0)

    def stack(outs, carry):
        done = []
        for out in outs:
            done.append([out[16 * f : 16 * f + 8] if carry is None else carry[f] + out[16 * f : 16 * f + 8]
                         for f in range(8)])
            carry = [out[16 * f + 8 : 16 * f + 16] for f in range(8)]
        return done, carry

    def sweep(results, save):
        def some(starts, kinds, carry):
            outs = []
            for k in range(0, len(starts), 2):
                outs.extend(results(starts[k : k + 2], kinds[k : k + 2]))
            done, carry = stack(outs, carry)
            for start, tiles in zip(starts, done):
                save(start, tiles)
            return tuple(carry)

        carry = some([8 * k for k in range(MIX)], [0] + [1] * (MIX - 1), None)

        def step(i, carry):
            start = pl.multiple_of(i * (8 * MIX), 8)
            return some([start + 8 * k for k in range(MIX)], [1] * MIX, carry)

        carry = lax.fori_loop(1, 64 // MIX, step, carry)
        carry = some([512], [2], carry)
        save(520, carry)

    def cut(out):
        return [out[:, 128 * k : 128 * k + 128] for k in range(out.shape[1] // 128)]

    def mix():
        def results(starts, kinds):
            if len(set(kinds)) > 1:
                return [dot(lhs[w], blocks([s])) for s, w in zip(starts, kinds)]
            return cut(dot(lhs[kinds[0]], blocks(starts)))

        def save(start, tiles):
            for f in range(8):
                acc[f, pl.ds(start, 8), :] = tiles[f]

        sweep(results, save)

    def take_frames():
        def pixels(start, kind):
            sample = start // 4
            rows = [0 if kind == 0 else sample - 1, FS - 1 if kind == 2 else sample]
            parts = []
            for i in rows:
                parts += [frb[pl.ds(i, 24, stride=FS), :], zero8]
            high, low = halves(jnp.concatenate(parts, axis=0))
            return jnp.concatenate([high, low], axis=0)

        def results(starts, kinds):
            if len(set(kinds)) > 1:
                return [results([s], [w])[0] for s, w in zip(starts, kinds)]
            both = join([pixels(s, w) for s, w in zip(starts, kinds)])
            return cut(dot(lhsb[kinds[0]], jnp.concatenate([both, both], axis=0)))

        def save(start, tiles):
            for f in range(8):
                more[f, pl.ds(start, 8), :] = tiles[f]

        sweep(results, save)

    def fold(v, sign, measure, counts):
        def step(i, sums):
            rows = pl.ds(pl.multiple_of(i * FOLD, 8), FOLD)
            first, last = edge_masks(FOLD)
            row_id = i * FOLD + lax.broadcasted_iota(jnp.int32, (FOLD, 128), 0)
            inside = (row_id >= 8) & (row_id < ROWS - 8)
            damp = jnp.where(inside, DAMP, 0.0)
            cur = [acc[q, rows, :] for q in range(4)]
            pre = [acc[4 + q, rows, :] for q in range(4)]
            if v == 0:
                cur = [c - more[q, rows, :] for q, c in enumerate(cur)]
                pre = [p - more[4 + q, rows, :] for q, p in enumerate(pre)]
            old = [whole[v, q, rows, :] for q in range(4)]
            rolled = [pltpu.roll(x, 127, axis=1) for x in pre]
            here = [c + jnp.where(last, 0.0, p) for c, p in zip(cur, rolled)]
            back = [p + jnp.where(last, 0.0, c) for c, p in zip(cur, rolled)]
            h01 = here[0] + here[1]
            h012 = h01 + here[2]
            k23 = back[2] + back[3]
            out = [here[0] + pltpu.roll(back[1] + k23, 1, axis=1), h01 + pltpu.roll(k23, 1, axis=1),
                   h012 + pltpu.roll(back[3], 1, axis=1), h012 + here[3]]
            h23 = here[2] + here[3]
            r01 = pre[0] + pre[1]
            r012 = r01 + pre[2]
            over = [jnp.where(first, pre[0], here[1] + h23), jnp.where(first, r01, h23),
                    jnp.where(first, r012, here[3]), jnp.where(first, r012 + pre[3], 0.0)]
            out = [o + damp * x for o, x in zip(out, old)]
            if sign < 0:
                out, over = [-o for o in out], [-o for o in over]
            packed = gather_edges([(4 * q + 1, out[q]) for q in range(4)] + [(4 * q + 3, over[q]) for q in range(4)])
            more_sums = measure(rows, inside, old, out)
            for q in range(4):
                vec[v + 1, q, rows, :] = out[q]
            wide_edges[rows, :] = packed
            return tuple(s + m for s, m in zip(sums, more_sums))

        sums = lax.fori_loop(0, ROWS // FOLD, step, (jnp.zeros((FOLD, 128), F32),) * counts)
        pack(v + 1)
        return [fewer_rows(s) for s in sums]

    def fewer_rows(x):
        total = x[0:8]
        for k in range(8, x.shape[0], 8):
            total = total + x[k : k + 8]
        return total

    def no_sums(rows, inside, old, out):
        return ()

    def outer_columns(product):
        kind = lax.broadcasted_iota(jnp.int32, (PACK, 128), 1) & 3
        return fewer_rows(jnp.where(kind >= 2, product, 0.0))

    def gather(value, slots, mates, sent, landed):
        slots[0] = value
        copies = []
        for k, device in enumerate(mates):
            copy = pltpu.make_async_remote_copy(
                src_ref=slots.at[0], dst_ref=slots.at[k + 1], send_sem=sent.at[k],
                recv_sem=landed.at[k], device_id=device, device_id_type=pl.DeviceIdType.MESH)
            copy.start()
            copies.append(copy)
        return copies

    def collect(copies, slots):
        for copy in copies:
            copy.wait()
        value = slots[0]
        for k in range(len(copies)):
            value = value + slots[k + 1]
        return value

    def gather_a(values):
        lines = [jnp.sum(value, axis=0, keepdims=True) for value in values]
        return gather(jnp.concatenate(lines + [zero8[0:4]], axis=0), sums_a, mates_a, asend, arecv)

    def gather_b(copies):
        return gather(collect(copies, sums_a), sums_b, mates_b, bsend, brecv)

    def finish_sums(copies):
        totals = jnp.broadcast_to(jnp.sum(collect(copies, sums_b), axis=1, keepdims=True), (8, 128))
        return [jnp.broadcast_to(totals[i : i + 1], (8, 128)) for i in range(4)]

    def write_pixels(v, out):
        for b in range(4):
            rows = slice(b * 128, b * 128 + 128)
            x = jnp.concatenate([whole[v, q, b * 128 + 8 : b * 128 + 136, :] for q in range(4)], axis=1)
            high, low = halves(x)
            pixels[v - 1, rows, :] = dot(high, perm[1]) + dot(low, perm[1])
        store = pltpu.make_async_copy(pixels.at[v - 1], out, stores.at[v - 1])
        store.start()
        return store

    unfold(0)
    mix()
    own.wait()
    for copy in frame_moves:
        copy.wait()
    take_frames()
    fold(0, -1.0, no_sums, 0)
    settle(1, exchange(1))

    unfold(1)
    mix()

    def measure_w(rows, inside, old, out):
        rr = old[0] * old[0] + old[1] * old[1] + (old[2] * old[2] + old[3] * old[3])
        rw = old[0] * out[0] + old[1] * out[1] + (old[2] * out[2] + old[3] * out[3])
        return jnp.where(inside, rr, 0.0), rw

    rr, rw = fold(1, 1.0, measure_w, 2)
    rw = rw + outer_columns(vec[1, 4, 0:PACK, :] * vec[2, 4, 0:PACK, :])
    moves = exchange(2)
    written = [write_pixels(1, r_hbm)]
    settle(2, moves)

    unfold(2)
    mix()
    ww = jnp.zeros((8, 128), F32)
    for q in range(4):
        own_rows = whole[2, q, 8 : ROWS - 8, :]
        ww = ww + fewer_rows(own_rows * own_rows)
    wz = DAMP * ww
    for f in range(8):
        wz = wz + fewer_rows(feat[f] * acc[f])
    sums = gather_a((rr, rw, ww, wz))
    fold(2, 1.0, no_sums, 0)
    moves = exchange(3)
    sums = gather_b(sums)
    written.append(write_pixels(2, w_hbm))
    settle(3, moves)
    unfold(3, features=False)
    written.append(write_pixels(3, z_hbm))
    rr, rw, ww, wz = finish_sums(sums)
    alpha = rr / rw
    ss = alpha * alpha * ww - rr
    sw = rw - alpha * ww
    beta = ss / rr
    curve = (sw - alpha * (ww - alpha * wz)) + 2.0 * beta * sw + beta * beta * rw
    step = ss / curve
    coef[0] = alpha + step * (1.0 + beta)
    coef[1] = step * alpha
    for store in written:
        store.wait()


def closing(guess_hbm, r_hbm, w_hbm, z_hbm, coef, solution_hbm, residual_hbm, held, made, loads, stores):
    sources = (r_hbm, w_hbm, z_hbm, guess_hbm)
    copies = {}
    for b in range(CLOSE):
        rows = slice(b * (TS // CLOSE), (b + 1) * (TS // CLOSE))
        for k, source in enumerate(sources):
            copies[b, k] = pltpu.make_async_copy(source.at[rows], held.at[k, rows], loads.at[b, k])
            copies[b, k].start()
    c1, c2 = coef[0, 0:1, 0:1], coef[1, 0:1, 0:1]
    writes = []
    for b in range(CLOSE):
        rows = slice(b * (TS // CLOSE), (b + 1) * (TS // CLOSE))
        for k in range(4):
            copies[b, k].wait()
        r, w = held[0, rows, :], held[1, rows, :]
        made[1, rows, :] = r - c1 * w + c2 * held[2, rows, :]
        made[0, rows, :] = held[3, rows, :] + c1 * r - c2 * w
        for k, target in enumerate((solution_hbm, residual_hbm)):
            writes.append(pltpu.make_async_copy(made.at[k, rows], target.at[rows], stores.at[b, k]))
            writes[-1].start()
    for write in writes:
        write.wait()


def on_device(n_wide, n_narrow, frames, anchor, shift, guess):
    vmem, hbm = pl.BlockSpec(memory_space=pltpu.VMEM), pl.BlockSpec(memory_space=pltpu.HBM)
    image = jax.ShapeDtypeStruct((TS, TS), F32)
    dma = pltpu.SemaphoreType.DMA
    n_a, n_b = 2 * n_narrow, n_wide // 2
    r, w, z, coef = pl.pallas_call(
        functools.partial(kernel, n_wide, n_narrow),
        out_shape=(image, image, image, jax.ShapeDtypeStruct((2, 8, 128), F32)),
        in_specs=[hbm, vmem, vmem, hbm, hbm],
        out_specs=(hbm, hbm, hbm, vmem),
        scratch_shapes=[
            pltpu.VMEM((TS, TS), F32),
            pltpu.VMEM((3, TS, TS), F32),
            pltpu.VMEM((3, 128, 128), F32),
            pltpu.VMEM((4, 5, ROWS, 128), F32),
            pltpu.VMEM((4, 4, ROWS, 128), F32),
            pltpu.VMEM((ROWS, 128), F32),
            pltpu.VMEM((8, ROWS, 128), F32),
            pltpu.VMEM((8, ROWS, 128), F32),
            pltpu.VMEM((8, ROWS, 128), F32),
            pltpu.VMEM((24 * FS, 128), F32),
            pltpu.VMEM((2, 512, 512), BF16),
            pltpu.VMEM((3, 128, 384), BF16),
            pltpu.VMEM((3, 128, 256), BF16),
            pltpu.VMEM((4, 2, PACK, 128), F32),
            pltpu.VMEM((4, 2, 5, 16, 128), F32),
            pltpu.VMEM((4, 4, 16, 128), F32),
            pltpu.VMEM((n_a, 8, 128), F32),
            pltpu.VMEM((n_b, 8, 128), F32),
            dma((4, 8)), dma((4, 8)), dma((2,)), dma((2,)), dma((3,)), dma((3,)),
            dma((n_a,)), dma((n_a,)), dma((n_b,)), dma((n_b,)),
        ],
        compiler_params=pltpu.CompilerParams(
            collective_id=0, has_side_effects=True, vmem_limit_bytes=VMEM_BYTES),
    )(frames.reshape(8 * FS, FS), anchor, shift.transpose(0, 2, 1), guess, jnp.asarray(tables()))
    return pl.pallas_call(
        closing,
        out_shape=(image, image),
        in_specs=[hbm, hbm, hbm, hbm, vmem],
        out_specs=(hbm, hbm),
        scratch_shapes=[pltpu.VMEM((4, TS, TS), F32), pltpu.VMEM((2, TS, TS), F32), dma((CLOSE, 4)), dma((CLOSE, 2))],
        compiler_params=pltpu.CompilerParams(vmem_limit_bytes=VMEM_BYTES),
    )(guess, r, w, z, coef)


def solution(mesh):
    placed = (P("narrow", "wide", None, None), P("narrow", None), P("narrow", None, None), P("narrow", "wide"))
    return jax.shard_map(
        functools.partial(on_device, mesh.shape["wide"], mesh.shape["narrow"]),
        mesh=mesh,
        in_specs=placed,
        out_specs=(P("narrow", "wide"), P("narrow", "wide")),
        check_vma=False,
    )
```

```python
import functools

import jax
import jax.numpy as jnp
import numpy as np
from jax import lax
from jax.experimental import pallas as pl
from jax.experimental.pallas import tpu as pltpu
from jax.sharding import PartitionSpec as P

NSHIFT = 16
DAMP = 0.05
TS = 512
FS = 128
ROWS = TS + 16
TILES = ROWS // 8
GROUP = 11
PACK = GROUP * 8
F32 = jnp.float32
BF16 = jnp.bfloat16
UNFOLD = 528
FOLD = 528
MIX = 64
CLOSE = 4
PARTS = 4
VMEM_BYTES = 62 * 2**20
HIGHEST = lax.Precision.HIGHEST


def tables():
    fraction = np.arange(NSHIFT, dtype=np.float64) / NSHIFT
    offsets = np.arange(8, dtype=np.float64)[None, :] - 3.0 - fraction[:, None]
    lanczos = np.sinc(offsets) * np.sinc(offsets / 4.0)
    lanczos = lanczos / lanczos.sum(axis=1, keepdims=True)
    spread = np.arange(11)[None, :] - np.arange(8)[:, None]
    taps = lanczos @ np.where((spread >= 0) & (spread < 4), 0.25, 0.0)
    out = np.zeros((3, 128, 128), np.float64)
    for feature in range(8):
        weight = feature + 4 if feature < 4 else feature - 4
        for r in range(16):
            for second in range(2):
                if 0 <= r - 4 * second <= 10:
                    out[second, feature * 16 + r, :NSHIFT] = taps[:, r - 4 * second]
            out[2, feature * 16 + r, :NSHIFT] = lanczos[:, weight] * 0.25
    return out.astype(np.float32)


def halves(x):
    high = x.astype(BF16)
    return high, (x - high.astype(F32)).astype(BF16)


def dot(a, b):
    return jnp.dot(a, b, preferred_element_type=F32)


def exact_dot(a, b):
    return jnp.dot(a, b, precision=HIGHEST, preferred_element_type=F32)


def exact_dot_nt(a, b):
    return lax.dot_general(a, b, (((1,), (1,)), ((), ())), precision=HIGHEST, preferred_element_type=F32)


def kernel(
    n_wide, n_narrow,
    frames, anchor, shift, guess_hbm, table_hbm,
    solution_hbm, residual_hbm,
    guess, pixels, table, vec, whole, wide_edges, feat, acc, more, frb, perm, lhs, lhsb,
    from_side, from_row, from_corner, sums_a, sums_b,
    send, recv, fsend, frecv, loc, stores, asend, arecv, bsend, brecv,
):
    column = lax.axis_index("wide")
    row = lax.axis_index("narrow")
    left, right = lax.rem(column + n_wide - 1, n_wide), lax.rem(column + 1, n_wide)
    up, down = lax.rem(row + n_narrow - 1, n_narrow), lax.rem(row + 1, n_narrow)
    core, chip = lax.rem(column, 2), column // 2
    n_chip = n_wide // 2

    def at(w, n):
        return {"wide": w, "narrow": n}

    near = [at(right, row), at(left, row), at(column, down), at(column, up),
            at(right, down), at(left, down), at(right, up), at(left, up)]
    mates_a = [(row + (k // 2), core + (k % 2)) for k in range(1, 2 * n_narrow)]
    mates_a = [at(chip * 2 + lax.rem(c, 2), lax.rem(r, n_narrow)) for r, c in mates_a]
    mates_b = [at(lax.rem(chip + k, n_chip) * 2 + core, row) for k in range(1, n_chip)]

    barrier = pltpu.get_barrier_semaphore()
    everyone = near + mates_a + mates_b
    for device in everyone:
        pl.semaphore_signal(barrier, inc=1, device_id=device, device_id_type=pl.DeviceIdType.MESH)

    load_guess = pltpu.make_async_copy(guess_hbm, guess, loc.at[0])
    load_table = pltpu.make_async_copy(table_hbm, table, loc.at[1])
    own = pltpu.make_async_copy(frames, frb.at[8 * FS : 16 * FS], loc.at[2])
    load_guess.start()
    load_table.start()

    k_id = lax.broadcasted_iota(jnp.int32, (512, 128), 0)
    n_id = lax.broadcasted_iota(jnp.int32, (512, 128), 1)

    def permutation(which, target):
        for c in range(4):
            perm[which, :, c * 128 : c * 128 + 128] = jnp.where(n_id + 128 * c == target, 1.0, 0.0).astype(BF16)

    permutation(0, 128 * (k_id & 3) + (k_id >> 2))

    zero8 = jnp.zeros((8, 128), F32)

    def edge_masks(size):
        lane = lax.broadcasted_iota(jnp.int32, (size, 128), 1)
        return lane == 0, lane == 127

    def gather_edges(sides):
        packed = None
        for shift_by, part in sides:
            first, last = edge_masks(part.shape[0])
            term = pltpu.roll(jnp.where(first | last, part, 0.0), shift_by, axis=1)
            packed = term if packed is None else packed + term
        return packed

    def pack(v):
        packed = wide_edges[0:PACK, :]
        for g in range(1, 6):
            packed = packed + pltpu.roll(wide_edges[g * PACK : g * PACK + PACK, :], 16 * g, axis=1)
        vec[v, 4, 0:PACK, :] = packed
        vec[v, 4, 512:528, :] = packed[72:88]

    def unpack(v):
        for g in range(6):
            wide_edges[g * PACK : g * PACK + PACK, :] = pltpu.roll(vec[v, 4, 0:PACK, :], 127 - 16 * g, axis=1)

    for q in range(4):
        vec[0, q, 0:8, :] = zero8
        vec[0, q, ROWS - 8 : ROWS, :] = zero8
    wide_edges[0:8, :] = zero8
    wide_edges[ROWS - 8 : ROWS, :] = zero8

    def spread_guess(b):
        into = slice(b * 128 + 8, b * 128 + 136)
        high, low = halves(guess[b * 128 : b * 128 + 128, :])
        x = dot(high, perm[0]) + dot(low, perm[0])
        x = [x[:, q * 128 : q * 128 + 128] for q in range(4)]
        for q in range(4):
            vec[0, q, into, :] = x[q]
        wide_edges[into, :] = gather_edges([(4 * q + 1, x[q]) for q in range(4)])

    load_guess.wait()
    for b in range(4):
        spread_guess(b)
    pack(0)

    pl.semaphore_wait(barrier, len(everyone))

    def exchange(v):
        edges = vec.at[v, 4]
        parts = [
            (edges.at[0:PACK], from_side.at[v, 0]),
            (edges.at[0:PACK], from_side.at[v, 1]),
            (vec.at[v, :, 512:528], from_row.at[v, 0]),
            (vec.at[v, :, 0:16], from_row.at[v, 1]),
            (edges.at[72:88], from_corner.at[v, 0]),
            (edges.at[72:88], from_corner.at[v, 1]),
            (edges.at[0:16], from_corner.at[v, 2]),
            (edges.at[0:16], from_corner.at[v, 3]),
        ]
        copies = []
        for k in (4, 5, 6, 7, 0, 1, 2, 3):
            source, target = parts[k]
            copy = pltpu.make_async_remote_copy(
                src_ref=source, dst_ref=target, send_sem=send.at[v, k], recv_sem=recv.at[v, k],
                device_id=near[k], device_id_type=pl.DeviceIdType.MESH)
            copy.start()
            copies.append(copy)
        return copies

    def settle(v, copies):
        for copy in copies:
            copy.wait()
        has_left, has_right = column > 0, column < n_wide - 1
        has_up, has_down = row > 0, row < n_narrow - 1
        lane16 = lax.broadcasted_iota(jnp.int32, (16, 128), 1)
        sub16 = lax.broadcasted_iota(jnp.int32, (16, 128), 0)
        in_top, in_low = lane16 < 16, (lane16 >= 80) & (lane16 < 96)

        def with_rows(middle, above, below):
            above = jnp.where(in_top & has_up, pltpu.roll(above, 48, axis=1), 0.0)
            below = jnp.where(in_low & has_down, pltpu.roll(below, 80, axis=1), 0.0)
            return jnp.concatenate([middle[0:16] + above, middle[16:72], middle[72:88] + below], axis=0)

        mine = with_rows(vec[v, 4, 0:PACK, :], from_row[v, 0, 4], from_row[v, 1, 4])
        lefts = with_rows(from_side[v, 0], from_corner[v, 0], from_corner[v, 2])
        rights = with_rows(from_side[v, 1], from_corner[v, 1], from_corner[v, 3])
        kind = lax.rem(lax.broadcasted_iota(jnp.int32, (PACK, 128), 1), 4)
        other = jnp.where(kind == 1, pltpu.roll(lefts, 127, axis=1), 0.0)
        other = jnp.where(kind == 3, pltpu.roll(lefts, 3, axis=1), other)
        other = jnp.where(((kind == 1) | (kind == 3)) & has_left, other, 0.0)
        facing = jnp.where(kind == 0, pltpu.roll(rights, 125, axis=1), 0.0)
        facing = jnp.where(kind == 2, pltpu.roll(rights, 1, axis=1), facing)
        facing = jnp.where(((kind == 0) | (kind == 2)) & has_right, facing, 0.0)
        both = mine + other + facing
        both = jnp.where((kind == 3) & (column == 0), 0.0, both)
        both = jnp.where((kind == 2) & (column == n_wide - 1), 0.0, both)
        top = jnp.where(in_top & (sub16 < 8) & (row == 0), 0.0, both[0:16])
        low = jnp.where(in_low & (sub16 >= 8) & (row == n_narrow - 1), 0.0, both[72:88])
        vec[v, 4, 0:PACK, :] = jnp.concatenate([top, both[16:72], low], axis=0)
        for q in range(4):
            x = vec[v, q, 0:16, :] + jnp.where(has_up, from_row[v, 0, q], 0.0)
            vec[v, q, 0:16, :] = jnp.where((sub16 < 8) & (row == 0), 0.0, x)
            x = vec[v, q, 512:528, :] + jnp.where(has_down, from_row[v, 1, q], 0.0)
            vec[v, q, 512:528, :] = jnp.where((sub16 >= 8) & (row == n_narrow - 1), 0.0, x)

    moves = exchange(0)
    frame_moves = []
    for k, device in enumerate((at(right, row), at(left, row))):
        copy = pltpu.make_async_remote_copy(
            src_ref=frames, dst_ref=frb.at[16 * FS * k : 16 * FS * k + 8 * FS], send_sem=fsend.at[k],
            recv_sem=frecv.at[k], device_id=device, device_id_type=pl.DeviceIdType.MESH)
        copy.start()
        frame_moves.append(copy)
    own.start()
    permutation(1, 4 * (k_id & 127) + (k_id >> 7))

    n_frames = 8 * n_wide
    f_id = lax.broadcasted_iota(jnp.int32, (n_frames, 128), 0)
    slot = lax.broadcasted_iota(jnp.int32, (n_frames, 128), 1)
    slot = slot - (slot // 32) * 32
    wanted = lax.rem(slot + 8 * left, n_frames)
    pick = jnp.where((f_id == wanted) & (slot < 24), 1.0, 0.0).astype(BF16)
    looks = jnp.where(jnp.broadcast_to(anchor[...], (16, n_frames)) == column, 1.0, 0.0)
    code_row = lax.broadcasted_iota(jnp.int32, (16, n_frames), 0)
    codes = jnp.where(code_row == 0, looks, jnp.where(
        code_row == 1, jnp.broadcast_to(shift[0, 0:1, :], (16, n_frames)).astype(F32),
        jnp.broadcast_to(shift[0, 1:2, :], (16, n_frames)).astype(F32)))
    codes = dot(codes.astype(BF16), pick)
    used = codes[0:1]
    load_table.wait()
    lane128 = lax.broadcasted_iota(jnp.int32, (128, 128), 1)
    sub128 = lax.broadcasted_iota(jnp.int32, (128, 128), 0)
    one_a = jnp.where(jnp.broadcast_to(codes[1:2], (128, 128)).astype(jnp.int32) == sub128, 1.0, 0.0)
    one_b = jnp.where(jnp.broadcast_to(codes[2:3], (128, 128)).astype(jnp.int32) == sub128, 1.0, 0.0)
    second = lax.rem(lane128 // 32, 2) == 1
    tall = exact_dot(table[2], one_b) * jnp.where(
        second, exact_dot(table[1], one_a), exact_dot(table[0], one_a)) * used
    for which, keep in enumerate((second, lane128 >= 0, jnp.logical_not(second))):
        kept = jnp.where(keep, tall, 0.0)
        high, low = halves(kept)
        lhsb[which, :, 0:128] = high
        lhsb[which, :, 128:256] = jnp.where(lane128 < 64, low.astype(F32), 0.0).astype(BF16)
        half = jnp.where(lane128 < 64, kept, 0.0)
        high, low = halves(exact_dot_nt(half, half))
        lhs[which, :, 0:128] = high
        lhs[which, :, 128:256] = high
        lhs[which, :, 256:384] = low

    settle(0, moves)

    def unfold(v, features=True):
        unpack(v)

        def step(i, carry):
            rows = pl.ds(pl.multiple_of(i * UNFOLD, 8), UNFOLD)
            first, last = edge_masks(UNFOLD)
            packed = wide_edges[rows, :]
            raw = [vec[v, q, rows, :] for q in range(4)]
            mid, nxt, prv = [], [], []
            for q in range(4):
                spun = packed if q == 0 else pltpu.roll(packed, 128 - 4 * q, axis=1)
                x = jnp.where(first | last, spun, raw[q])
                mid.append(x)
                if features:
                    side = pltpu.roll(packed, 126 - 4 * q, axis=1)
                    prv.append(jnp.where(first, side, pltpu.roll(x, 1, axis=1)))
                    if q < 3:
                        nxt.append(jnp.where(last, side, pltpu.roll(x, 127, axis=1)))
            for q in range(4):
                whole[v, q, rows, :] = mid[q]
            if not features:
                return carry
            m23, p23 = mid[2] + mid[3], prv[2] + prv[3]
            m123, p123 = mid[1] + m23, prv[1] + p23
            m01, n01 = mid[0] + mid[1], nxt[0] + nxt[1]
            out = [mid[0] + m123, m123 + nxt[0], m23 + n01, mid[3] + (n01 + nxt[2]),
                   prv[0] + p123, p123 + mid[0], p23 + m01, prv[3] + (m01 + mid[2])]
            for f in range(8):
                feat[f, rows, :] = out[f]
            return carry

        lax.fori_loop(0, ROWS // UNFOLD, step, 0)

    def join(parts):
        return parts[0] if len(parts) == 1 else jnp.concatenate(parts, axis=1)

    def blocks(starts):
        highs, lows = [], []
        for start in starts:
            pairs = [halves(feat[f, pl.ds(start, 16), :]) for f in range(8)]
            highs.append(jnp.concatenate([p[0] for p in pairs], axis=0))
            lows.append(jnp.concatenate([p[1] for p in pairs], axis=0))
        high, low = join(highs), join(lows)
        return jnp.concatenate([high, low, high], axis=0)

    def stack(outs, carry):
        done = []
        for out in outs:
            done.append([out[16 * f : 16 * f + 8] if carry is None else carry[f] + out[16 * f : 16 * f + 8]
                         for f in range(8)])
            carry = [out[16 * f + 8 : 16 * f + 16] for f in range(8)]
        return done, carry

    def sweep(results, save):
        def some(starts, kinds, carry):
            outs = []
            for k in range(0, len(starts), 2):
                outs.extend(results(starts[k : k + 2], kinds[k : k + 2]))
            done, carry = stack(outs, carry)
            for start, tiles in zip(starts, done):
                save(start, tiles)
            return tuple(carry)

        carry = some([8 * k for k in range(MIX)], [0] + [1] * (MIX - 1), None)

        def step(i, carry):
            start = pl.multiple_of(i * (8 * MIX), 8)
            return some([start + 8 * k for k in range(MIX)], [1] * MIX, carry)

        carry = lax.fori_loop(1, 64 // MIX, step, carry)
        carry = some([512], [2], carry)
        save(520, carry)

    def cut(out):
        return [out[:, 128 * k : 128 * k + 128] for k in range(out.shape[1] // 128)]

    def mix():
        def results(starts, kinds):
            if len(set(kinds)) > 1:
                return [dot(lhs[w], blocks([s])) for s, w in zip(starts, kinds)]
            return cut(dot(lhs[kinds[0]], blocks(starts)))

        def save(start, tiles):
            for f in range(8):
                acc[f, pl.ds(start, 8), :] = tiles[f]

        sweep(results, save)

    def take_frames():
        def pixels(start, kind):
            sample = start // 4
            rows = [0 if kind == 0 else sample - 1, FS - 1 if kind == 2 else sample]
            parts = []
            for i in rows:
                parts += [frb[pl.ds(i, 24, stride=FS), :], zero8]
            high, low = halves(jnp.concatenate(parts, axis=0))
            return jnp.concatenate([high, low], axis=0)

        def results(starts, kinds):
            if len(set(kinds)) > 1:
                return [results([s], [w])[0] for s, w in zip(starts, kinds)]
            both = join([pixels(s, w) for s, w in zip(starts, kinds)])
            return cut(dot(lhsb[kinds[0]], jnp.concatenate([both, both], axis=0)))

        def save(start, tiles):
            for f in range(8):
                more[f, pl.ds(start, 8), :] = tiles[f]

        sweep(results, save)

    def fold(v, sign, measure, counts):
        def step(i, sums):
            rows = pl.ds(pl.multiple_of(i * FOLD, 8), FOLD)
            first, last = edge_masks(FOLD)
            row_id = i * FOLD + lax.broadcasted_iota(jnp.int32, (FOLD, 128), 0)
            inside = (row_id >= 8) & (row_id < ROWS - 8)
            damp = jnp.where(inside, DAMP, 0.0)
            cur = [acc[q, rows, :] for q in range(4)]
            pre = [acc[4 + q, rows, :] for q in range(4)]
            if v == 0:
                cur = [c - more[q, rows, :] for q, c in enumerate(cur)]
                pre = [p - more[4 + q, rows, :] for q, p in enumerate(pre)]
            old = [whole[v, q, rows, :] for q in range(4)]
            rolled = [pltpu.roll(x, 127, axis=1) for x in pre]
            here = [c + jnp.where(last, 0.0, p) for c, p in zip(cur, rolled)]
            back = [p + jnp.where(last, 0.0, c) for c, p in zip(cur, rolled)]
            h01 = here[0] + here[1]
            h012 = h01 + here[2]
            k23 = back[2] + back[3]
            out = [here[0] + pltpu.roll(back[1] + k23, 1, axis=1), h01 + pltpu.roll(k23, 1, axis=1),
                   h012 + pltpu.roll(back[3], 1, axis=1), h012 + here[3]]
            h23 = here[2] + here[3]
            r01 = pre[0] + pre[1]
            r012 = r01 + pre[2]
            over = [jnp.where(first, pre[0], here[1] + h23), jnp.where(first, r01, h23),
                    jnp.where(first, r012, here[3]), jnp.where(first, r012 + pre[3], 0.0)]
            out = [o + damp * x for o, x in zip(out, old)]
            if sign < 0:
                out, over = [-o for o in out], [-o for o in over]
            packed = gather_edges([(4 * q + 1, out[q]) for q in range(4)] + [(4 * q + 3, over[q]) for q in range(4)])
            more_sums = measure(rows, inside, old, out)
            for q in range(4):
                vec[v + 1, q, rows, :] = out[q]
            wide_edges[rows, :] = packed
            return tuple(s + m for s, m in zip(sums, more_sums))

        sums = lax.fori_loop(0, ROWS // FOLD, step, (jnp.zeros((FOLD, 128), F32),) * counts)
        pack(v + 1)
        return [fewer_rows(s) for s in sums]

    def fewer_rows(x):
        total = x[0:8]
        for k in range(8, x.shape[0], 8):
            total = total + x[k : k + 8]
        return total

    def no_sums(rows, inside, old, out):
        return ()

    def outer_columns(product):
        kind = lax.broadcasted_iota(jnp.int32, (PACK, 128), 1) & 3
        return fewer_rows(jnp.where(kind >= 2, product, 0.0))

    def gather(value, slots, mates, sent, landed):
        slots[0] = value
        copies = []
        for k, device in enumerate(mates):
            copy = pltpu.make_async_remote_copy(
                src_ref=slots.at[0], dst_ref=slots.at[k + 1], send_sem=sent.at[k],
                recv_sem=landed.at[k], device_id=device, device_id_type=pl.DeviceIdType.MESH)
            copy.start()
            copies.append(copy)
        return copies

    def collect(copies, slots):
        for copy in copies:
            copy.wait()
        value = slots[0]
        for k in range(len(copies)):
            value = value + slots[k + 1]
        return value

    def gather_a(values):
        lines = [jnp.sum(value, axis=0, keepdims=True) for value in values]
        return gather(jnp.concatenate(lines + [zero8[0:4]], axis=0), sums_a, mates_a, asend, arecv)

    def gather_b(copies):
        return gather(collect(copies, sums_a), sums_b, mates_b, bsend, brecv)

    def finish_sums(copies):
        totals = jnp.broadcast_to(jnp.sum(collect(copies, sums_b), axis=1, keepdims=True), (8, 128))
        return [jnp.broadcast_to(totals[i : i + 1], (8, 128)) for i in range(4)]

    def write_pixels(v):
        for b in range(4):
            rows = slice(b * 128, b * 128 + 128)
            x = jnp.concatenate([whole[v, q, b * 128 + 8 : b * 128 + 136, :] for q in range(4)], axis=1)
            high, low = halves(x)
            pixels[v - 1, rows, :] = dot(high, perm[1]) + dot(low, perm[1])

    unfold(0)
    mix()
    own.wait()
    for copy in frame_moves:
        copy.wait()
    take_frames()
    fold(0, -1.0, no_sums, 0)
    settle(1, exchange(1))

    unfold(1)
    mix()

    def measure_w(rows, inside, old, out):
        rr = old[0] * old[0] + old[1] * old[1] + (old[2] * old[2] + old[3] * old[3])
        rw = old[0] * out[0] + old[1] * out[1] + (old[2] * out[2] + old[3] * out[3])
        return jnp.where(inside, rr, 0.0), rw

    rr, rw = fold(1, 1.0, measure_w, 2)
    rw = rw + outer_columns(vec[1, 4, 0:PACK, :] * vec[2, 4, 0:PACK, :])
    moves = exchange(2)
    write_pixels(1)
    settle(2, moves)

    unfold(2)
    mix()
    ww = jnp.zeros((8, 128), F32)
    for q in range(4):
        own_rows = whole[2, q, 8 : ROWS - 8, :]
        ww = ww + fewer_rows(own_rows * own_rows)
    wz = DAMP * ww
    for f in range(8):
        wz = wz + fewer_rows(feat[f] * acc[f])
    sums = gather_a((rr, rw, ww, wz))
    fold(2, 1.0, no_sums, 0)
    moves = exchange(3)
    write_pixels(2)
    sums = gather_b(sums)
    settle(3, moves)
    unfold(3, features=False)
    write_pixels(3)
    rr, rw, ww, wz = finish_sums(sums)
    alpha = rr / rw
    ss = alpha * alpha * ww - rr
    sw = rw - alpha * ww
    beta = ss / rr
    curve = (sw - alpha * (ww - alpha * wz)) + 2.0 * beta * sw + beta * beta * rw
    step = ss / curve
    c1, c2 = (alpha + step * (1.0 + beta))[0:1], (step * alpha)[0:1]
    c1, c2 = jnp.concatenate([c1] * 4, axis=1), jnp.concatenate([c2] * 4, axis=1)
    written = []
    for b in range(CLOSE):
        rows = slice(b * (TS // CLOSE), (b + 1) * (TS // CLOSE))
        r, w = pixels[0, rows, :], pixels[1, rows, :]
        pixels[2, rows, :] = r - c1 * w + c2 * pixels[2, rows, :]
        guess[rows, :] = guess[rows, :] + c1 * r - c2 * w
        for k, (source, target) in enumerate(((guess, solution_hbm), (pixels.at[2], residual_hbm))):
            written.append(pltpu.make_async_copy(source.at[rows], target.at[rows], stores.at[b, k]))
            written[-1].start()
    for store in written:
        store.wait()


def hand_over(solution_in, residual_in, solution_out, residual_out, held, loads, sems):
    arrays = ((solution_in, solution_out), (residual_in, residual_out))
    spots = [(b, k, slice(b * (TS // PARTS), (b + 1) * (TS // PARTS))) for b in range(PARTS) for k in range(2)]
    copies = []
    for b, k, rows in spots:
        copies.append(pltpu.make_async_copy(arrays[k][0].at[rows], held.at[k, rows], loads.at[b, k]))
        copies[-1].start()
    stores = []
    for copy, (b, k, rows) in zip(copies, spots):
        copy.wait()
        stores.append(pltpu.make_async_copy(held.at[k, rows], arrays[k][1].at[rows], sems.at[b, k]))
        stores[-1].start()
    for store in stores:
        store.wait()


def on_device(n_wide, n_narrow, frames, anchor, shift, guess):
    vmem, hbm = pl.BlockSpec(memory_space=pltpu.VMEM), pl.BlockSpec(memory_space=pltpu.HBM)
    image = jax.ShapeDtypeStruct((TS, TS), F32)
    dma = pltpu.SemaphoreType.DMA
    n_a, n_b = 2 * n_narrow, n_wide // 2
    made = pl.pallas_call(
        functools.partial(kernel, n_wide, n_narrow),
        out_shape=(image, image),
        in_specs=[hbm, vmem, vmem, hbm, hbm],
        out_specs=(hbm, hbm),
        scratch_shapes=[
            pltpu.VMEM((TS, TS), F32),
            pltpu.VMEM((3, TS, TS), F32),
            pltpu.VMEM((3, 128, 128), F32),
            pltpu.VMEM((4, 5, ROWS, 128), F32),
            pltpu.VMEM((4, 4, ROWS, 128), F32),
            pltpu.VMEM((ROWS, 128), F32),
            pltpu.VMEM((8, ROWS, 128), F32),
            pltpu.VMEM((8, ROWS, 128), F32),
            pltpu.VMEM((8, ROWS, 128), F32),
            pltpu.VMEM((24 * FS, 128), F32),
            pltpu.VMEM((2, 512, 512), BF16),
            pltpu.VMEM((3, 128, 384), BF16),
            pltpu.VMEM((3, 128, 256), BF16),
            pltpu.VMEM((4, 2, PACK, 128), F32),
            pltpu.VMEM((4, 2, 5, 16, 128), F32),
            pltpu.VMEM((4, 4, 16, 128), F32),
            pltpu.VMEM((n_a, 8, 128), F32),
            pltpu.VMEM((n_b, 8, 128), F32),
            dma((4, 8)), dma((4, 8)), dma((2,)), dma((2,)), dma((3,)), dma((CLOSE, 2)),
            dma((n_a,)), dma((n_a,)), dma((n_b,)), dma((n_b,)),
        ],
        compiler_params=pltpu.CompilerParams(
            collective_id=0, has_side_effects=True, vmem_limit_bytes=VMEM_BYTES),
    )(frames.reshape(8 * FS, FS), anchor, shift.transpose(0, 2, 1), guess, jnp.asarray(tables()))
    return pl.pallas_call(
        hand_over,
        out_shape=(image, image),
        in_specs=[hbm, hbm],
        out_specs=(hbm, hbm),
        scratch_shapes=[pltpu.VMEM((2, TS, TS), F32), dma((PARTS, 2)), dma((PARTS, 2))],
        compiler_params=pltpu.CompilerParams(vmem_limit_bytes=VMEM_BYTES),
    )(*made)


def solution(mesh):
    placed = (P("narrow", "wide", None, None), P("narrow", None), P("narrow", None, None), P("narrow", "wide"))
    return jax.shard_map(
        functools.partial(on_device, mesh.shape["wide"], mesh.shape["narrow"]),
        mesh=mesh,
        in_specs=placed,
        out_specs=(P("narrow", "wide"), P("narrow", "wide")),
        check_vma=False,
    )
```

```python
import functools

import jax
import jax.numpy as jnp
import numpy as np
from jax import lax
from jax.experimental import pallas as pl
from jax.experimental.pallas import tpu as pltpu
from jax.sharding import PartitionSpec as P

NSHIFT = 16
DAMP = 0.05
TS = 512
FS = 128
ROWS = TS + 16
TILES = ROWS // 8
GROUP = 11
PACK = GROUP * 8
F32 = jnp.float32
BF16 = jnp.bfloat16
UNFOLD = 528
FOLD = 528
MIX = 64
CLOSE = 4
PARTS = 4
VMEM_BYTES = 62 * 2**20
HIGHEST = lax.Precision.HIGHEST


def tables():
    fraction = np.arange(NSHIFT, dtype=np.float64) / NSHIFT
    offsets = np.arange(8, dtype=np.float64)[None, :] - 3.0 - fraction[:, None]
    lanczos = np.sinc(offsets) * np.sinc(offsets / 4.0)
    lanczos = lanczos / lanczos.sum(axis=1, keepdims=True)
    spread = np.arange(11)[None, :] - np.arange(8)[:, None]
    taps = lanczos @ np.where((spread >= 0) & (spread < 4), 0.25, 0.0)
    out = np.zeros((3, 128, 128), np.float64)
    for feature in range(8):
        weight = feature + 4 if feature < 4 else feature - 4
        for r in range(16):
            for second in range(2):
                if 0 <= r - 4 * second <= 10:
                    out[second, feature * 16 + r, :NSHIFT] = taps[:, r - 4 * second]
            out[2, feature * 16 + r, :NSHIFT] = lanczos[:, weight] * 0.25
    return out.astype(np.float32)


def halves(x):
    high = x.astype(BF16)
    return high, (x - high.astype(F32)).astype(BF16)


def dot(a, b):
    return jnp.dot(a, b, preferred_element_type=F32)


def exact_dot(a, b):
    return jnp.dot(a, b, precision=HIGHEST, preferred_element_type=F32)


def exact_dot_nt(a, b):
    return lax.dot_general(a, b, (((1,), (1,)), ((), ())), precision=HIGHEST, preferred_element_type=F32)


def kernel(
    n_wide, n_narrow,
    frames, anchor, shift, guess_hbm, table_hbm,
    solution_hbm, residual_hbm,
    guess, pixels, table, vec, whole, wide_edges, feat, acc, more, frb, perm, lhs, lhsb,
    from_side, from_row, from_corner, sums_a, sums_b,
    send, recv, fsend, frecv, loc, stores, asend, arecv, bsend, brecv,
):
    column = lax.axis_index("wide")
    row = lax.axis_index("narrow")
    left, right = lax.rem(column + n_wide - 1, n_wide), lax.rem(column + 1, n_wide)
    up, down = lax.rem(row + n_narrow - 1, n_narrow), lax.rem(row + 1, n_narrow)
    core, chip = lax.rem(column, 2), column // 2
    n_chip = n_wide // 2

    def at(w, n):
        return {"wide": w, "narrow": n}

    near = [at(right, row), at(left, row), at(column, down), at(column, up),
            at(right, down), at(left, down), at(right, up), at(left, up)]
    mates_a = [(row + (k // 2), core + (k % 2)) for k in range(1, 2 * n_narrow)]
    mates_a = [at(chip * 2 + lax.rem(c, 2), lax.rem(r, n_narrow)) for r, c in mates_a]
    mates_b = [at(lax.rem(chip + k, n_chip) * 2 + core, row) for k in range(1, n_chip)]

    barrier = pltpu.get_barrier_semaphore()
    everyone = near + mates_a + mates_b
    for device in everyone:
        pl.semaphore_signal(barrier, inc=1, device_id=device, device_id_type=pl.DeviceIdType.MESH)

    load_guess = pltpu.make_async_copy(guess_hbm, guess, loc.at[0])
    load_table = pltpu.make_async_copy(table_hbm, table, loc.at[1])
    own = pltpu.make_async_copy(frames, frb.at[8 * FS : 16 * FS], loc.at[2])
    load_guess.start()
    load_table.start()

    k_id = lax.broadcasted_iota(jnp.int32, (512, 128), 0)
    n_id = lax.broadcasted_iota(jnp.int32, (512, 128), 1)

    def permutation(which, target):
        for c in range(4):
            perm[which, :, c * 128 : c * 128 + 128] = jnp.where(n_id + 128 * c == target, 1.0, 0.0).astype(BF16)

    permutation(0, 128 * (k_id & 3) + (k_id >> 2))

    zero8 = jnp.zeros((8, 128), F32)

    def edge_masks(size):
        lane = lax.broadcasted_iota(jnp.int32, (size, 128), 1)
        return lane == 0, lane == 127

    def gather_edges(sides):
        packed = None
        for shift_by, part in sides:
            first, last = edge_masks(part.shape[0])
            term = pltpu.roll(jnp.where(first | last, part, 0.0), shift_by, axis=1)
            packed = term if packed is None else packed + term
        return packed

    def pack(v):
        packed = wide_edges[0:PACK, :]
        for g in range(1, 6):
            packed = packed + pltpu.roll(wide_edges[g * PACK : g * PACK + PACK, :], 16 * g, axis=1)
        vec[v, 4, 0:PACK, :] = packed
        vec[v, 4, 512:528, :] = packed[72:88]

    def unpack(v):
        for g in range(6):
            wide_edges[g * PACK : g * PACK + PACK, :] = pltpu.roll(vec[v, 4, 0:PACK, :], 127 - 16 * g, axis=1)

    for q in range(4):
        vec[0, q, 0:8, :] = zero8
        vec[0, q, ROWS - 8 : ROWS, :] = zero8
    wide_edges[0:8, :] = zero8
    wide_edges[ROWS - 8 : ROWS, :] = zero8

    def spread_guess(b):
        into = slice(b * 128 + 8, b * 128 + 136)
        high, low = halves(guess[b * 128 : b * 128 + 128, :])
        x = dot(high, perm[0]) + dot(low, perm[0])
        x = [x[:, q * 128 : q * 128 + 128] for q in range(4)]
        for q in range(4):
            vec[0, q, into, :] = x[q]
        wide_edges[into, :] = gather_edges([(4 * q + 1, x[q]) for q in range(4)])

    load_guess.wait()
    for b in range(4):
        spread_guess(b)
    pack(0)

    pl.semaphore_wait(barrier, len(everyone))

    def exchange(v):
        edges = vec.at[v, 4]
        parts = [
            (edges.at[0:PACK], from_side.at[v, 0]),
            (edges.at[0:PACK], from_side.at[v, 1]),
            (vec.at[v, :, 512:528], from_row.at[v, 0]),
            (vec.at[v, :, 0:16], from_row.at[v, 1]),
            (edges.at[72:88], from_corner.at[v, 0]),
            (edges.at[72:88], from_corner.at[v, 1]),
            (edges.at[0:16], from_corner.at[v, 2]),
            (edges.at[0:16], from_corner.at[v, 3]),
        ]
        copies = []
        for k in (4, 5, 6, 7, 0, 1, 2, 3):
            source, target = parts[k]
            copy = pltpu.make_async_remote_copy(
                src_ref=source, dst_ref=target, send_sem=send.at[v, k], recv_sem=recv.at[v, k],
                device_id=near[k], device_id_type=pl.DeviceIdType.MESH)
            copy.start()
            copies.append(copy)
        return copies

    def settle(v, copies):
        for copy in copies:
            copy.wait()
        has_left, has_right = column > 0, column < n_wide - 1
        has_up, has_down = row > 0, row < n_narrow - 1
        lane16 = lax.broadcasted_iota(jnp.int32, (16, 128), 1)
        sub16 = lax.broadcasted_iota(jnp.int32, (16, 128), 0)
        in_top, in_low = lane16 < 16, (lane16 >= 80) & (lane16 < 96)

        def with_rows(middle, above, below):
            above = jnp.where(in_top & has_up, pltpu.roll(above, 48, axis=1), 0.0)
            below = jnp.where(in_low & has_down, pltpu.roll(below, 80, axis=1), 0.0)
            return jnp.concatenate([middle[0:16] + above, middle[16:72], middle[72:88] + below], axis=0)

        mine = with_rows(vec[v, 4, 0:PACK, :], from_row[v, 0, 4], from_row[v, 1, 4])
        lefts = with_rows(from_side[v, 0], from_corner[v, 0], from_corner[v, 2])
        rights = with_rows(from_side[v, 1], from_corner[v, 1], from_corner[v, 3])
        kind = lax.rem(lax.broadcasted_iota(jnp.int32, (PACK, 128), 1), 4)
        other = jnp.where(kind == 1, pltpu.roll(lefts, 127, axis=1), 0.0)
        other = jnp.where(kind == 3, pltpu.roll(lefts, 3, axis=1), other)
        other = jnp.where(((kind == 1) | (kind == 3)) & has_left, other, 0.0)
        facing = jnp.where(kind == 0, pltpu.roll(rights, 125, axis=1), 0.0)
        facing = jnp.where(kind == 2, pltpu.roll(rights, 1, axis=1), facing)
        facing = jnp.where(((kind == 0) | (kind == 2)) & has_right, facing, 0.0)
        both = mine + other + facing
        both = jnp.where((kind == 3) & (column == 0), 0.0, both)
        both = jnp.where((kind == 2) & (column == n_wide - 1), 0.0, both)
        top = jnp.where(in_top & (sub16 < 8) & (row == 0), 0.0, both[0:16])
        low = jnp.where(in_low & (sub16 >= 8) & (row == n_narrow - 1), 0.0, both[72:88])
        vec[v, 4, 0:PACK, :] = jnp.concatenate([top, both[16:72], low], axis=0)
        for q in range(4):
            x = vec[v, q, 0:16, :] + jnp.where(has_up, from_row[v, 0, q], 0.0)
            vec[v, q, 0:16, :] = jnp.where((sub16 < 8) & (row == 0), 0.0, x)
            x = vec[v, q, 512:528, :] + jnp.where(has_down, from_row[v, 1, q], 0.0)
            vec[v, q, 512:528, :] = jnp.where((sub16 >= 8) & (row == n_narrow - 1), 0.0, x)

    moves = exchange(0)
    frame_moves = []
    for k, device in enumerate((at(right, row), at(left, row))):
        copy = pltpu.make_async_remote_copy(
            src_ref=frames, dst_ref=frb.at[16 * FS * k : 16 * FS * k + 8 * FS], send_sem=fsend.at[k],
            recv_sem=frecv.at[k], device_id=device, device_id_type=pl.DeviceIdType.MESH)
        copy.start()
        frame_moves.append(copy)
    own.start()
    permutation(1, 4 * (k_id & 127) + (k_id >> 7))

    n_frames = 8 * n_wide
    f_id = lax.broadcasted_iota(jnp.int32, (n_frames, 128), 0)
    slot = lax.broadcasted_iota(jnp.int32, (n_frames, 128), 1)
    slot = slot - (slot // 32) * 32
    wanted = lax.rem(slot + 8 * left, n_frames)
    pick = jnp.where((f_id == wanted) & (slot < 24), 1.0, 0.0).astype(BF16)
    looks = jnp.where(jnp.broadcast_to(anchor[...], (16, n_frames)) == column, 1.0, 0.0)
    code_row = lax.broadcasted_iota(jnp.int32, (16, n_frames), 0)
    codes = jnp.where(code_row == 0, looks, jnp.where(
        code_row == 1, jnp.broadcast_to(shift[0, 0:1, :], (16, n_frames)).astype(F32),
        jnp.broadcast_to(shift[0, 1:2, :], (16, n_frames)).astype(F32)))
    codes = dot(codes.astype(BF16), pick)
    used = codes[0:1]
    load_table.wait()
    lane128 = lax.broadcasted_iota(jnp.int32, (128, 128), 1)
    sub128 = lax.broadcasted_iota(jnp.int32, (128, 128), 0)
    one_a = jnp.where(jnp.broadcast_to(codes[1:2], (128, 128)).astype(jnp.int32) == sub128, 1.0, 0.0)
    one_b = jnp.where(jnp.broadcast_to(codes[2:3], (128, 128)).astype(jnp.int32) == sub128, 1.0, 0.0)
    second = lax.rem(lane128 // 32, 2) == 1
    tall = exact_dot(table[2], one_b) * jnp.where(
        second, exact_dot(table[1], one_a), exact_dot(table[0], one_a)) * used
    for which, keep in enumerate((second, lane128 >= 0, jnp.logical_not(second))):
        kept = jnp.where(keep, tall, 0.0)
        high, low = halves(kept)
        lhsb[which, :, 0:128] = high
        lhsb[which, :, 128:256] = jnp.where(lane128 < 64, low.astype(F32), 0.0).astype(BF16)
        half = jnp.where(lane128 < 64, kept, 0.0)
        high, low = halves(exact_dot_nt(half, half))
        lhs[which, :, 0:128] = high
        lhs[which, :, 128:256] = high
        lhs[which, :, 256:384] = low

    settle(0, moves)

    def unfold(v):
        unpack(v)

        def step(i, carry):
            rows = pl.ds(pl.multiple_of(i * UNFOLD, 8), UNFOLD)
            first, last = edge_masks(UNFOLD)
            packed = wide_edges[rows, :]
            raw = [vec[v, q, rows, :] for q in range(4)]
            mid, nxt, prv = [], [], []
            for q in range(4):
                spun = packed if q == 0 else pltpu.roll(packed, 128 - 4 * q, axis=1)
                x = jnp.where(first | last, spun, raw[q])
                mid.append(x)
                side = pltpu.roll(packed, 126 - 4 * q, axis=1)
                prv.append(jnp.where(first, side, pltpu.roll(x, 1, axis=1)))
                if q < 3:
                    nxt.append(jnp.where(last, side, pltpu.roll(x, 127, axis=1)))
            for q in range(4):
                whole[v, q, rows, :] = mid[q]
            m23, p23 = mid[2] + mid[3], prv[2] + prv[3]
            m123, p123 = mid[1] + m23, prv[1] + p23
            m01, n01 = mid[0] + mid[1], nxt[0] + nxt[1]
            out = [mid[0] + m123, m123 + nxt[0], m23 + n01, mid[3] + (n01 + nxt[2]),
                   prv[0] + p123, p123 + mid[0], p23 + m01, prv[3] + (m01 + mid[2])]
            for f in range(8):
                feat[f, rows, :] = out[f]
            return carry

        lax.fori_loop(0, ROWS // UNFOLD, step, 0)

    def join(parts):
        return parts[0] if len(parts) == 1 else jnp.concatenate(parts, axis=1)

    def blocks(starts):
        highs, lows = [], []
        for start in starts:
            pairs = [halves(feat[f, pl.ds(start, 16), :]) for f in range(8)]
            highs.append(jnp.concatenate([p[0] for p in pairs], axis=0))
            lows.append(jnp.concatenate([p[1] for p in pairs], axis=0))
        high, low = join(highs), join(lows)
        return jnp.concatenate([high, low, high], axis=0)

    def stack(outs, carry):
        done = []
        for out in outs:
            done.append([out[16 * f : 16 * f + 8] if carry is None else carry[f] + out[16 * f : 16 * f + 8]
                         for f in range(8)])
            carry = [out[16 * f + 8 : 16 * f + 16] for f in range(8)]
        return done, carry

    def sweep(results, save):
        def some(starts, kinds, carry):
            outs = []
            for k in range(0, len(starts), 2):
                outs.extend(results(starts[k : k + 2], kinds[k : k + 2]))
            done, carry = stack(outs, carry)
            for start, tiles in zip(starts, done):
                save(start, tiles)
            return tuple(carry)

        carry = some([8 * k for k in range(MIX)], [0] + [1] * (MIX - 1), None)

        def step(i, carry):
            start = pl.multiple_of(i * (8 * MIX), 8)
            return some([start + 8 * k for k in range(MIX)], [1] * MIX, carry)

        carry = lax.fori_loop(1, 64 // MIX, step, carry)
        carry = some([512], [2], carry)
        save(520, carry)

    def cut(out):
        return [out[:, 128 * k : 128 * k + 128] for k in range(out.shape[1] // 128)]

    def mix():
        def results(starts, kinds):
            if len(set(kinds)) > 1:
                return [dot(lhs[w], blocks([s])) for s, w in zip(starts, kinds)]
            return cut(dot(lhs[kinds[0]], blocks(starts)))

        def save(start, tiles):
            for f in range(8):
                acc[f, pl.ds(start, 8), :] = tiles[f]

        sweep(results, save)

    def take_frames():
        def pixels(start, kind):
            sample = start // 4
            rows = [0 if kind == 0 else sample - 1, FS - 1 if kind == 2 else sample]
            parts = []
            for i in rows:
                parts += [frb[pl.ds(i, 24, stride=FS), :], zero8]
            high, low = halves(jnp.concatenate(parts, axis=0))
            return jnp.concatenate([high, low], axis=0)

        def results(starts, kinds):
            if len(set(kinds)) > 1:
                return [results([s], [w])[0] for s, w in zip(starts, kinds)]
            both = join([pixels(s, w) for s, w in zip(starts, kinds)])
            return cut(dot(lhsb[kinds[0]], jnp.concatenate([both, both], axis=0)))

        def save(start, tiles):
            for f in range(8):
                more[f, pl.ds(start, 8), :] = tiles[f]

        sweep(results, save)

    def fold(v, sign, measure, counts):
        def step(i, sums):
            rows = pl.ds(pl.multiple_of(i * FOLD, 8), FOLD)
            first, last = edge_masks(FOLD)
            row_id = i * FOLD + lax.broadcasted_iota(jnp.int32, (FOLD, 128), 0)
            inside = (row_id >= 8) & (row_id < ROWS - 8)
            damp = jnp.where(inside, DAMP, 0.0)
            cur = [acc[q, rows, :] for q in range(4)]
            pre = [acc[4 + q, rows, :] for q in range(4)]
            if v == 0:
                cur = [c - more[q, rows, :] for q, c in enumerate(cur)]
                pre = [p - more[4 + q, rows, :] for q, p in enumerate(pre)]
            old = [whole[v, q, rows, :] for q in range(4)]
            rolled = [pltpu.roll(x, 127, axis=1) for x in pre]
            here = [c + jnp.where(last, 0.0, p) for c, p in zip(cur, rolled)]
            back = [p + jnp.where(last, 0.0, c) for c, p in zip(cur, rolled)]
            h01 = here[0] + here[1]
            h012 = h01 + here[2]
            k23 = back[2] + back[3]
            out = [here[0] + pltpu.roll(back[1] + k23, 1, axis=1), h01 + pltpu.roll(k23, 1, axis=1),
                   h012 + pltpu.roll(back[3], 1, axis=1), h012 + here[3]]
            h23 = here[2] + here[3]
            r01 = pre[0] + pre[1]
            r012 = r01 + pre[2]
            over = [jnp.where(first, pre[0], here[1] + h23), jnp.where(first, r01, h23),
                    jnp.where(first, r012, here[3]), jnp.where(first, r012 + pre[3], 0.0)]
            out = [o + damp * x for o, x in zip(out, old)]
            if sign < 0:
                out, over = [-o for o in out], [-o for o in over]
            packed = gather_edges([(4 * q + 1, out[q]) for q in range(4)] + [(4 * q + 3, over[q]) for q in range(4)])
            more_sums = measure(rows, inside, old, out)
            for q in range(4):
                vec[v + 1, q, rows, :] = out[q]
            wide_edges[rows, :] = packed
            return tuple(s + m for s, m in zip(sums, more_sums))

        sums = lax.fori_loop(0, ROWS // FOLD, step, (jnp.zeros((FOLD, 128), F32),) * counts)
        pack(v + 1)
        return [fewer_rows(s) for s in sums]

    def fewer_rows(x):
        total = x[0:8]
        for k in range(8, x.shape[0], 8):
            total = total + x[k : k + 8]
        return total

    def no_sums(rows, inside, old, out):
        return ()

    def outer_columns(product):
        kind = lax.broadcasted_iota(jnp.int32, (PACK, 128), 1) & 3
        return fewer_rows(jnp.where(kind >= 2, product, 0.0))

    def gather(value, slots, mates, sent, landed):
        slots[0] = value
        copies = []
        for k, device in enumerate(mates):
            copy = pltpu.make_async_remote_copy(
                src_ref=slots.at[0], dst_ref=slots.at[k + 1], send_sem=sent.at[k],
                recv_sem=landed.at[k], device_id=device, device_id_type=pl.DeviceIdType.MESH)
            copy.start()
            copies.append(copy)
        return copies

    def collect(copies, slots):
        for copy in copies:
            copy.wait()
        value = slots[0]
        for k in range(len(copies)):
            value = value + slots[k + 1]
        return value

    def gather_a(values):
        lines = [jnp.sum(value, axis=0, keepdims=True) for value in values]
        return gather(jnp.concatenate(lines + [zero8[0:4]], axis=0), sums_a, mates_a, asend, arecv)

    def gather_b(copies):
        return gather(collect(copies, sums_a), sums_b, mates_b, bsend, brecv)

    def finish_sums(copies):
        totals = jnp.broadcast_to(jnp.sum(collect(copies, sums_b), axis=1, keepdims=True), (8, 128))
        return [jnp.broadcast_to(totals[i : i + 1], (8, 128)) for i in range(4)]

    def write_pixels(source, v, starts=(0, 128, 256, 384), size=128):
        for start in starts:
            x = jnp.concatenate([source[v, q, start + 8 : start + 8 + size, :] for q in range(4)], axis=1)
            high, low = halves(x)
            pixels[v - 1, start : start + size, :] = dot(high, perm[1]) + dot(low, perm[1])

    def patch_pixels(v):
        write_pixels(vec, v, (0, TS - 16), 16)
        edges = [vec[v, 4, 0:PACK, :]]
        edges += [pltpu.roll(edges[0], 128 - 16 * g, axis=1) for g in range(1, 6)]
        high, low = halves(jnp.concatenate(edges, axis=0))
        k_id = lax.broadcasted_iota(jnp.int32, (128, 256), 0)
        n_id = lax.broadcasted_iota(jnp.int32, (128, 256), 1)
        left_one = (n_id < 4) & (k_id == 4 * n_id + 1)
        right_one = (n_id >= 252) & (k_id == 4 * (n_id - 252))
        place = jnp.where(left_one | right_one, 1.0, 0.0).astype(BF16)
        outer = (dot(high, place) + dot(low, place))[8 : ROWS - 8]
        lane = lax.broadcasted_iota(jnp.int32, (TS, 128), 1)
        pixels[v - 1, :, 0:128] = jnp.where(lane < 4, outer[:, 0:128], pixels[v - 1, :, 0:128])
        pixels[v - 1, :, 384:512] = jnp.where(lane >= 124, outer[:, 128:256], pixels[v - 1, :, 384:512])

    unfold(0)
    mix()
    own.wait()
    for copy in frame_moves:
        copy.wait()
    take_frames()
    fold(0, -1.0, no_sums, 0)
    settle(1, exchange(1))

    unfold(1)
    mix()

    def measure_w(rows, inside, old, out):
        rr = old[0] * old[0] + old[1] * old[1] + (old[2] * old[2] + old[3] * old[3])
        rw = old[0] * out[0] + old[1] * out[1] + (old[2] * out[2] + old[3] * out[3])
        return jnp.where(inside, rr, 0.0), rw

    rr, rw = fold(1, 1.0, measure_w, 2)
    rw = rw + outer_columns(vec[1, 4, 0:PACK, :] * vec[2, 4, 0:PACK, :])
    moves = exchange(2)
    write_pixels(whole, 1)
    settle(2, moves)

    unfold(2)
    mix()
    ww = jnp.zeros((8, 128), F32)
    for q in range(4):
        own_rows = whole[2, q, 8 : ROWS - 8, :]
        ww = ww + fewer_rows(own_rows * own_rows)
    wz = DAMP * ww
    for f in range(8):
        wz = wz + fewer_rows(feat[f] * acc[f])
    sums = gather_a((rr, rw, ww, wz))
    fold(2, 1.0, no_sums, 0)
    moves = exchange(3)
    write_pixels(whole, 2)
    write_pixels(vec, 3)
    sums = gather_b(sums)
    settle(3, moves)
    patch_pixels(3)
    rr, rw, ww, wz = finish_sums(sums)
    alpha = rr / rw
    ss = alpha * alpha * ww - rr
    sw = rw - alpha * ww
    beta = ss / rr
    curve = (sw - alpha * (ww - alpha * wz)) + 2.0 * beta * sw + beta * beta * rw
    step = ss / curve
    c1, c2 = (alpha + step * (1.0 + beta))[0:1], (step * alpha)[0:1]
    c1, c2 = jnp.concatenate([c1] * 4, axis=1), jnp.concatenate([c2] * 4, axis=1)
    written = []
    for b in range(CLOSE):
        rows = slice(b * (TS // CLOSE), (b + 1) * (TS // CLOSE))
        r, w = pixels[0, rows, :], pixels[1, rows, :]
        pixels[2, rows, :] = r - c1 * w + c2 * pixels[2, rows, :]
        guess[rows, :] = guess[rows, :] + c1 * r - c2 * w
        for k, (source, target) in enumerate(((guess, solution_hbm), (pixels.at[2], residual_hbm))):
            written.append(pltpu.make_async_copy(source.at[rows], target.at[rows], stores.at[b, k]))
            written[-1].start()
    for store in written:
        store.wait()


def hand_over(solution_in, residual_in, solution_out, residual_out, held, loads, sems):
    arrays = ((solution_in, solution_out), (residual_in, residual_out))
    spots = [(b, k, slice(b * (TS // PARTS), (b + 1) * (TS // PARTS))) for b in range(PARTS) for k in range(2)]
    copies = []
    for b, k, rows in spots:
        copies.append(pltpu.make_async_copy(arrays[k][0].at[rows], held.at[k, rows], loads.at[b, k]))
        copies[-1].start()
    stores = []
    for copy, (b, k, rows) in zip(copies, spots):
        copy.wait()
        stores.append(pltpu.make_async_copy(held.at[k, rows], arrays[k][1].at[rows], sems.at[b, k]))
        stores[-1].start()
    for store in stores:
        store.wait()


def on_device(n_wide, n_narrow, frames, anchor, shift, guess):
    vmem, hbm = pl.BlockSpec(memory_space=pltpu.VMEM), pl.BlockSpec(memory_space=pltpu.HBM)
    image = jax.ShapeDtypeStruct((TS, TS), F32)
    dma = pltpu.SemaphoreType.DMA
    n_a, n_b = 2 * n_narrow, n_wide // 2
    made = pl.pallas_call(
        functools.partial(kernel, n_wide, n_narrow),
        out_shape=(image, image),
        in_specs=[hbm, vmem, vmem, hbm, hbm],
        out_specs=(hbm, hbm),
        scratch_shapes=[
            pltpu.VMEM((TS, TS), F32),
            pltpu.VMEM((3, TS, TS), F32),
            pltpu.VMEM((3, 128, 128), F32),
            pltpu.VMEM((4, 5, ROWS, 128), F32),
            pltpu.VMEM((4, 4, ROWS, 128), F32),
            pltpu.VMEM((ROWS, 128), F32),
            pltpu.VMEM((8, ROWS, 128), F32),
            pltpu.VMEM((8, ROWS, 128), F32),
            pltpu.VMEM((8, ROWS, 128), F32),
            pltpu.VMEM((24 * FS, 128), F32),
            pltpu.VMEM((2, 512, 512), BF16),
            pltpu.VMEM((3, 128, 384), BF16),
            pltpu.VMEM((3, 128, 256), BF16),
            pltpu.VMEM((4, 2, PACK, 128), F32),
            pltpu.VMEM((4, 2, 5, 16, 128), F32),
            pltpu.VMEM((4, 4, 16, 128), F32),
            pltpu.VMEM((n_a, 8, 128), F32),
            pltpu.VMEM((n_b, 8, 128), F32),
            dma((4, 8)), dma((4, 8)), dma((2,)), dma((2,)), dma((3,)), dma((CLOSE, 2)),
            dma((n_a,)), dma((n_a,)), dma((n_b,)), dma((n_b,)),
        ],
        compiler_params=pltpu.CompilerParams(
            collective_id=0, has_side_effects=True, vmem_limit_bytes=VMEM_BYTES),
    )(frames.reshape(8 * FS, FS), anchor, shift.transpose(0, 2, 1), guess, jnp.asarray(tables()))
    return pl.pallas_call(
        hand_over,
        out_shape=(image, image),
        in_specs=[hbm, hbm],
        out_specs=(hbm, hbm),
        scratch_shapes=[pltpu.VMEM((2, TS, TS), F32), dma((PARTS, 2)), dma((PARTS, 2))],
        compiler_params=pltpu.CompilerParams(vmem_limit_bytes=VMEM_BYTES),
    )(*made)


def solution(mesh):
    placed = (P("narrow", "wide", None, None), P("narrow", None), P("narrow", None, None), P("narrow", "wide"))
    return jax.shard_map(
        functools.partial(on_device, mesh.shape["wide"], mesh.shape["narrow"]),
        mesh=mesh,
        in_specs=placed,
        out_specs=(P("narrow", "wide"), P("narrow", "wide")),
        check_vma=False,
    )
```

```python
import functools

import jax
import jax.numpy as jnp
import numpy as np
from jax import lax
from jax.experimental import pallas as pl
from jax.experimental.pallas import tpu as pltpu
from jax.sharding import PartitionSpec as P

NSHIFT = 16
DAMP = 0.05
TS = 512
FS = 128
ROWS = TS + 16
TILES = ROWS // 8
GROUP = 11
PACK = GROUP * 8
F32 = jnp.float32
BF16 = jnp.bfloat16
UNFOLD = 528
FOLD = 528
MIX = 64
CLOSE = 4
PARTS = 4
VMEM_BYTES = 62 * 2**20
HIGHEST = lax.Precision.HIGHEST


def tables():
    fraction = np.arange(NSHIFT, dtype=np.float64) / NSHIFT
    offsets = np.arange(8, dtype=np.float64)[None, :] - 3.0 - fraction[:, None]
    lanczos = np.sinc(offsets) * np.sinc(offsets / 4.0)
    lanczos = lanczos / lanczos.sum(axis=1, keepdims=True)
    spread = np.arange(11)[None, :] - np.arange(8)[:, None]
    taps = lanczos @ np.where((spread >= 0) & (spread < 4), 0.25, 0.0)
    out = np.zeros((3, 128, 128), np.float64)
    for feature in range(8):
        weight = feature + 4 if feature < 4 else feature - 4
        for r in range(16):
            for second in range(2):
                if 0 <= r - 4 * second <= 10:
                    out[second, feature * 16 + r, :NSHIFT] = taps[:, r - 4 * second]
            out[2, feature * 16 + r, :NSHIFT] = lanczos[:, weight] * 0.25
    return out.astype(np.float32)


def halves(x):
    high = x.astype(BF16)
    return high, (x - high.astype(F32)).astype(BF16)


def dot(a, b):
    return jnp.dot(a, b, preferred_element_type=F32)


def exact_dot(a, b):
    return jnp.dot(a, b, precision=HIGHEST, preferred_element_type=F32)


def exact_dot_nt(a, b):
    return lax.dot_general(a, b, (((1,), (1,)), ((), ())), precision=HIGHEST, preferred_element_type=F32)


def kernel(
    n_wide, n_narrow,
    frames, anchor, shift, guess_hbm, table_hbm,
    solution_hbm, residual_hbm,
    guess, pixels, table, vec, whole, wide_edges, feat, acc, more, frb, perm, lhs, lhsb,
    from_side, from_row, from_corner, sums_a, sums_b,
    send, recv, fsend, frecv, loc, stores, asend, arecv, bsend, brecv,
):
    column = lax.axis_index("wide")
    row = lax.axis_index("narrow")
    left, right = lax.rem(column + n_wide - 1, n_wide), lax.rem(column + 1, n_wide)
    up, down = lax.rem(row + n_narrow - 1, n_narrow), lax.rem(row + 1, n_narrow)

    def at(w, n):
        return {"wide": w, "narrow": n}

    near = [at(right, row), at(left, row), at(column, down), at(column, up),
            at(right, down), at(left, down), at(right, up), at(left, up)]
    n_far = n_wide // 8
    mates_a = [at(lax.rem(column + 8 * (k % n_far), n_wide), lax.rem(row + k // n_far, n_narrow))
               for k in range(1, n_narrow * n_far)]
    mates_b = [at((column // 8) * 8 + lax.rem(column + k, 8), row) for k in range(1, 8)]

    barrier = pltpu.get_barrier_semaphore()
    everyone = near + mates_a + mates_b
    for device in everyone:
        pl.semaphore_signal(barrier, inc=1, device_id=device, device_id_type=pl.DeviceIdType.MESH)

    load_guess = pltpu.make_async_copy(guess_hbm, guess, loc.at[0])
    load_table = pltpu.make_async_copy(table_hbm, table, loc.at[1])
    own = pltpu.make_async_copy(frames, frb.at[8 * FS : 16 * FS], loc.at[2])
    load_guess.start()
    load_table.start()

    k_id = lax.broadcasted_iota(jnp.int32, (512, 128), 0)
    n_id = lax.broadcasted_iota(jnp.int32, (512, 128), 1)

    def permutation(which, target):
        for c in range(4):
            perm[which, :, c * 128 : c * 128 + 128] = jnp.where(n_id + 128 * c == target, 1.0, 0.0).astype(BF16)

    permutation(0, 128 * (k_id & 3) + (k_id >> 2))

    zero8 = jnp.zeros((8, 128), F32)

    def edge_masks(size):
        lane = lax.broadcasted_iota(jnp.int32, (size, 128), 1)
        return lane == 0, lane == 127

    def gather_edges(sides):
        packed = None
        for shift_by, part in sides:
            first, last = edge_masks(part.shape[0])
            term = pltpu.roll(jnp.where(first | last, part, 0.0), shift_by, axis=1)
            packed = term if packed is None else packed + term
        return packed

    def pack(v):
        packed = wide_edges[0:PACK, :]
        for g in range(1, 6):
            packed = packed + pltpu.roll(wide_edges[g * PACK : g * PACK + PACK, :], 16 * g, axis=1)
        vec[v, 4, 0:PACK, :] = packed
        vec[v, 4, 512:528, :] = packed[72:88]

    def unpack(v):
        for g in range(6):
            wide_edges[g * PACK : g * PACK + PACK, :] = pltpu.roll(vec[v, 4, 0:PACK, :], 127 - 16 * g, axis=1)

    for q in range(4):
        vec[0, q, 0:8, :] = zero8
        vec[0, q, ROWS - 8 : ROWS, :] = zero8
    wide_edges[0:8, :] = zero8
    wide_edges[ROWS - 8 : ROWS, :] = zero8

    def spread_guess(b):
        into = slice(b * 128 + 8, b * 128 + 136)
        high, low = halves(guess[b * 128 : b * 128 + 128, :])
        x = dot(high, perm[0]) + dot(low, perm[0])
        x = [x[:, q * 128 : q * 128 + 128] for q in range(4)]
        for q in range(4):
            vec[0, q, into, :] = x[q]
        wide_edges[into, :] = gather_edges([(4 * q + 1, x[q]) for q in range(4)])

    load_guess.wait()
    for b in range(4):
        spread_guess(b)
    pack(0)

    pl.semaphore_wait(barrier, len(everyone))

    def exchange(v):
        edges = vec.at[v, 4]
        parts = [
            (edges.at[0:PACK], from_side.at[v, 0]),
            (edges.at[0:PACK], from_side.at[v, 1]),
            (vec.at[v, :, 512:528], from_row.at[v, 0]),
            (vec.at[v, :, 0:16], from_row.at[v, 1]),
            (edges.at[72:88], from_corner.at[v, 0]),
            (edges.at[72:88], from_corner.at[v, 1]),
            (edges.at[0:16], from_corner.at[v, 2]),
            (edges.at[0:16], from_corner.at[v, 3]),
        ]
        copies = []
        for k in (4, 5, 6, 7, 0, 1, 2, 3):
            source, target = parts[k]
            copy = pltpu.make_async_remote_copy(
                src_ref=source, dst_ref=target, send_sem=send.at[v, k], recv_sem=recv.at[v, k],
                device_id=near[k], device_id_type=pl.DeviceIdType.MESH)
            copy.start()
            copies.append(copy)
        return copies

    def settle(v, copies):
        for copy in copies:
            copy.wait()
        has_left, has_right = column > 0, column < n_wide - 1
        has_up, has_down = row > 0, row < n_narrow - 1
        lane16 = lax.broadcasted_iota(jnp.int32, (16, 128), 1)
        sub16 = lax.broadcasted_iota(jnp.int32, (16, 128), 0)
        in_top, in_low = lane16 < 16, (lane16 >= 80) & (lane16 < 96)

        def with_rows(middle, above, below):
            above = jnp.where(in_top & has_up, pltpu.roll(above, 48, axis=1), 0.0)
            below = jnp.where(in_low & has_down, pltpu.roll(below, 80, axis=1), 0.0)
            return jnp.concatenate([middle[0:16] + above, middle[16:72], middle[72:88] + below], axis=0)

        mine = with_rows(vec[v, 4, 0:PACK, :], from_row[v, 0, 4], from_row[v, 1, 4])
        lefts = with_rows(from_side[v, 0], from_corner[v, 0], from_corner[v, 2])
        rights = with_rows(from_side[v, 1], from_corner[v, 1], from_corner[v, 3])
        kind = lax.rem(lax.broadcasted_iota(jnp.int32, (PACK, 128), 1), 4)
        other = jnp.where(kind == 1, pltpu.roll(lefts, 127, axis=1), 0.0)
        other = jnp.where(kind == 3, pltpu.roll(lefts, 3, axis=1), other)
        other = jnp.where(((kind == 1) | (kind == 3)) & has_left, other, 0.0)
        facing = jnp.where(kind == 0, pltpu.roll(rights, 125, axis=1), 0.0)
        facing = jnp.where(kind == 2, pltpu.roll(rights, 1, axis=1), facing)
        facing = jnp.where(((kind == 0) | (kind == 2)) & has_right, facing, 0.0)
        both = mine + other + facing
        both = jnp.where((kind == 3) & (column == 0), 0.0, both)
        both = jnp.where((kind == 2) & (column == n_wide - 1), 0.0, both)
        top = jnp.where(in_top & (sub16 < 8) & (row == 0), 0.0, both[0:16])
        low = jnp.where(in_low & (sub16 >= 8) & (row == n_narrow - 1), 0.0, both[72:88])
        vec[v, 4, 0:PACK, :] = jnp.concatenate([top, both[16:72], low], axis=0)
        for q in range(4):
            x = vec[v, q, 0:16, :] + jnp.where(has_up, from_row[v, 0, q], 0.0)
            vec[v, q, 0:16, :] = jnp.where((sub16 < 8) & (row == 0), 0.0, x)
            x = vec[v, q, 512:528, :] + jnp.where(has_down, from_row[v, 1, q], 0.0)
            vec[v, q, 512:528, :] = jnp.where((sub16 >= 8) & (row == n_narrow - 1), 0.0, x)

    moves = exchange(0)
    frame_moves = []
    for k, device in enumerate((at(right, row), at(left, row))):
        copy = pltpu.make_async_remote_copy(
            src_ref=frames, dst_ref=frb.at[16 * FS * k : 16 * FS * k + 8 * FS], send_sem=fsend.at[k],
            recv_sem=frecv.at[k], device_id=device, device_id_type=pl.DeviceIdType.MESH)
        copy.start()
        frame_moves.append(copy)
    own.start()
    permutation(1, 4 * (k_id & 127) + (k_id >> 7))

    n_frames = 8 * n_wide
    f_id = lax.broadcasted_iota(jnp.int32, (n_frames, 128), 0)
    slot = lax.broadcasted_iota(jnp.int32, (n_frames, 128), 1)
    slot = slot - (slot // 32) * 32
    wanted = lax.rem(slot + 8 * left, n_frames)
    pick = jnp.where((f_id == wanted) & (slot < 24), 1.0, 0.0).astype(BF16)
    looks = jnp.where(jnp.broadcast_to(anchor[...], (16, n_frames)) == column, 1.0, 0.0)
    code_row = lax.broadcasted_iota(jnp.int32, (16, n_frames), 0)
    codes = jnp.where(code_row == 0, looks, jnp.where(
        code_row == 1, jnp.broadcast_to(shift[0, 0:1, :], (16, n_frames)).astype(F32),
        jnp.broadcast_to(shift[0, 1:2, :], (16, n_frames)).astype(F32)))
    codes = dot(codes.astype(BF16), pick)
    used = codes[0:1]
    load_table.wait()
    lane128 = lax.broadcasted_iota(jnp.int32, (128, 128), 1)
    sub128 = lax.broadcasted_iota(jnp.int32, (128, 128), 0)
    one_a = jnp.where(jnp.broadcast_to(codes[1:2], (128, 128)).astype(jnp.int32) == sub128, 1.0, 0.0)
    one_b = jnp.where(jnp.broadcast_to(codes[2:3], (128, 128)).astype(jnp.int32) == sub128, 1.0, 0.0)
    second = lax.rem(lane128 // 32, 2) == 1
    tall = exact_dot(table[2], one_b) * jnp.where(
        second, exact_dot(table[1], one_a), exact_dot(table[0], one_a)) * used
    for which, keep in enumerate((second, lane128 >= 0, jnp.logical_not(second))):
        kept = jnp.where(keep, tall, 0.0)
        high, low = halves(kept)
        lhsb[which, :, 0:128] = high
        lhsb[which, :, 128:256] = jnp.where(lane128 < 64, low.astype(F32), 0.0).astype(BF16)
        half = jnp.where(lane128 < 64, kept, 0.0)
        high, low = halves(exact_dot_nt(half, half))
        lhs[which, :, 0:128] = high
        lhs[which, :, 128:256] = high
        lhs[which, :, 256:384] = low

    settle(0, moves)

    def unfold(v):
        unpack(v)

        def step(i, carry):
            rows = pl.ds(pl.multiple_of(i * UNFOLD, 8), UNFOLD)
            first, last = edge_masks(UNFOLD)
            packed = wide_edges[rows, :]
            raw = [vec[v, q, rows, :] for q in range(4)]
            mid, nxt, prv = [], [], []
            for q in range(4):
                spun = packed if q == 0 else pltpu.roll(packed, 128 - 4 * q, axis=1)
                x = jnp.where(first | last, spun, raw[q])
                mid.append(x)
                side = pltpu.roll(packed, 126 - 4 * q, axis=1)
                prv.append(jnp.where(first, side, pltpu.roll(x, 1, axis=1)))
                if q < 3:
                    nxt.append(jnp.where(last, side, pltpu.roll(x, 127, axis=1)))
            for q in range(4):
                whole[v, q, rows, :] = mid[q]
            m23, p23 = mid[2] + mid[3], prv[2] + prv[3]
            m123, p123 = mid[1] + m23, prv[1] + p23
            m01, n01 = mid[0] + mid[1], nxt[0] + nxt[1]
            out = [mid[0] + m123, m123 + nxt[0], m23 + n01, mid[3] + (n01 + nxt[2]),
                   prv[0] + p123, p123 + mid[0], p23 + m01, prv[3] + (m01 + mid[2])]
            for f in range(8):
                feat[f, rows, :] = out[f]
            return carry

        lax.fori_loop(0, ROWS // UNFOLD, step, 0)

    def join(parts):
        return parts[0] if len(parts) == 1 else jnp.concatenate(parts, axis=1)

    def blocks(starts):
        highs, lows = [], []
        for start in starts:
            pairs = [halves(feat[f, pl.ds(start, 16), :]) for f in range(8)]
            highs.append(jnp.concatenate([p[0] for p in pairs], axis=0))
            lows.append(jnp.concatenate([p[1] for p in pairs], axis=0))
        high, low = join(highs), join(lows)
        return jnp.concatenate([high, low, high], axis=0)

    def stack(outs, carry):
        done = []
        for out in outs:
            done.append([out[16 * f : 16 * f + 8] if carry is None else carry[f] + out[16 * f : 16 * f + 8]
                         for f in range(8)])
            carry = [out[16 * f + 8 : 16 * f + 16] for f in range(8)]
        return done, carry

    def sweep(results, save):
        def some(starts, kinds, carry):
            outs = []
            for k in range(0, len(starts), 2):
                outs.extend(results(starts[k : k + 2], kinds[k : k + 2]))
            done, carry = stack(outs, carry)
            for start, tiles in zip(starts, done):
                save(start, tiles)
            return tuple(carry)

        carry = some([8 * k for k in range(MIX)], [0] + [1] * (MIX - 1), None)

        def step(i, carry):
            start = pl.multiple_of(i * (8 * MIX), 8)
            return some([start + 8 * k for k in range(MIX)], [1] * MIX, carry)

        carry = lax.fori_loop(1, 64 // MIX, step, carry)
        carry = some([512], [2], carry)
        save(520, carry)

    def cut(out):
        return [out[:, 128 * k : 128 * k + 128] for k in range(out.shape[1] // 128)]

    def mix():
        def results(starts, kinds):
            if len(set(kinds)) > 1:
                return [dot(lhs[w], blocks([s])) for s, w in zip(starts, kinds)]
            return cut(dot(lhs[kinds[0]], blocks(starts)))

        def save(start, tiles):
            for f in range(8):
                acc[f, pl.ds(start, 8), :] = tiles[f]

        sweep(results, save)

    def take_frames():
        def pixels(start, kind):
            sample = start // 4
            rows = [0 if kind == 0 else sample - 1, FS - 1 if kind == 2 else sample]
            parts = []
            for i in rows:
                parts += [frb[pl.ds(i, 24, stride=FS), :], zero8]
            high, low = halves(jnp.concatenate(parts, axis=0))
            return jnp.concatenate([high, low], axis=0)

        def results(starts, kinds):
            if len(set(kinds)) > 1:
                return [results([s], [w])[0] for s, w in zip(starts, kinds)]
            both = join([pixels(s, w) for s, w in zip(starts, kinds)])
            return cut(dot(lhsb[kinds[0]], jnp.concatenate([both, both], axis=0)))

        def save(start, tiles):
            for f in range(8):
                more[f, pl.ds(start, 8), :] = tiles[f]

        sweep(results, save)

    def fold(v, sign, measure, counts):
        def step(i, sums):
            rows = pl.ds(pl.multiple_of(i * FOLD, 8), FOLD)
            first, last = edge_masks(FOLD)
            row_id = i * FOLD + lax.broadcasted_iota(jnp.int32, (FOLD, 128), 0)
            inside = (row_id >= 8) & (row_id < ROWS - 8)
            damp = jnp.where(inside, DAMP, 0.0)
            cur = [acc[q, rows, :] for q in range(4)]
            pre = [acc[4 + q, rows, :] for q in range(4)]
            if v == 0:
                cur = [c - more[q, rows, :] for q, c in enumerate(cur)]
                pre = [p - more[4 + q, rows, :] for q, p in enumerate(pre)]
            old = [whole[v, q, rows, :] for q in range(4)]
            rolled = [pltpu.roll(x, 127, axis=1) for x in pre]
            here = [c + jnp.where(last, 0.0, p) for c, p in zip(cur, rolled)]
            back = [p + jnp.where(last, 0.0, c) for c, p in zip(cur, rolled)]
            h01 = here[0] + here[1]
            h012 = h01 + here[2]
            k23 = back[2] + back[3]
            out = [here[0] + pltpu.roll(back[1] + k23, 1, axis=1), h01 + pltpu.roll(k23, 1, axis=1),
                   h012 + pltpu.roll(back[3], 1, axis=1), h012 + here[3]]
            h23 = here[2] + here[3]
            r01 = pre[0] + pre[1]
            r012 = r01 + pre[2]
            over = [jnp.where(first, pre[0], here[1] + h23), jnp.where(first, r01, h23),
                    jnp.where(first, r012, here[3]), jnp.where(first, r012 + pre[3], 0.0)]
            out = [o + damp * x for o, x in zip(out, old)]
            if sign < 0:
                out, over = [-o for o in out], [-o for o in over]
            packed = gather_edges([(4 * q + 1, out[q]) for q in range(4)] + [(4 * q + 3, over[q]) for q in range(4)])
            more_sums = measure(rows, inside, old, out)
            for q in range(4):
                vec[v + 1, q, rows, :] = out[q]
            wide_edges[rows, :] = packed
            return tuple(s + m for s, m in zip(sums, more_sums))

        sums = lax.fori_loop(0, ROWS // FOLD, step, (jnp.zeros((FOLD, 128), F32),) * counts)
        pack(v + 1)
        return [fewer_rows(s) for s in sums]

    def fewer_rows(x):
        total = x[0:8]
        for k in range(8, x.shape[0], 8):
            total = total + x[k : k + 8]
        return total

    def no_sums(rows, inside, old, out):
        return ()

    def outer_columns(product):
        kind = lax.broadcasted_iota(jnp.int32, (PACK, 128), 1) & 3
        return fewer_rows(jnp.where(kind >= 2, product, 0.0))

    def gather(value, slots, mates, sent, landed):
        slots[0] = value
        copies = []
        for k, device in enumerate(mates):
            copy = pltpu.make_async_remote_copy(
                src_ref=slots.at[0], dst_ref=slots.at[k + 1], send_sem=sent.at[k],
                recv_sem=landed.at[k], device_id=device, device_id_type=pl.DeviceIdType.MESH)
            copy.start()
            copies.append(copy)
        return copies

    def collect(copies, slots):
        for copy in copies:
            copy.wait()
        value = slots[0]
        for k in range(len(copies)):
            value = value + slots[k + 1]
        return value

    def gather_a(values):
        lines = [jnp.sum(value, axis=0, keepdims=True) for value in values]
        return gather(jnp.concatenate(lines + [zero8[0:4]], axis=0), sums_a, mates_a, asend, arecv)

    def gather_b(copies):
        return gather(collect(copies, sums_a), sums_b, mates_b, bsend, brecv)

    def finish_sums(copies):
        totals = jnp.broadcast_to(jnp.sum(collect(copies, sums_b), axis=1, keepdims=True), (8, 128))
        return [jnp.broadcast_to(totals[i : i + 1], (8, 128)) for i in range(4)]

    def write_pixels(source, v, starts=(0, 128, 256, 384), size=128):
        for start in starts:
            x = jnp.concatenate([source[v, q, start + 8 : start + 8 + size, :] for q in range(4)], axis=1)
            high, low = halves(x)
            pixels[v - 1, start : start + size, :] = dot(high, perm[1]) + dot(low, perm[1])

    def patch_pixels(v):
        write_pixels(vec, v, (0, TS - 16), 16)
        edges = [vec[v, 4, 0:PACK, :]]
        edges += [pltpu.roll(edges[0], 128 - 16 * g, axis=1) for g in range(1, 6)]
        high, low = halves(jnp.concatenate(edges, axis=0))
        k_id = lax.broadcasted_iota(jnp.int32, (128, 256), 0)
        n_id = lax.broadcasted_iota(jnp.int32, (128, 256), 1)
        left_one = (n_id < 4) & (k_id == 4 * n_id + 1)
        right_one = (n_id >= 252) & (k_id == 4 * (n_id - 252))
        place = jnp.where(left_one | right_one, 1.0, 0.0).astype(BF16)
        outer = (dot(high, place) + dot(low, place))[8 : ROWS - 8]
        lane = lax.broadcasted_iota(jnp.int32, (TS, 128), 1)
        pixels[v - 1, :, 0:128] = jnp.where(lane < 4, outer[:, 0:128], pixels[v - 1, :, 0:128])
        pixels[v - 1, :, 384:512] = jnp.where(lane >= 124, outer[:, 128:256], pixels[v - 1, :, 384:512])

    unfold(0)
    mix()
    own.wait()
    for copy in frame_moves:
        copy.wait()
    take_frames()
    fold(0, -1.0, no_sums, 0)
    settle(1, exchange(1))

    unfold(1)
    mix()

    def measure_w(rows, inside, old, out):
        rr = old[0] * old[0] + old[1] * old[1] + (old[2] * old[2] + old[3] * old[3])
        rw = old[0] * out[0] + old[1] * out[1] + (old[2] * out[2] + old[3] * out[3])
        return jnp.where(inside, rr, 0.0), rw

    rr, rw = fold(1, 1.0, measure_w, 2)
    rw = rw + outer_columns(vec[1, 4, 0:PACK, :] * vec[2, 4, 0:PACK, :])
    moves = exchange(2)
    write_pixels(whole, 1)
    settle(2, moves)

    unfold(2)
    mix()
    ww = jnp.zeros((8, 128), F32)
    for q in range(4):
        own_rows = whole[2, q, 8 : ROWS - 8, :]
        ww = ww + fewer_rows(own_rows * own_rows)
    wz = DAMP * ww
    for f in range(8):
        wz = wz + fewer_rows(feat[f] * acc[f])
    sums = gather_a((rr, rw, ww, wz))
    fold(2, 1.0, no_sums, 0)
    moves = exchange(3)
    write_pixels(whole, 2)
    write_pixels(vec, 3)
    sums = gather_b(sums)
    settle(3, moves)
    patch_pixels(3)
    rr, rw, ww, wz = finish_sums(sums)
    alpha = rr / rw
    ss = alpha * alpha * ww - rr
    sw = rw - alpha * ww
    beta = ss / rr
    curve = (sw - alpha * (ww - alpha * wz)) + 2.0 * beta * sw + beta * beta * rw
    step = ss / curve
    c1, c2 = (alpha + step * (1.0 + beta))[0:1], (step * alpha)[0:1]
    c1, c2 = jnp.concatenate([c1] * 4, axis=1), jnp.concatenate([c2] * 4, axis=1)
    written = []
    for b in range(CLOSE):
        rows = slice(b * (TS // CLOSE), (b + 1) * (TS // CLOSE))
        r, w = pixels[0, rows, :], pixels[1, rows, :]
        pixels[2, rows, :] = r - c1 * w + c2 * pixels[2, rows, :]
        guess[rows, :] = guess[rows, :] + c1 * r - c2 * w
        for k, (source, target) in enumerate(((guess, solution_hbm), (pixels.at[2], residual_hbm))):
            written.append(pltpu.make_async_copy(source.at[rows], target.at[rows], stores.at[b, k]))
            written[-1].start()
    for store in written:
        store.wait()


def hand_over(solution_in, residual_in, solution_out, residual_out, held, loads, sems):
    arrays = ((solution_in, solution_out), (residual_in, residual_out))
    spots = [(b, k, slice(b * (TS // PARTS), (b + 1) * (TS // PARTS))) for b in range(PARTS) for k in range(2)]
    copies = []
    for b, k, rows in spots:
        copies.append(pltpu.make_async_copy(arrays[k][0].at[rows], held.at[k, rows], loads.at[b, k]))
        copies[-1].start()
    stores = []
    for copy, (b, k, rows) in zip(copies, spots):
        copy.wait()
        stores.append(pltpu.make_async_copy(held.at[k, rows], arrays[k][1].at[rows], sems.at[b, k]))
        stores[-1].start()
    for store in stores:
        store.wait()


def on_device(n_wide, n_narrow, frames, anchor, shift, guess):
    vmem, hbm = pl.BlockSpec(memory_space=pltpu.VMEM), pl.BlockSpec(memory_space=pltpu.HBM)
    image = jax.ShapeDtypeStruct((TS, TS), F32)
    dma = pltpu.SemaphoreType.DMA
    n_a, n_b = n_narrow * (n_wide // 8), 8
    made = pl.pallas_call(
        functools.partial(kernel, n_wide, n_narrow),
        out_shape=(image, image),
        in_specs=[hbm, vmem, vmem, hbm, hbm],
        out_specs=(hbm, hbm),
        scratch_shapes=[
            pltpu.VMEM((TS, TS), F32),
            pltpu.VMEM((3, TS, TS), F32),
            pltpu.VMEM((3, 128, 128), F32),
            pltpu.VMEM((4, 5, ROWS, 128), F32),
            pltpu.VMEM((4, 4, ROWS, 128), F32),
            pltpu.VMEM((ROWS, 128), F32),
            pltpu.VMEM((8, ROWS, 128), F32),
            pltpu.VMEM((8, ROWS, 128), F32),
            pltpu.VMEM((8, ROWS, 128), F32),
            pltpu.VMEM((24 * FS, 128), F32),
            pltpu.VMEM((2, 512, 512), BF16),
            pltpu.VMEM((3, 128, 384), BF16),
            pltpu.VMEM((3, 128, 256), BF16),
            pltpu.VMEM((4, 2, PACK, 128), F32),
            pltpu.VMEM((4, 2, 5, 16, 128), F32),
            pltpu.VMEM((4, 4, 16, 128), F32),
            pltpu.VMEM((n_a, 8, 128), F32),
            pltpu.VMEM((n_b, 8, 128), F32),
            dma((4, 8)), dma((4, 8)), dma((2,)), dma((2,)), dma((3,)), dma((CLOSE, 2)),
            dma((n_a,)), dma((n_a,)), dma((n_b,)), dma((n_b,)),
        ],
        compiler_params=pltpu.CompilerParams(
            collective_id=0, has_side_effects=True, vmem_limit_bytes=VMEM_BYTES),
    )(frames.reshape(8 * FS, FS), anchor, shift.transpose(0, 2, 1), guess, jnp.asarray(tables()))
    return pl.pallas_call(
        hand_over,
        out_shape=(image, image),
        in_specs=[hbm, hbm],
        out_specs=(hbm, hbm),
        scratch_shapes=[pltpu.VMEM((2, TS, TS), F32), dma((PARTS, 2)), dma((PARTS, 2))],
        compiler_params=pltpu.CompilerParams(vmem_limit_bytes=VMEM_BYTES),
    )(*made)


def solution(mesh):
    placed = (P("narrow", "wide", None, None), P("narrow", None), P("narrow", None, None), P("narrow", "wide"))
    return jax.shard_map(
        functools.partial(on_device, mesh.shape["wide"], mesh.shape["narrow"]),
        mesh=mesh,
        in_specs=placed,
        out_specs=(P("narrow", "wide"), P("narrow", "wide")),
        check_vma=False,
    )
```
